128 devices in a mesh: row: 16 (over y, x_lo, core), col: 8 (over z, x_hi).
Axes of the slice: x: 4 (x_hi: 2, x_lo: 2; x = x_hi * 2 + x_lo), y: 4, z: 4, core: 2. Of those that a mesh axis runs over, the one named last changes fastest.
Arguments:
- value_matrix: float32 [16384, 16384], P('row', 'col'), may hold values from -1 to 3, as said below
- inputs: float32 [16384, 1024], P('row'), may hold values from -0.09375 to 0.09375
- plant_diag: float32 [128, 128], replicated, may hold values from 0.3 to 0.9
- state_cost: float32 [16384], P('row'), may hold values from 0.05 to 1
- control_weight: float32 [1], replicated, may hold values from 0.25 to 40
Outputs:
- value_next: float32 [16384, 16384], P('row', 'col')
The draws below stay inside these ranges and needn't reach their ends.
Inputs may be any that keep to these rules, and one draw needn't show every extreme that they name: value_matrix is symmetric and positive definite.
All inputs are finite; a program needn't handle non-finite values.
Results may differ from the reference program's by a relative error of at most 0.00005.
Values sent between devices are 32-bit elements; how exact they have to be, the bound alone decides.
No kernel may reach another device: no remote copies, remote signals or barrier semaphores. Data moves between devices by JAX's collectives and lax.ppermute only.
A program may use at most 192 MiB of HBM per device.

```python
import math
import jax
import jax.numpy as jnp
from jax import lax

GRID = 128
ACT = 1024
STATES = 16384


def draw_value_matrix(key, part):
    key = jax.random.fold_in(key, 11)
    states = GRID * GRID
    key_noise, key_diag = jax.random.split(key)
    noise = jax.random.uniform(key_noise, (states, states), jnp.float32, -0.85 / GRID, 0.85 / GRID)
    diagonal = jax.random.uniform(key_diag, (states,), jnp.float32, 1.2, 2.2)
    symmetric = 0.5 * (noise + noise.T)
    positions = jnp.arange(states)
    on_diagonal = positions[:, None] == positions[None, :]
    return jnp.where(on_diagonal, diagonal[:, None], symmetric)


def block_scale(own_key, dims, cuts, smallest, high):
    gain = 1.0
    for position, shards_of in cuts:
        steps = jax.random.uniform(jax.random.fold_in(jax.random.fold_in(own_key, 6), position), (shards_of,), jnp.float32, smallest / len(cuts), high / len(cuts))
        gain = gain * jnp.repeat(jnp.exp(steps), dims[position] // shards_of).reshape((-1,) + (1,) * (len(dims) - 1 - position))
    return gain


def bell_draw(key, dims, deviation, reach, shards=(), held_as=jnp.bfloat16):
    drawn = deviation * jax.random.normal(key, dims, jnp.float32)
    if shards:
        drawn = drawn * block_scale(key, dims, shards, -0.22, 0.18)
    return jnp.clip(drawn, -reach, reach).astype(held_as)


def setup_inputs(seed: int = 0) -> dict:
    splits = jax.random.split(jax.random.key(seed), 6)
    value_matrix = draw_value_matrix(jax.random.fold_in(splits[5], 71), 0)
    inputs = bell_draw(splits[1], (STATES, ACT), (2.0 / GRID), 0.09375, ((0, 16),), jnp.float32)
    plant_diag = jnp.clip(jax.random.uniform(splits[2], (GRID, GRID), jnp.float32, 0.3, 0.9), 0.3, 0.9)
    state_cost = jnp.clip(jnp.exp(math.log(1.0) - 2.9957323 * jax.random.uniform(splits[3], (STATES,), jnp.float32) ** block_scale(splits[3], (STATES,), ((0, 16),), -0.2, 0.2)), 0.05, 1.0)
    control_weight = jnp.clip(jnp.exp(jax.random.uniform(splits[4], (1,), jnp.float32, math.log(0.25), math.log(40.0))), 0.25, 40.0)
    return dict(value_matrix=value_matrix, inputs=inputs, plant_diag=plant_diag, state_cost=state_cost, control_weight=control_weight)


COUPLING = 0.25
HIGHEST_PRECISION = lax.Precision.HIGHEST

def stencil_first(field, diagonal):
    centre = field[1:-1]
    side_padded = jnp.pad(centre, ((0, 0), (1, 1), (0, 0)))
    neighbours = field[:-2] + field[2:] + side_padded[:, :-2] + side_padded[:, 2:]
    return diagonal[:, :, None] * centre + COUPLING * neighbours

def stencil_last(field, diagonal):
    centre = field[:, 1:-1]
    side_padded = jnp.pad(centre, ((0, 0), (0, 0), (1, 1)))
    neighbours = field[:, :-2] + field[:, 2:] + side_padded[:, :, :-2] + side_padded[:, :, 2:]
    return diagonal[None] * centre + COUPLING * neighbours

def reference(value_matrix, inputs, plant_diag, state_cost, control_weight):
    states = GRID * GRID
    pb_full = jnp.dot(value_matrix, inputs, precision=HIGHEST_PRECISION)
    gram_matrix = jnp.dot(inputs.T, pb_full, precision=HIGHEST_PRECISION)
    gram_matrix = gram_matrix + control_weight[0] * jnp.eye(ACT, dtype=pb_full.dtype)
    padded_gain = jnp.pad(pb_full.reshape(GRID, GRID, ACT), ((1, 1), (0, 0), (0, 0)))
    gain_rows = stencil_first(padded_gain, plant_diag).reshape(states, ACT)
    factor = jnp.linalg.cholesky(gram_matrix)
    scaled_gain = jax.scipy.linalg.solve_triangular(factor, gain_rows.T, lower=True)
    padded_value = jnp.pad(value_matrix.reshape(GRID, GRID, states), ((1, 1), (0, 0), (0, 0)))
    left_side = stencil_first(padded_value, plant_diag).reshape(states, states)
    padded_left = jnp.pad(left_side.reshape(states, GRID, GRID), ((0, 0), (1, 1), (0, 0)))
    propagated = stencil_last(padded_left, plant_diag).reshape(states, states)
    downdate = jnp.dot(scaled_gain.T, scaled_gain, precision=HIGHEST_PRECISION)
    positions = jnp.arange(states)
    result = propagated - downdate
    return result.at[positions, positions].add(state_cost)
```

```python
import functools

import jax
import jax.numpy as jnp
from jax import lax
from jax.experimental import pallas as pl
from jax.experimental.pallas import tpu as pltpu
from jax.sharding import PartitionSpec as P

COUPLING = 0.25
HIGHEST_PRECISION = lax.Precision.HIGHEST
F32 = jnp.float32
BF16 = jnp.bfloat16
NN = (((1,), (0,)), ((), ()))
NT = (((1,), (1,)), ((), ()))
TN = (((0,), (0,)), ((), ()))
LINE = 128
PANEL = 256
VMEM_LIMIT = 56 << 20


def split(x):
    high = x.astype(BF16)
    return high, (x - high.astype(F32)).astype(BF16)


def dot1(a, b, dims):
    return lax.dot_general(a, b, dims, preferred_element_type=F32)


def dot3(a, b, dims):
    (a_high, a_low), (b_high, b_low) = a, b
    return dot1(a_high, b_high, dims) + dot1(a_high, b_low, dims) + dot1(a_low, b_high, dims)


def line_of(device):
    return (device & 1) * 8 + (device >> 1)


def product_kernel(me_ref, first, second, inputs, out, high, low):
    @pl.when(pl.program_id(0) == 0)
    def _():
        high[...], low[...] = split(inputs[...])

    lines = split(jnp.concatenate([first[...], second[...]], 1))
    out[...] = dot3(lines, (high[...], low[...]), TN).reshape(out.shape)


def product_lines(me, value_matrix, inputs, odd):
    rows, acts = inputs.shape
    return pl.pallas_call(
        product_kernel,
        grid_spec=pltpu.PrefetchScalarGridSpec(
            num_scalar_prefetch=1,
            grid=(4,),
            in_specs=[
                pl.BlockSpec((rows, LINE), lambda i, m: (0, line_of(m[0] ^ (4 * i + odd)))),
                pl.BlockSpec((rows, LINE), lambda i, m: (0, line_of(m[0] ^ (4 * i + 2 + odd)))),
                pl.BlockSpec((rows, acts), lambda i, m: (0, 0)),
            ],
            out_specs=pl.BlockSpec((2, LINE, acts), lambda i, m: (i, 0, 0)),
            scratch_shapes=[pltpu.VMEM((rows, acts), BF16)] * 2,
        ),
        out_shape=jax.ShapeDtypeStruct((8, LINE, acts), F32),
        compiler_params=pltpu.CompilerParams(vmem_limit_bytes=VMEM_LIMIT),
        cost_estimate=pl.CostEstimate(flops=6 * 1024 * rows * acts, bytes_accessed=12 << 20, transcendentals=0),
    )(me, value_matrix, value_matrix, inputs)


def swap(x, mask, axis="row"):
    count = 16 if axis == "row" else 8
    return lax.ppermute(x, axis, [(i, i ^ mask) for i in range(count)])


def reduce_y(near, far, blocks):
    kept = [blocks[0], blocks[far]]
    got = swap(jnp.stack([blocks[near], blocks[near ^ far]]), near * 4)
    kept = [kept[0] + got[0], kept[1] + got[1]]
    return kept[0] + swap(kept[1], far * 4)


def scatter_lines(even, odd):
    got = swap(odd, 1)
    quarter = LINE // 4
    cut = lambda i, q: even[i, q * quarter : (q + 1) * quarter] + got[i, q * quarter : (q + 1) * quarter]
    half = lambda i, q: jnp.concatenate([cut(i, q), cut(i, q + 1)], 0)
    came = swap(jnp.stack([half(2 * m + 1, 0) for m in range(4)]), 2)
    own = [half(2 * m, 0) + came[m] for m in range(4)]
    a = reduce_y(1, 3, [o[:quarter] for o in own])
    b = reduce_y(3, 1, [o[quarter:] for o in own])
    pair = lambda m, q: jnp.stack([cut(2 * m, q), cut(2 * m + 1, q)])
    c = reduce_y(1, 3, [pair(m, 2) for m in range(4)])
    d = reduce_y(3, 1, [pair(m, 3) for m in range(4)])
    rest = jnp.concatenate([c[0], d[0]], 0) + swap(jnp.concatenate([c[1], d[1]], 0), 2)
    return jnp.concatenate([a, b, rest], 0)


def halves(x, bit):
    count = x.shape[0] // 2
    low, high = x[:count], x[count:]
    return jnp.where(bit, high, low), jnp.where(bit, low, high)


def joined(mine, got, bit):
    return jnp.concatenate([jnp.where(bit, got, mine), jnp.where(bit, mine, got)], 0)


def sum_all(x, row_index, col_index):
    bit = lambda k: (row_index >> k) & 1 == 1
    keep, send = halves(x, bit(0))
    x = keep + swap(send, 1)
    y = row_index >> 2
    count = x.shape[0] // 4
    own = lambda m: lax.dynamic_slice_in_dim(x, (y ^ m) * count, count, 0)
    x = own(0) + swap(own(1), 4) + swap(own(3), 12) + swap(own(2), 8)
    keep, send = halves(x, bit(1))
    x = keep + swap(send, 2)
    x = x + swap(x, 2, "col") + swap(x, 6, "col") + swap(x, 4, "col")
    x = x + swap(x, 1, "col")
    x = joined(x, swap(x, 2), bit(1))
    parts = [x, swap(x, 4), swap(x, 8), swap(x, 12)]
    parts = jnp.stack(parts)
    x = jnp.concatenate([lax.dynamic_index_in_dim(parts, y ^ m, 0, False) for m in range(4)], 0)
    return joined(x, swap(x, 1), bit(0))


def gram_kernel(inputs, product, out):
    a = inputs[...]
    b = product[...]
    at = 0
    for k in range(4):
        for i in range(k, 4):
            left = a[:, i * PANEL : (i + 1) * PANEL]
            right = b[:, k * PANEL : (k + 1) * PANEL]
            out[at] = lax.dot_general(left, right, TN, precision=HIGHEST_PRECISION, preferred_element_type=F32)
            at += 1


def gram_blocks(inputs, product):
    return pl.pallas_call(
        gram_kernel,
        out_shape=jax.ShapeDtypeStruct((10, PANEL, PANEL), F32),
        compiler_params=pltpu.CompilerParams(vmem_limit_bytes=VMEM_LIMIT),
    )(inputs, product)


def block_index(i, k):
    return k * 4 - (k * (k - 1)) // 2 + i - k


def series_inverse(a, eye, mask):
    picked = jnp.where(mask, a, 0.0)
    across = lax.rsqrt(jnp.sum(picked, axis=0, keepdims=True))
    down = lax.rsqrt(jnp.sum(picked, axis=1, keepdims=True))
    error = jnp.where(mask, 0.0, -(a * across * down))
    result = eye + error
    for _ in range(3):
        parts = split(error)
        error = dot3(parts, parts, NN)
        result = result + dot3(split(result), split(error), NN)
    short = error.astype(BF16)
    error = dot1(short, short, NN)
    result = result + dot1(result.astype(BF16), error.astype(BF16), NN)
    return result * across * down, jnp.sum(error * error, keepdims=True)


def pivot_inverse(a, work):
    size = a.shape[0]
    work[...] = a
    lanes = lax.broadcasted_iota(jnp.int32, (1, size), 1)
    rows = lax.broadcasted_iota(jnp.int32, (size, 1), 0)

    def step(p, carry):
        now = work[...]
        across = work[pl.ds(p, 1), :]
        down = jnp.sum(jnp.where(lanes == p, now, 0.0), axis=1, keepdims=True)
        inverse = 1.0 / jnp.sum(jnp.where(lanes == p, across, 0.0), axis=1, keepdims=True)
        new = now - down * (across * inverse)
        new = jnp.where(lanes == p, down * inverse, new)
        new = jnp.where(rows == p, across * inverse, new)
        work[...] = jnp.where((rows == p) & (lanes == p), -inverse, new)
        return carry

    lax.fori_loop(0, size, step, 0)
    return -work[...]


def solve_kernel(weight, gram, sides, out, factor, inverses, work, worst):
    size = PANEL
    mask = lax.broadcasted_iota(jnp.int32, (size, size), 0) == lax.broadcasted_iota(jnp.int32, (size, size), 1)
    eye = jnp.where(mask, 1.0, 0.0).astype(F32)
    at = lambda k: slice(k * size, (k + 1) * size)

    def run(robust):
        for k in range(4):
            for i in range(k, 4):
                here = gram[block_index(i, k)]
                factor[block_index(i, k)] = here + weight[0] * eye if i == k else here
        out[...] = sides[...]
        for k in range(4):
            here = factor[block_index(k, k)]
            if robust:
                inverse = pivot_inverse(here, work)
            else:
                inverse, off = series_inverse(here, eye, mask)
                worst[...] = off if k == 0 else jnp.where(off < worst[...], worst[...], off)
            inverses[k] = inverse
            parts = split(inverse)
            solved = split(out[:, at(k)])
            columns = [split(factor[block_index(i, k)]) for i in range(k + 1, 4)]
            lefts = []
            for i in range(k + 1, 4):
                left = dot3(columns[i - k - 1], parts, NN)
                factor[block_index(i, k)] = left
                lefts.append(split(left))
            for j in range(k + 1, 4):
                for i in range(j, 4):
                    factor[block_index(i, j)] -= dot3(lefts[i - k - 1], columns[j - k - 1], NT)
            for i in range(k + 1, 4):
                out[:, at(i)] -= dot3(solved, lefts[i - k - 1], NT)
        for k in range(3, -1, -1):
            total = dot3(split(out[:, at(k)]), split(inverses[k]), NN)
            for i in range(k + 1, 4):
                total = total - dot3(split(out[:, at(i)]), split(factor[block_index(i, k)]), NN)
            out[:, at(k)] = total

    run(False)

    @pl.when(jnp.logical_not(worst[0, 0] < 1e-6))
    def _():
        run(True)


def solve(weight, gram, sides):
    return pl.pallas_call(
        solve_kernel,
        out_shape=jax.ShapeDtypeStruct(sides.shape, F32),
        in_specs=[
            pl.BlockSpec(memory_space=pltpu.SMEM),
            pl.BlockSpec(memory_space=pltpu.VMEM),
            pl.BlockSpec(memory_space=pltpu.VMEM),
        ],
        out_specs=pl.BlockSpec(memory_space=pltpu.VMEM),
        scratch_shapes=[
            pltpu.VMEM((10, PANEL, PANEL), F32),
            pltpu.VMEM((4, PANEL, PANEL), F32),
            pltpu.VMEM((PANEL, PANEL), F32),
            pltpu.VMEM((1, 1), F32),
        ],
        compiler_params=pltpu.CompilerParams(vmem_limit_bytes=VMEM_LIMIT),
    )(weight, gram, sides)


def extended(cells, sides, width):
    for axis, dim in sides:
        count = lax.axis_size(axis)
        ends = count - 1
        head = lax.slice_in_dim(cells, 0, width, axis=dim)
        tail = lax.slice_in_dim(cells, cells.shape[dim] - width, cells.shape[dim], axis=dim)
        cells = jnp.concatenate(
            [
                lax.ppermute(tail, axis, [(i, (i + 1) % count) for i in range(ends)]),
                cells,
                lax.ppermute(head, axis, [((i + 1) % count, i) for i in range(ends)]),
            ],
            axis=dim,
        )
    return cells


def stencil_first(field, diagonal):
    centre = field[1:-1]
    side_padded = jnp.pad(centre, ((0, 0), (1, 1), (0, 0)))
    neighbours = field[:-2] + field[2:] + side_padded[:, :-2] + side_padded[:, 2:]
    return diagonal[:, :, None] * centre + COUPLING * neighbours


def stencil_last(field, diagonal):
    centre = field[:, 1:-1]
    side_padded = jnp.pad(centre, ((0, 0), (0, 0), (1, 1)))
    neighbours = field[:, :-2] + field[:, 2:] + side_padded[:, :, :-2] + side_padded[:, :, 2:]
    return diagonal[None] * centre + COUPLING * neighbours


def device_of(line):
    chip_row, core, col = line % 8, (line // 8) % 2, line // 16
    return (chip_row * 2 + core) * 8 + col


def local(value_matrix, inputs, plant_diag, state_cost, control_weight):
    row_index = lax.axis_index("row")
    col_index = lax.axis_index("col")
    both = ("row", "col")
    grid_side = plant_diag.shape[0]
    rows_block, cols_block = value_matrix.shape
    actuators = inputs.shape[1]
    lines_rows = rows_block // grid_side
    lines_cols = cols_block // grid_side
    diag_rows = lax.dynamic_slice_in_dim(plant_diag, row_index * lines_rows, lines_rows, 0)
    diag_cols = lax.dynamic_slice_in_dim(plant_diag, col_index * lines_cols, lines_cols, 0)
    me = row_index.astype(jnp.int32).reshape(1)
    trade = [((a * 2 + core) * 8 + b, (b * 2 + core) * 8 + a) for a in range(8) for b in range(8) for core in range(2)]
    mine_inputs = lax.dynamic_slice_in_dim(inputs, col_index * LINE, LINE, 0)
    mine_inputs = lax.ppermute(mine_inputs, both, trade)
    odd = product_lines(me, value_matrix, inputs, 1)
    even = product_lines(me, value_matrix, inputs, 0)
    product = scatter_lines(even, odd)

    gram = gram_blocks(mine_inputs, product)
    gram = sum_all(gram.reshape(10 * PANEL, PANEL), row_index, col_index).reshape(10, PANEL, PANEL)

    lines = STATES_LINES = 128
    above = lax.ppermute(product, both, [(device_of(i), device_of(i + 1)) for i in range(lines - 1)])
    below = lax.ppermute(product, both, [(device_of(i + 1), device_of(i)) for i in range(lines - 1)])
    line = col_index * 16 + line_of(row_index)
    diagonal = lax.dynamic_slice_in_dim(plant_diag, line, 1, 0)
    gain = stencil_first(jnp.stack([above, product, below]), diagonal)[0]
    gain_cols = lax.all_gather(gain, "row", axis=0)
    gain_cols = gain_cols.reshape(8, 2, LINE, actuators).swapaxes(0, 1).reshape(cols_block, actuators)
    gain_rows = lax.all_gather(lax.ppermute(gain, both, trade), "col", axis=0, tiled=True)

    padded_value = extended(value_matrix, (("col", 1),), grid_side)
    plant_cols = stencil_last(padded_value.reshape(rows_block, lines_cols + 2, grid_side), diag_cols)
    padded_product = extended(plant_cols.reshape(rows_block, cols_block), (("row", 0),), grid_side)
    propagated = stencil_first(padded_product.reshape(lines_rows + 2, grid_side, cols_block), diag_rows)
    propagated = propagated.reshape(rows_block, cols_block)
    row_states = row_index * rows_block + jnp.arange(rows_block, dtype=jnp.int32)
    col_states = col_index * cols_block + jnp.arange(cols_block, dtype=jnp.int32)
    diagonal_mask = row_states[:, None] == col_states[None, :]
    propagated = propagated + jnp.where(diagonal_mask, state_cost[:, None], jnp.float32(0.0))

    solved = solve(control_weight, gram, gain_rows)
    downdate = lax.dot_general(solved, gain_cols, NT, precision=lax.Precision.HIGH)
    return propagated - downdate


def solution(mesh):
    in_specs = (P("row", "col"), P("row", None), P(), P("row"), P())
    out_specs = P("row", "col")
    return jax.shard_map(local, mesh=mesh, in_specs=in_specs, out_specs=out_specs, check_vma=False)
```

```python
import functools

import jax
import jax.numpy as jnp
from jax import lax
from jax.experimental import pallas as pl
from jax.experimental.pallas import tpu as pltpu
from jax.sharding import PartitionSpec as P

COUPLING = 0.25
F32 = jnp.float32
BF16 = jnp.bfloat16
NN = (((1,), (0,)), ((), ()))
NT = (((1,), (1,)), ((), ()))
TN = (((0,), (0,)), ((), ()))
LINE = 128
PANEL = 256
VMEM_LIMIT = 56 << 20


def split(x):
    high = x.astype(BF16)
    return high, (x - high.astype(F32)).astype(BF16)


def dot1(a, b, dims):
    return lax.dot_general(a, b, dims, preferred_element_type=F32)


def dot3(a, b, dims):
    (a_high, a_low), (b_high, b_low) = a, b
    return dot1(a_high, b_high, dims) + dot1(a_high, b_low, dims) + dot1(a_low, b_high, dims)


def line_of(device):
    return (device & 1) * 8 + (device >> 1)


def product_kernel(me_ref, first, second, inputs, out, high, low):
    @pl.when(pl.program_id(0) == 0)
    def _():
        high[...], low[...] = split(inputs[...])

    lines = split(jnp.concatenate([first[...], second[...]], 1))
    out[...] = dot3(lines, (high[...], low[...]), TN).reshape(out.shape)


def product_lines(me, value_matrix, inputs, odd):
    rows, acts = inputs.shape
    return pl.pallas_call(
        product_kernel,
        grid_spec=pltpu.PrefetchScalarGridSpec(
            num_scalar_prefetch=1,
            grid=(4,),
            in_specs=[
                pl.BlockSpec((rows, LINE), lambda i, m: (0, line_of(m[0] ^ (4 * i + odd)))),
                pl.BlockSpec((rows, LINE), lambda i, m: (0, line_of(m[0] ^ (4 * i + 2 + odd)))),
                pl.BlockSpec((rows, acts), lambda i, m: (0, 0)),
            ],
            out_specs=pl.BlockSpec((2, LINE, acts), lambda i, m: (i, 0, 0)),
            scratch_shapes=[pltpu.VMEM((rows, acts), BF16)] * 2,
        ),
        out_shape=jax.ShapeDtypeStruct((8, LINE, acts), F32),
        compiler_params=pltpu.CompilerParams(vmem_limit_bytes=VMEM_LIMIT),
        cost_estimate=pl.CostEstimate(flops=6 * 1024 * rows * acts, bytes_accessed=12 << 20, transcendentals=0),
    )(me, value_matrix, value_matrix, inputs)


def swap(x, mask):
    return lax.ppermute(x, ("row", "col"), [(i, i ^ mask) for i in range(128)])


CORE, X_LOW, X_HIGH = 8, 16, 1
Y = (0, 32, 64, 96)
Z = (0, 2, 4, 6)
X = (0, 16, 1, 17)


def reduce_y(near, far, blocks):
    kept = [blocks[0], blocks[far]]
    got = swap(jnp.stack([blocks[near], blocks[near ^ far]]), Y[near])
    kept = [kept[0] + got[0], kept[1] + got[1]]
    return kept[0] + swap(kept[1], Y[far])


def scatter_lines(even, odd):
    got = swap(odd, CORE)
    quarter = LINE // 4
    cut = lambda i, q: even[i, q * quarter : (q + 1) * quarter] + got[i, q * quarter : (q + 1) * quarter]
    half = lambda i, q: jnp.concatenate([cut(i, q), cut(i, q + 1)], 0)
    came = swap(jnp.stack([half(2 * m + 1, 0) for m in range(4)]), X_LOW)
    own = [half(2 * m, 0) + came[m] for m in range(4)]
    a = reduce_y(1, 3, [o[:quarter] for o in own])
    b = reduce_y(3, 1, [o[quarter:] for o in own])
    pair = lambda m, q: jnp.stack([cut(2 * m, q), cut(2 * m + 1, q)])
    c = reduce_y(1, 3, [pair(m, 2) for m in range(4)])
    d = reduce_y(3, 1, [pair(m, 3) for m in range(4)])
    rest = jnp.concatenate([c[0], d[0]], 0) + swap(jnp.concatenate([c[1], d[1]], 0), X_LOW)
    return jnp.concatenate([a, b, rest], 0)


def halves(x, bit):
    count = x.shape[0] // 2
    low, high = x[:count], x[count:]
    return jnp.where(bit, high, low), jnp.where(bit, low, high)


def joined(mine, got, bit):
    return jnp.concatenate([jnp.where(bit, got, mine), jnp.where(bit, mine, got)], 0)


def scatter_four(x, place, masks):
    count = x.shape[0] // 4
    own = lambda m: lax.dynamic_slice_in_dim(x, (place ^ m) * count, count, 0)
    return own(0) + swap(own(1), masks[1]) + swap(own(2), masks[2]) + swap(own(3), masks[3])


def gather_four(x, place, masks):
    parts = jnp.stack([x] + [swap(x, masks[m]) for m in range(1, 4)])
    return jnp.concatenate([lax.dynamic_index_in_dim(parts, place ^ m, 0, False) for m in range(4)], 0)


def sum_all(x, row_index, col_index):
    core, x_low, y = row_index & 1, (row_index >> 1) & 1, row_index >> 2
    x_place = (col_index & 1) * 2 + x_low
    keep, send = halves(x, core == 1)
    x = keep + swap(send, CORE)
    x = scatter_four(x, y, Y)
    x = scatter_four(x, x_place, X)
    x = x + swap(x, Z[1]) + swap(x, Z[2]) + swap(x, Z[3])
    x = gather_four(x, x_place, X)
    x = gather_four(x, y, Y)
    return joined(x, swap(x, CORE), core == 1)


def gather_rows(x, col_index):
    pair = joined(x, swap(x, X_HIGH), (col_index & 1) == 1)
    first, second = pair[:LINE], pair[LINE:]
    first_near = swap(first, Z[1])
    second_near = swap(second, Z[3])
    first_far = swap(jnp.stack([first, first_near]), Z[3])
    second_far = swap(jnp.stack([second, second_near]), Z[1])
    return first, first_near, first_far, second, second_near, second_far


def gram_kernel(inputs, product, out):
    a = split(inputs[...])
    b = split(product[...])
    at = 0
    for k in range(4):
        for i in range(k, 4):
            left = [part[:, i * PANEL : (i + 1) * PANEL] for part in a]
            right = [part[:, k * PANEL : (k + 1) * PANEL] for part in b]
            out[at] = dot3(left, right, TN)
            at += 1


def gram_blocks(inputs, product):
    return pl.pallas_call(
        gram_kernel,
        out_shape=jax.ShapeDtypeStruct((10, PANEL, PANEL), F32),
        compiler_params=pltpu.CompilerParams(vmem_limit_bytes=VMEM_LIMIT),
    )(inputs, product)


def block_index(i, k):
    return k * 4 - (k * (k - 1)) // 2 + i - k


def series_inverse(a, eye, mask):
    picked = jnp.where(mask, a, 0.0)
    across = lax.rsqrt(jnp.sum(picked, axis=0, keepdims=True))
    down = lax.rsqrt(jnp.sum(picked, axis=1, keepdims=True))
    error = jnp.where(mask, 0.0, -(a * across * down))
    result = eye + error
    for _ in range(3):
        parts = split(error)
        error = dot3(parts, parts, NN)
        result = result + dot3(split(result), split(error), NN)
    short = error.astype(BF16)
    error = dot1(short, short, NN)
    result = result + dot1(result.astype(BF16), error.astype(BF16), NN)
    return result * across * down, jnp.sum(error * error, keepdims=True)


def pivot_inverse(a, work):
    size = a.shape[0]
    work[...] = a
    lanes = lax.broadcasted_iota(jnp.int32, (1, size), 1)
    rows = lax.broadcasted_iota(jnp.int32, (size, 1), 0)

    def step(p, carry):
        now = work[...]
        across = work[pl.ds(p, 1), :]
        down = jnp.sum(jnp.where(lanes == p, now, 0.0), axis=1, keepdims=True)
        inverse = 1.0 / jnp.sum(jnp.where(lanes == p, across, 0.0), axis=1, keepdims=True)
        new = now - down * (across * inverse)
        new = jnp.where(lanes == p, down * inverse, new)
        new = jnp.where(rows == p, across * inverse, new)
        work[...] = jnp.where((rows == p) & (lanes == p), -inverse, new)
        return carry

    lax.fori_loop(0, size, step, 0)
    return -work[...]


def solve_kernel(weight, z, gram, s0, s1, s2, t0, t1, t2, high, low, out, factor, inverses, work, worst):
    size = PANEL
    mask = lax.broadcasted_iota(jnp.int32, (size, size), 0) == lax.broadcasted_iota(jnp.int32, (size, size), 1)
    eye = jnp.where(mask, 1.0, 0.0).astype(F32)
    at = lambda k: slice(k * size, (k + 1) * size)

    def run(robust):
        for k in range(4):
            for i in range(k, 4):
                here = gram[block_index(i, k)]
                factor[block_index(i, k)] = here + weight[0] * eye if i == k else here
        rows = lambda step, h: pl.ds(pl.multiple_of(((z[0] ^ step) * 2 + h) * LINE, LINE), LINE)
        out[rows(0, 0), :] = s0[...]
        out[rows(1, 0), :] = s1[...]
        out[rows(3, 0), :] = s2[0]
        out[rows(2, 0), :] = s2[1]
        out[rows(0, 1), :] = t0[...]
        out[rows(3, 1), :] = t1[...]
        out[rows(1, 1), :] = t2[0]
        out[rows(2, 1), :] = t2[1]
        for k in range(4):
            here = factor[block_index(k, k)]
            if robust:
                inverse = pivot_inverse(here, work)
            else:
                inverse, off = series_inverse(here, eye, mask)
                worst[...] = off if k == 0 else jnp.where(off < worst[...], worst[...], off)
            inverses[k] = inverse
            parts = split(inverse)
            solved = split(out[:, at(k)])
            columns = [split(factor[block_index(i, k)]) for i in range(k + 1, 4)]
            lefts = []
            for i in range(k + 1, 4):
                left = dot3(columns[i - k - 1], parts, NN)
                factor[block_index(i, k)] = left
                lefts.append(split(left))
            for j in range(k + 1, 4):
                for i in range(j, 4):
                    factor[block_index(i, j)] -= dot3(lefts[i - k - 1], columns[j - k - 1], NT)
            for i in range(k + 1, 4):
                out[:, at(i)] -= dot3(solved, lefts[i - k - 1], NT)
        for k in range(3, -1, -1):
            total = dot3(split(out[:, at(k)]), split(inverses[k]), NN)
            for i in range(k + 1, 4):
                total = total - dot3(split(out[:, at(i)]), split(factor[block_index(i, k)]), NN)
            out[:, at(k)] = total
            high[:, at(k)], low[:, at(k)] = split(total)

    run(False)

    @pl.when(jnp.logical_not(worst[0, 0] < 1e-6))
    def _():
        run(True)


def solve(weight, z, gram, sides):
    scalar = pl.BlockSpec(memory_space=pltpu.SMEM)
    array = pl.BlockSpec(memory_space=pltpu.VMEM)
    size = 8 * LINE
    return pl.pallas_call(
        solve_kernel,
        out_shape=[jax.ShapeDtypeStruct((size, 4 * PANEL), BF16)] * 2,
        in_specs=[scalar, scalar] + [array] * 7,
        out_specs=[array, array],
        scratch_shapes=[
            pltpu.VMEM((size, 4 * PANEL), F32),
            pltpu.VMEM((10, PANEL, PANEL), F32),
            pltpu.VMEM((4, PANEL, PANEL), F32),
            pltpu.VMEM((PANEL, PANEL), F32),
            pltpu.VMEM((1, 1), F32),
        ],
        compiler_params=pltpu.CompilerParams(vmem_limit_bytes=VMEM_LIMIT),
        cost_estimate=pl.CostEstimate(flops=9 << 30, bytes_accessed=12 << 20, transcendentals=0),
    )(weight, z, gram, *sides)


def downdate_kernel(high, low, first, second, base, out):
    lines = split(jnp.concatenate([first[0], second[0]], 0))
    out[...] = base[...] - dot3((high[...], low[...]), lines, NT)


def downdate(solved, gain_cols, base):
    rows, acts = solved[0].shape
    whole = pl.BlockSpec((rows, acts), lambda b: (0, 0))
    line = lambda b: (b % 8) * 2 + b // 8
    block = pl.BlockSpec((rows, 2 * LINE), lambda b: (0, b))
    return pl.pallas_call(
        downdate_kernel,
        grid=(8,),
        in_specs=[
            whole,
            whole,
            pl.BlockSpec((1, LINE, acts), lambda b: (line(2 * b), 0, 0)),
            pl.BlockSpec((1, LINE, acts), lambda b: (line(2 * b + 1), 0, 0)),
            block,
        ],
        out_specs=block,
        out_shape=jax.ShapeDtypeStruct(base.shape, F32),
        compiler_params=pltpu.CompilerParams(vmem_limit_bytes=VMEM_LIMIT),
        cost_estimate=pl.CostEstimate(flops=12 << 30, bytes_accessed=28 << 20, transcendentals=0),
    )(*solved, gain_cols, gain_cols, base)


def stencil_first(field, diagonal):
    centre = field[1:-1]
    side_padded = jnp.pad(centre, ((0, 0), (1, 1), (0, 0)))
    neighbours = field[:-2] + field[2:] + side_padded[:, :-2] + side_padded[:, 2:]
    return diagonal[:, :, None] * centre + COUPLING * neighbours


def plant_kernel(place, value, above, below, left, right, rows_diag, cols_diag, cost, out):
    b = pl.program_id(0)
    last = pl.num_programs(0) - 1
    rows = value.shape[0]
    lanes = lax.broadcasted_iota(jnp.int32, (1, LINE), 1)
    inner = lax.broadcasted_iota(jnp.int32, (LINE, 1), 0)

    def column(at):
        cols = pl.ds(pl.multiple_of(at * LINE, LINE), LINE)
        return jnp.concatenate([above[:, cols], value[:, cols], below[:, cols]], 0)

    here = column(b)
    before = jnp.where(b == 0, left[...], column(jnp.maximum(b - 1, 0)))
    after = jnp.where(b == last, right[...], column(jnp.minimum(b + 1, last)))
    sides = jnp.where(lanes == 0, 0.0, pltpu.roll(here, 1, 1)) + jnp.where(
        lanes == LINE - 1, 0.0, pltpu.roll(here, LINE - 1, 1)
    )
    field = cols_diag[pl.ds(b, 1), :] * here + COUPLING * (before + after + sides)
    for a in range(rows // LINE):
        line = lambda k: field[(a + k) * LINE : (a + k + 1) * LINE]
        centre = line(1)
        sides = jnp.where(inner == 0, 0.0, pltpu.roll(centre, 1, 0)) + jnp.where(
            inner == LINE - 1, 0.0, pltpu.roll(centre, LINE - 1, 0)
        )
        new = rows_diag[:, a : a + 1] * centre + COUPLING * (line(0) + line(2) + sides)
        on_diagonal = (inner == lanes) & (place[0] + a == place[1] + b)
        out[a * LINE : (a + 1) * LINE, :] = new + jnp.where(on_diagonal, cost[a : a + 1, :], 0.0)


def plant_both(place, value, above, below, left, right, rows_diag, cols_diag, cost):
    rows, cols = value.shape
    array = pl.BlockSpec(memory_space=pltpu.VMEM)
    return pl.pallas_call(
        plant_kernel,
        grid=(cols // LINE,),
        in_specs=[pl.BlockSpec(memory_space=pltpu.SMEM)] + [array] * 8,
        out_specs=pl.BlockSpec((rows, LINE), lambda b: (0, b)),
        out_shape=jax.ShapeDtypeStruct(value.shape, F32),
        compiler_params=pltpu.CompilerParams(vmem_limit_bytes=VMEM_LIMIT),
        cost_estimate=pl.CostEstimate(flops=32 << 20, bytes_accessed=40 << 20, transcendentals=0),
    )(place, value, above, below, left, right, rows_diag, cols_diag, cost)


def device_of(line):
    chip_row, core, col = line % 8, (line // 8) % 2, line // 16
    return (chip_row * 2 + core) * 8 + col


def local(value_matrix, inputs, plant_diag, state_cost, control_weight):
    row_index = lax.axis_index("row")
    col_index = lax.axis_index("col")
    both = ("row", "col")
    grid_side = plant_diag.shape[0]
    rows_block, cols_block = value_matrix.shape
    actuators = inputs.shape[1]
    lines_rows = rows_block // grid_side
    lines_cols = cols_block // grid_side
    diag_rows = lax.dynamic_slice_in_dim(plant_diag, row_index * lines_rows, lines_rows, 0)
    diag_cols = lax.dynamic_slice_in_dim(plant_diag, col_index * lines_cols, lines_cols, 0)
    me = row_index.astype(jnp.int32).reshape(1)
    trade = [((a * 2 + core) * 8 + b, (b * 2 + core) * 8 + a) for a in range(8) for b in range(8) for core in range(2)]
    mine_inputs = lax.dynamic_slice_in_dim(inputs, col_index * LINE, LINE, 0)
    mine_inputs = lax.ppermute(mine_inputs, both, trade)

    def shifted(x, down, right):
        pairs = [
            (r * 8 + c, (r + down) * 8 + c + right)
            for r in range(16)
            for c in range(8)
            if 0 <= r + down < 16 and 0 <= c + right < 8
        ]
        return lax.ppermute(x, both, pairs)

    top, bottom = value_matrix[:LINE], value_matrix[-LINE:]
    above, below = shifted(bottom, 1, 0), shifted(top, -1, 0)
    left = [
        shifted(bottom[:, -LINE:], 1, 1),
        shifted(value_matrix[:, -LINE:], 0, 1),
        shifted(top[:, -LINE:], -1, 1),
    ]
    right = [
        shifted(bottom[:, :LINE], 1, -1),
        shifted(value_matrix[:, :LINE], 0, -1),
        shifted(top[:, :LINE], -1, -1),
    ]
    odd = product_lines(me, value_matrix, inputs, 1)
    held = (value_matrix, inputs, mine_inputs, above, below, left, right)
    value_here, inputs_here, mine_inputs, above, below, left, right = lax.optimization_barrier(held)
    even = product_lines(me, value_here, inputs_here, 0)
    product = scatter_lines(even, odd)

    gram = gram_blocks(mine_inputs, product)
    product, gram = lax.optimization_barrier((product, gram))
    gram = sum_all(gram.reshape(10 * PANEL, PANEL), row_index, col_index).reshape(10, PANEL, PANEL)

    lines = 128
    over = lax.ppermute(product, both, [(device_of(i), device_of(i + 1)) for i in range(lines - 1)])
    under = lax.ppermute(product, both, [(device_of(i + 1), device_of(i)) for i in range(lines - 1)])
    line = col_index * 16 + line_of(row_index)
    diagonal = lax.dynamic_slice_in_dim(plant_diag, line, 1, 0)
    gain = stencil_first(jnp.stack([over, product, under]), diagonal)[0]
    gain_cols = lax.all_gather(gain, "row", axis=0)
    gain_rows = gather_rows(lax.ppermute(gain, both, trade), col_index)

    place = jnp.stack([row_index * lines_rows, col_index * lines_cols]).astype(jnp.int32)
    base = plant_both(
        place,
        value_matrix,
        above,
        below,
        jnp.concatenate(left, 0),
        jnp.concatenate(right, 0),
        diag_rows.T,
        diag_cols,
        state_cost.reshape(lines_rows, grid_side),
    )
    z = (col_index >> 1).astype(jnp.int32).reshape(1)
    solved = solve(control_weight, z, gram, gain_rows)
    return downdate(solved, gain_cols, base)


def solution(mesh):
    in_specs = (P("row", "col"), P("row", None), P(), P("row"), P())
    out_specs = P("row", "col")
    return jax.shard_map(local, mesh=mesh, in_specs=in_specs, out_specs=out_specs, check_vma=False)
```

```python
import functools

import jax
import jax.numpy as jnp
from jax import lax
from jax.experimental import pallas as pl
from jax.experimental.pallas import tpu as pltpu
from jax.sharding import PartitionSpec as P

COUPLING = 0.25
F32 = jnp.float32
BF16 = jnp.bfloat16
NN = (((1,), (0,)), ((), ()))
NT = (((1,), (1,)), ((), ()))
TN = (((0,), (0,)), ((), ()))
LINE = 128
PANEL = 256
VMEM_LIMIT = 56 << 20


def split(x):
    high = x.astype(BF16)
    return high, (x - high.astype(F32)).astype(BF16)


def dot1(a, b, dims):
    return lax.dot_general(a, b, dims, preferred_element_type=F32)


def dot3(a, b, dims):
    (a_high, a_low), (b_high, b_low) = a, b
    return dot1(a_high, b_high, dims) + dot1(a_high, b_low, dims) + dot1(a_low, b_high, dims)


def line_of(device):
    return (device & 1) * 8 + (device >> 1)


def product_kernel(me_ref, first, second, inputs, out, high, low):
    @pl.when(pl.program_id(0) == 0)
    def _():
        high[...], low[...] = split(inputs[...])

    lines = split(jnp.concatenate([first[...], second[...]], 1))
    out[...] = dot3(lines, (high[...], low[...]), TN).reshape(out.shape)


def product_lines(me, value_matrix, inputs, odd):
    rows, acts = inputs.shape
    return pl.pallas_call(
        product_kernel,
        grid_spec=pltpu.PrefetchScalarGridSpec(
            num_scalar_prefetch=1,
            grid=(4,),
            in_specs=[
                pl.BlockSpec((rows, LINE), lambda i, m: (0, line_of(m[0] ^ (4 * i + odd)))),
                pl.BlockSpec((rows, LINE), lambda i, m: (0, line_of(m[0] ^ (4 * i + 2 + odd)))),
                pl.BlockSpec((rows, acts), lambda i, m: (0, 0)),
            ],
            out_specs=pl.BlockSpec((2, LINE, acts), lambda i, m: (i, 0, 0)),
            scratch_shapes=[pltpu.VMEM((rows, acts), BF16)] * 2,
        ),
        out_shape=jax.ShapeDtypeStruct((8, LINE, acts), F32),
        compiler_params=pltpu.CompilerParams(vmem_limit_bytes=VMEM_LIMIT),
        cost_estimate=pl.CostEstimate(flops=1 << 20, bytes_accessed=1 << 20, transcendentals=0),
    )(me, value_matrix, value_matrix, inputs)


def swap(x, mask):
    return lax.ppermute(x, ("row", "col"), [(i, i ^ mask) for i in range(128)])


CORE, X_LOW, X_HIGH = 8, 16, 1
Y = (0, 32, 64, 96)
Z = (0, 2, 4, 6)
X = (0, 16, 1, 17)


def y_first(near, blocks):
    return swap(jnp.stack([blocks[near], blocks[2]]), Y[near])


def y_second(near, blocks, got):
    far = 4 - near
    kept = blocks[far] + got[1]
    return blocks[0] + got[0] + swap(kept, Y[far])


def scatter_lines(even, odd, first_wait, second_wait):
    got = swap(odd, CORE)
    quarter = LINE // 4
    cut = lambda i, q: even[i, q * quarter : (q + 1) * quarter] + got[i, q * quarter : (q + 1) * quarter]
    half = lambda i, q: jnp.concatenate([cut(i, q), cut(i, q + 1)], 0)
    pair = lambda m, q: jnp.stack([cut(2 * m, q), cut(2 * m + 1, q)])
    came = swap(jnp.stack([half(2 * m + 1, 0) for m in range(4)]), X_LOW)
    c = [pair(m, 2) for m in range(4)]
    d = [pair(m, 3) for m in range(4)]
    c_got, d_got = first_wait(y_first(1, c), y_first(3, d))
    c, d = y_second(1, c, c_got), y_second(3, d, d_got)
    came = second_wait(came)
    own = [half(2 * m, 0) + came[m] for m in range(4)]
    a = [o[:quarter] for o in own]
    b = [o[quarter:] for o in own]
    a, b = y_second(1, a, y_first(1, a)), y_second(3, b, y_first(3, b))
    rest = jnp.concatenate([c[0], d[0]], 0) + swap(jnp.concatenate([c[1], d[1]], 0), X_LOW)
    return jnp.concatenate([a, b, rest], 0)


def halves(x, bit):
    count = x.shape[0] // 2
    low, high = x[:count], x[count:]
    return jnp.where(bit, high, low), jnp.where(bit, low, high)


def joined(mine, got, bit):
    return jnp.concatenate([jnp.where(bit, got, mine), jnp.where(bit, mine, got)], 0)


def scatter_four(x, place, masks, wait=lambda *got: got):
    count = x.shape[0] // 4
    own = lambda m: lax.dynamic_slice_in_dim(x, (place ^ m) * count, count, 0)
    near, far, across = wait(swap(own(1), masks[1]), swap(own(2), masks[2]), swap(own(3), masks[3]))
    return own(0) + near + far + across


def gather_four(x, place, masks):
    parts = jnp.stack([x] + [swap(x, masks[m]) for m in range(1, 4)])
    return jnp.concatenate([lax.dynamic_index_in_dim(parts, place ^ m, 0, False) for m in range(4)], 0)


def tied(*values):
    return lax.optimization_barrier(values)


def sum_start(x, core, y, wait):
    keep, send = halves(x, core == 1)
    x = keep + swap(send, CORE)
    return scatter_four(x, y, Y, wait)


def sum_middle(x, x_place):
    x = scatter_four(x, x_place, X)
    return x + swap(x, Z[1]) + swap(x, Z[2]) + swap(x, Z[3])


def sum_spread(x, x_place, y):
    return gather_four(gather_four(x, x_place, X), y, Y)


def gather_rows_start(line):
    first, second = line[: LINE // 2], line[LINE // 2 :]
    pair = jnp.stack([first, swap(first, X_HIGH)])
    quad = jnp.stack([second] + [swap(second, Z[m]) for m in range(1, 4)])
    return pair, quad


def gather_rows_end(pair, quad):
    return [pair] + [swap(pair, Z[m]) for m in range(1, 4)] + [quad, swap(quad, X_HIGH)]


def gram_kernel(inputs, product, out):
    a = split(inputs[...])
    b = split(product[...])
    at = 0
    for k in range(4):
        for i in range(k, 4):
            left = [part[:, i * PANEL : (i + 1) * PANEL] for part in a]
            right = [part[:, k * PANEL : (k + 1) * PANEL] for part in b]
            out[at] = dot3(left, right, TN)
            at += 1


def gram_blocks(inputs, product):
    return pl.pallas_call(
        gram_kernel,
        out_shape=jax.ShapeDtypeStruct((10, PANEL, PANEL), F32),
        compiler_params=pltpu.CompilerParams(vmem_limit_bytes=VMEM_LIMIT),
    )(inputs, product)


def block_index(i, k):
    return k * 4 - (k * (k - 1)) // 2 + i - k


def series_inverse(a, eye, mask):
    picked = jnp.where(mask, a, 0.0)
    across = lax.rsqrt(jnp.sum(picked, axis=0, keepdims=True))
    down = lax.rsqrt(jnp.sum(picked, axis=1, keepdims=True))
    error = jnp.where(mask, 0.0, -(a * across * down))
    result = eye + error
    for _ in range(3):
        parts = split(error)
        error = dot3(parts, parts, NN)
        result = result + dot3(split(result), split(error), NN)
    short = error.astype(BF16)
    error = dot1(short, short, NN)
    result = result + dot1(result.astype(BF16), error.astype(BF16), NN)
    return result * across * down, jnp.sum(error * error, keepdims=True)


def pivot_inverse(a, work):
    size = a.shape[0]
    work[...] = a
    lanes = lax.broadcasted_iota(jnp.int32, (1, size), 1)
    rows = lax.broadcasted_iota(jnp.int32, (size, 1), 0)

    def step(p, carry):
        now = work[...]
        across = work[pl.ds(p, 1), :]
        down = jnp.sum(jnp.where(lanes == p, now, 0.0), axis=1, keepdims=True)
        inverse = 1.0 / jnp.sum(jnp.where(lanes == p, across, 0.0), axis=1, keepdims=True)
        new = now - down * (across * inverse)
        new = jnp.where(lanes == p, down * inverse, new)
        new = jnp.where(rows == p, across * inverse, new)
        work[...] = jnp.where((rows == p) & (lanes == p), -inverse, new)
        return carry

    lax.fori_loop(0, size, step, 0)
    return -work[...]


def factor_kernel(weight, gram, factor, inverses, work, worst):
    size = PANEL
    mask = lax.broadcasted_iota(jnp.int32, (size, size), 0) == lax.broadcasted_iota(jnp.int32, (size, size), 1)
    eye = jnp.where(mask, 1.0, 0.0).astype(F32)

    def run(robust):
        for k in range(4):
            for i in range(k, 4):
                here = gram[block_index(i, k)]
                factor[block_index(i, k)] = here + weight[0] * eye if i == k else here
        for k in range(4):
            here = factor[block_index(k, k)]
            if robust:
                inverse = pivot_inverse(here, work)
            else:
                inverse, off = series_inverse(here, eye, mask)
                worst[...] = off if k == 0 else jnp.where(off < worst[...], worst[...], off)
            inverses[k] = inverse
            parts = split(inverse)
            columns = [split(factor[block_index(i, k)]) for i in range(k + 1, 4)]
            lefts = []
            for i in range(k + 1, 4):
                left = dot3(columns[i - k - 1], parts, NN)
                factor[block_index(i, k)] = left
                lefts.append(split(left))
            for j in range(k + 1, 4):
                for i in range(j, 4):
                    factor[block_index(i, j)] -= dot3(lefts[i - k - 1], columns[j - k - 1], NT)

    run(False)

    @pl.when(jnp.logical_not(worst[0, 0] < 1e-6))
    def _():
        run(True)


def factored(weight, gram):
    scalar = pl.BlockSpec(memory_space=pltpu.SMEM)
    array = pl.BlockSpec(memory_space=pltpu.VMEM)
    return pl.pallas_call(
        factor_kernel,
        out_shape=[
            jax.ShapeDtypeStruct((10, PANEL, PANEL), F32),
            jax.ShapeDtypeStruct((4, PANEL, PANEL), F32),
        ],
        in_specs=[scalar, array],
        out_specs=[array, array],
        scratch_shapes=[pltpu.VMEM((PANEL, PANEL), F32), pltpu.VMEM((1, 1), F32)],
        compiler_params=pltpu.CompilerParams(vmem_limit_bytes=VMEM_LIMIT),
        cost_estimate=pl.CostEstimate(flops=9 << 30, bytes_accessed=12 << 20, transcendentals=0),
    )(weight, gram)


def solve_kernel(place, factor, inverses, own, near, across, far, quad, other, high, low, out):
    size = PANEL
    half = LINE // 2
    at = lambda k: slice(k * size, (k + 1) * size)

    def put(step, e, second, value):
        line = (place[0] ^ step) * 2 + (place[1] ^ e)
        out[pl.ds(pl.multiple_of(line * LINE + second * half, half), half), :] = value

    for step, pair in enumerate((own, near, across, far)):
        for e in range(2):
            put(step, e, 0, pair[e])
    for e, lines in enumerate((quad, other)):
        for step in range(4):
            put(step, e, 1, lines[step])
    for k in range(4):
        solved = split(out[:, at(k)])
        for i in range(k + 1, 4):
            out[:, at(i)] -= dot3(solved, split(factor[block_index(i, k)]), NT)
    for k in range(3, -1, -1):
        total = dot3(split(out[:, at(k)]), split(inverses[k]), NN)
        for i in range(k + 1, 4):
            total = total - dot3((high[:, at(i)], low[:, at(i)]), split(factor[block_index(i, k)]), NN)
        high[:, at(k)], low[:, at(k)] = split(total)


def solve(place, factors, sides):
    scalar = pl.BlockSpec(memory_space=pltpu.SMEM)
    array = pl.BlockSpec(memory_space=pltpu.VMEM)
    size = 8 * LINE
    return pl.pallas_call(
        solve_kernel,
        out_shape=[jax.ShapeDtypeStruct((size, 4 * PANEL), BF16)] * 2,
        in_specs=[scalar] + [array] * 8,
        out_specs=[array, array],
        scratch_shapes=[pltpu.VMEM((size, 4 * PANEL), F32)],
        compiler_params=pltpu.CompilerParams(vmem_limit_bytes=VMEM_LIMIT),
        cost_estimate=pl.CostEstimate(flops=9 << 30, bytes_accessed=12 << 20, transcendentals=0),
    )(place, *factors, *sides)


def downdate_kernel(high, low, first, second, base, out):
    lines = split(jnp.concatenate([first[0], second[0]], 0))
    out[...] = base[...] - dot3((high[...], low[...]), lines, NT)


def downdate(solved, gain_cols, base):
    rows, acts = solved[0].shape
    whole = pl.BlockSpec((rows, acts), lambda b: (0, 0))
    line = lambda b: (b % 8) * 2 + b // 8
    block = pl.BlockSpec((rows, 2 * LINE), lambda b: (0, b))
    return pl.pallas_call(
        downdate_kernel,
        grid=(8,),
        in_specs=[
            whole,
            whole,
            pl.BlockSpec((1, LINE, acts), lambda b: (line(2 * b), 0, 0)),
            pl.BlockSpec((1, LINE, acts), lambda b: (line(2 * b + 1), 0, 0)),
            block,
        ],
        out_specs=block,
        out_shape=jax.ShapeDtypeStruct(base.shape, F32),
        compiler_params=pltpu.CompilerParams(vmem_limit_bytes=VMEM_LIMIT),
        cost_estimate=pl.CostEstimate(flops=12 << 30, bytes_accessed=28 << 20, transcendentals=0),
    )(*solved, gain_cols, gain_cols, base)


def stencil_first(field, diagonal):
    centre = field[1:-1]
    side_padded = jnp.pad(centre, ((0, 0), (1, 1), (0, 0)))
    neighbours = field[:-2] + field[2:] + side_padded[:, :-2] + side_padded[:, 2:]
    return diagonal[:, :, None] * centre + COUPLING * neighbours


def plant_kernel(start, last, sides, place, *refs):
    blocks, ends = refs[:9], refs[9 : 9 + sides]
    rows_diag, cols_diag, cost = refs[9 + sides : 12 + sides]
    out = refs[-1]
    b = pl.program_id(0) + start
    rows = out.shape[0]
    lanes = lax.broadcasted_iota(jnp.int32, (1, LINE), 1)
    inner = lax.broadcasted_iota(jnp.int32, (LINE, 1), 0)
    column = lambda k: jnp.concatenate([blocks[3 * k][...], blocks[3 * k + 1][...], blocks[3 * k + 2][...]], 0)
    here = column(1)
    before, after = column(0), column(2)
    if sides:
        before = jnp.where(b == 0, ends[0][...], before)
        after = jnp.where(b == last, ends[1][...], after)
    sides = jnp.where(lanes == 0, 0.0, pltpu.roll(here, 1, 1)) + jnp.where(
        lanes == LINE - 1, 0.0, pltpu.roll(here, LINE - 1, 1)
    )
    field = cols_diag[pl.ds(b, 1), :] * here + COUPLING * (before + after + sides)
    for a in range(rows // LINE):
        line = lambda k: field[(a + k) * LINE : (a + k + 1) * LINE]
        centre = line(1)
        sides = jnp.where(inner == 0, 0.0, pltpu.roll(centre, 1, 0)) + jnp.where(
            inner == LINE - 1, 0.0, pltpu.roll(centre, LINE - 1, 0)
        )
        new = rows_diag[:, a : a + 1] * centre + COUPLING * (line(0) + line(2) + sides)
        on_diagonal = (inner == lanes) & (place[0] + a == place[1] + b)
        out[a * LINE : (a + 1) * LINE, :] = new + jnp.where(on_diagonal, cost[a : a + 1, :], 0.0)


def plant_part(start, count, place, value, above, below, left, right, rows_diag, cols_diag, cost, before):
    rows, cols = value.shape
    last = cols // LINE - 1
    array = pl.BlockSpec(memory_space=pltpu.VMEM)
    blocks, specs = [], []
    for step in (-1, 0, 1):
        index = lambda b, step=step: (0, jnp.clip(b + start + step, 0, last))
        for x in (above, value, below):
            blocks.append(x)
            specs.append(pl.BlockSpec((x.shape[0], LINE), index))
    sides = [] if left is None else [left, right]
    operands = [place, *blocks, *sides, rows_diag, cols_diag, cost]
    specs = [pl.BlockSpec(memory_space=pltpu.SMEM)] + specs + [array] * (3 + len(sides))
    aliases = {}
    if before is not None:
        aliases = {len(operands): 0}
        operands.append(before)
        specs.append(pl.BlockSpec(memory_space=pl.ANY))
    return pl.pallas_call(
        functools.partial(plant_kernel, start, last, len(sides)),
        grid=(count,),
        in_specs=specs,
        out_specs=pl.BlockSpec((rows, LINE), lambda b: (0, b + start)),
        out_shape=jax.ShapeDtypeStruct(value.shape, F32),
        input_output_aliases=aliases,
        compiler_params=pltpu.CompilerParams(vmem_limit_bytes=VMEM_LIMIT),
        cost_estimate=pl.CostEstimate(flops=32 << 20, bytes_accessed=16 << 20, transcendentals=0),
    )(*operands)


def device_of(line):
    chip_row, core, col = line % 8, (line // 8) % 2, line // 16
    return (chip_row * 2 + core) * 8 + col


def local(value_matrix, inputs, plant_diag, state_cost, control_weight):
    row_index = lax.axis_index("row")
    col_index = lax.axis_index("col")
    both = ("row", "col")
    grid_side = plant_diag.shape[0]
    rows_block, cols_block = value_matrix.shape
    actuators = inputs.shape[1]
    lines_rows = rows_block // grid_side
    lines_cols = cols_block // grid_side
    diag_rows = lax.dynamic_slice_in_dim(plant_diag, row_index * lines_rows, lines_rows, 0)
    diag_cols = lax.dynamic_slice_in_dim(plant_diag, col_index * lines_cols, lines_cols, 0)
    me = row_index.astype(jnp.int32).reshape(1)
    trade = [((a * 2 + core) * 8 + b, (b * 2 + core) * 8 + a) for a in range(8) for b in range(8) for core in range(2)]
    mine_inputs = lax.dynamic_slice_in_dim(inputs, col_index * LINE, LINE, 0)
    mine_inputs = lax.ppermute(mine_inputs, both, trade)

    def shifted(x, axis, by):
        count = lax.axis_size(axis)
        return lax.ppermute(x, axis, [(i, i + by) for i in range(count) if 0 <= i + by < count])

    above = shifted(value_matrix[-LINE:], "row", 1)
    below = shifted(value_matrix[:LINE], "row", -1)
    tall = lambda cols: jnp.concatenate([above[:, cols], value_matrix[:, cols], below[:, cols]], 0)
    left = shifted(tall(slice(-LINE, None)), "col", 1)
    right = shifted(tall(slice(None, LINE)), "col", -1)
    operands = (
        jnp.stack([row_index * lines_rows, col_index * lines_cols]).astype(jnp.int32),
        value_matrix,
        above,
        below,
        left,
        right,
        diag_rows.T,
        diag_cols,
        state_cost.reshape(lines_rows, grid_side),
    )
    odd = product_lines(me, value_matrix, inputs, 1)
    even = product_lines(me, value_matrix, inputs, 0)
    held = {}

    def first_wait(c_got, d_got):
        base = plant_part(4, 4, *operands[:4], None, None, *operands[6:], None)
        base = plant_part(8, 4, *operands[:4], None, None, *operands[6:], base)
        c_got, d_got, held["base"] = tied(c_got, d_got, base)
        return c_got, d_got

    def second_wait(came):
        came, held["inputs"], held["left"], held["right"] = tied(came, mine_inputs, left, right)
        return came

    product = scatter_lines(even, odd, first_wait, second_wait)
    mine_inputs = held["inputs"]
    operands = (*operands[:4], held["left"], held["right"], *operands[6:])

    gram = gram_blocks(mine_inputs, product)
    product, gram = tied(product, gram)
    core, x_low, y = row_index & 1, (row_index >> 1) & 1, row_index >> 2
    x_high, z = col_index & 1, col_index >> 1
    x_place = x_high * 2 + x_low

    lines = grid_side
    over = lax.ppermute(product, both, [(device_of(i), device_of(i + 1)) for i in range(lines - 1)])
    under = lax.ppermute(product, both, [(device_of(i + 1), device_of(i)) for i in range(lines - 1)])

    def third_wait(*got):
        base = plant_part(0, 4, *operands, held["base"])
        *got, held["base"] = tied(*got, base)
        return got

    total = sum_start(gram.reshape(10 * PANEL, PANEL), core, y, third_wait)
    line = col_index * 16 + line_of(row_index)
    diagonal = lax.dynamic_slice_in_dim(plant_diag, line, 1, 0)
    gain = stencil_first(jnp.stack([over, product, under]), diagonal)[0]
    gain, total = tied(gain, total)

    gain_cols = lax.all_gather(gain, "row", axis=0)
    traded = lax.ppermute(gain, both, trade)
    total = sum_middle(total, x_place)
    traded, total = tied(traded, total)

    pair, quad = gather_rows_start(traded)
    total = sum_spread(total, x_place, y)
    pair, quad, total = tied(pair, quad, total)

    sides = gather_rows_end(pair, quad)
    base = plant_part(12, 4, *operands, held["base"])
    total = joined(total, swap(total, CORE), core == 1)
    total, base = tied(total, base)
    factors = factored(control_weight, total.reshape(10, PANEL, PANEL))
    solved = solve(jnp.stack([z, x_high]).astype(jnp.int32), factors, sides)
    return downdate(solved, gain_cols, base)


def solution(mesh):
    in_specs = (P("row", "col"), P("row", None), P(), P("row"), P())
    out_specs = P("row", "col")
    return jax.shard_map(local, mesh=mesh, in_specs=in_specs, out_specs=out_specs, check_vma=False)
```

```python
import functools

import jax
import jax.numpy as jnp
from jax import lax
from jax.experimental import pallas as pl
from jax.experimental.pallas import tpu as pltpu
from jax.sharding import PartitionSpec as P

COUPLING = 0.25
F32 = jnp.float32
BF16 = jnp.bfloat16
NN = (((1,), (0,)), ((), ()))
NT = (((1,), (1,)), ((), ()))
TN = (((0,), (0,)), ((), ()))
LINE = 128
PANEL = 256
VMEM_LIMIT = 56 << 20


def split(x):
    high = x.astype(BF16)
    return high, (x - high.astype(F32)).astype(BF16)


def dot1(a, b, dims):
    return lax.dot_general(a, b, dims, preferred_element_type=F32)


def dot3(a, b, dims):
    (a_high, a_low), (b_high, b_low) = a, b
    return dot1(a_high, b_high, dims) + dot1(a_high, b_low, dims) + dot1(a_low, b_high, dims)


def line_of(device):
    return (device & 1) * 8 + (device >> 1)


def product_kernel(me_ref, first, second, inputs, out, high, low):
    @pl.when(pl.program_id(0) == 0)
    def _():
        high[...], low[...] = split(inputs[...])

    lines = split(jnp.concatenate([first[...], second[...]], 1))
    out[...] = dot3(lines, (high[...], low[...]), TN).reshape(out.shape)


def product_lines(me, value_matrix, inputs, odd):
    rows, acts = inputs.shape
    return pl.pallas_call(
        product_kernel,
        grid_spec=pltpu.PrefetchScalarGridSpec(
            num_scalar_prefetch=1,
            grid=(4,),
            in_specs=[
                pl.BlockSpec((rows, LINE), lambda i, m: (0, line_of(m[0] ^ (4 * i + odd)))),
                pl.BlockSpec((rows, LINE), lambda i, m: (0, line_of(m[0] ^ (4 * i + 2 + odd)))),
                pl.BlockSpec((rows, acts), lambda i, m: (0, 0)),
            ],
            out_specs=pl.BlockSpec((2, LINE, acts), lambda i, m: (i, 0, 0)),
            scratch_shapes=[pltpu.VMEM((rows, acts), BF16)] * 2,
        ),
        out_shape=jax.ShapeDtypeStruct((8, LINE, acts), F32),
        compiler_params=pltpu.CompilerParams(vmem_limit_bytes=VMEM_LIMIT),
        cost_estimate=pl.CostEstimate(flops=1 << 20, bytes_accessed=1 << 20, transcendentals=0),
    )(me, value_matrix, value_matrix, inputs)


def swap(x, mask):
    return lax.ppermute(x, ("row", "col"), [(i, i ^ mask) for i in range(128)])


CORE, X_LOW, X_HIGH = 8, 16, 1
Y = (0, 32, 64, 96)
Z = (0, 2, 4, 6)
X = (0, 16, 1, 17)


def y_first(near, blocks):
    return swap(jnp.stack([blocks[near], blocks[2]]), Y[near])


def y_second(near, blocks, got):
    far = 4 - near
    kept = blocks[far] + got[1]
    return blocks[0] + got[0] + swap(kept, Y[far])


def scatter_lines(even, odd, begun, first_wait, second_wait, third_wait):
    got = begun(swap(odd, CORE))
    quarter = LINE // 4
    cut = lambda i, q: even[i, q * quarter : (q + 1) * quarter] + got[i, q * quarter : (q + 1) * quarter]
    half = lambda i, q: jnp.concatenate([cut(i, q), cut(i, q + 1)], 0)
    pair = lambda m, q: jnp.stack([cut(2 * m, q), cut(2 * m + 1, q)])
    came = swap(jnp.stack([half(2 * m + 1, 0) for m in range(4)]), X_LOW)
    c = [pair(m, 2) for m in range(4)]
    d = [pair(m, 3) for m in range(4)]
    c_got, d_got = first_wait(y_first(1, c), y_first(3, d))
    c, d = y_second(1, c, c_got), y_second(3, d, d_got)
    came = second_wait(came)
    own = [half(2 * m, 0) + came[m] for m in range(4)]
    a = [o[:quarter] for o in own]
    b = [o[quarter:] for o in own]
    a_got, b_got = third_wait(y_first(1, a), y_first(3, b))
    a, b = y_second(1, a, a_got), y_second(3, b, b_got)
    rest = jnp.concatenate([c[0], d[0]], 0) + swap(jnp.concatenate([c[1], d[1]], 0), X_LOW)
    return jnp.concatenate([a, b, rest], 0)


def halves(x, bit):
    count = x.shape[0] // 2
    low, high = x[:count], x[count:]
    return jnp.where(bit, high, low), jnp.where(bit, low, high)


def joined(mine, got, bit):
    return jnp.concatenate([jnp.where(bit, got, mine), jnp.where(bit, mine, got)], 0)


def scatter_four(x, place, masks):
    count = x.shape[0] // 4
    own = lambda m: lax.dynamic_slice_in_dim(x, (place ^ m) * count, count, 0)
    return own(0) + swap(own(1), masks[1]) + swap(own(2), masks[2]) + swap(own(3), masks[3])


def gather_four(x, place, masks):
    parts = jnp.stack([x] + [swap(x, masks[m]) for m in range(1, 4)])
    return jnp.concatenate([lax.dynamic_index_in_dim(parts, place ^ m, 0, False) for m in range(4)], 0)


def tied(*values):
    return lax.optimization_barrier(values)


def sum_start(x, core, z, x_place):
    keep, send = halves(x, core == 1)
    x = keep + swap(send, CORE)
    return scatter_four(scatter_four(x, z, Z), x_place, X)


def sum_middle(x):
    return x + swap(x, Y[1]) + swap(x, Y[2]) + swap(x, Y[3])


def sum_spread(x, x_place, z):
    return gather_four(gather_four(x, x_place, X), z, Z)


def gather_rows_start(line):
    first, second = line[: LINE // 2], line[LINE // 2 :]
    pair = jnp.stack([first, swap(first, X_HIGH)])
    quad = jnp.stack([second] + [swap(second, Z[m]) for m in range(1, 4)])
    return pair, quad


def gather_rows_end(pair, quad):
    return [pair] + [swap(pair, Z[m]) for m in range(1, 4)] + [quad, swap(quad, X_HIGH)]


def gram_kernel(inputs, product, out):
    a = split(inputs[...])
    b = split(product[...])
    at = 0
    for k in range(4):
        for i in range(k, 4):
            left = [part[:, i * PANEL : (i + 1) * PANEL] for part in a]
            right = [part[:, k * PANEL : (k + 1) * PANEL] for part in b]
            out[at] = dot3(left, right, TN)
            at += 1


def gram_blocks(inputs, product):
    return pl.pallas_call(
        gram_kernel,
        out_shape=jax.ShapeDtypeStruct((10, PANEL, PANEL), F32),
        compiler_params=pltpu.CompilerParams(vmem_limit_bytes=VMEM_LIMIT),
    )(inputs, product)


def block_index(i, k):
    return k * 4 - (k * (k - 1)) // 2 + i - k


def series_inverse(a, eye, mask):
    picked = jnp.where(mask, a, 0.0)
    across = lax.rsqrt(jnp.sum(picked, axis=0, keepdims=True))
    down = lax.rsqrt(jnp.sum(picked, axis=1, keepdims=True))
    error = jnp.where(mask, 0.0, -(a * across * down))
    result = eye + error
    for _ in range(3):
        parts = split(error)
        error = dot3(parts, parts, NN)
        result = result + dot3(split(result), split(error), NN)
    short = error.astype(BF16)
    error = dot1(short, short, NN)
    result = result + dot1(result.astype(BF16), error.astype(BF16), NN)
    return result * across * down, jnp.sum(error * error, keepdims=True)


def pivot_inverse(a, work):
    size = a.shape[0]
    work[...] = a
    lanes = lax.broadcasted_iota(jnp.int32, (1, size), 1)
    rows = lax.broadcasted_iota(jnp.int32, (size, 1), 0)

    def step(p, carry):
        now = work[...]
        across = work[pl.ds(p, 1), :]
        down = jnp.sum(jnp.where(lanes == p, now, 0.0), axis=1, keepdims=True)
        inverse = 1.0 / jnp.sum(jnp.where(lanes == p, across, 0.0), axis=1, keepdims=True)
        new = now - down * (across * inverse)
        new = jnp.where(lanes == p, down * inverse, new)
        new = jnp.where(rows == p, across * inverse, new)
        work[...] = jnp.where((rows == p) & (lanes == p), -inverse, new)
        return carry

    lax.fori_loop(0, size, step, 0)
    return -work[...]


def factor_kernel(weight, gram, factor, inverses, work, worst):
    size = PANEL
    mask = lax.broadcasted_iota(jnp.int32, (size, size), 0) == lax.broadcasted_iota(jnp.int32, (size, size), 1)
    eye = jnp.where(mask, 1.0, 0.0).astype(F32)

    def run(robust):
        for k in range(4):
            for i in range(k, 4):
                here = gram[block_index(i, k)]
                factor[block_index(i, k)] = here + weight[0] * eye if i == k else here
        for k in range(4):
            here = factor[block_index(k, k)]
            if robust:
                inverse = pivot_inverse(here, work)
            else:
                inverse, off = series_inverse(here, eye, mask)
                worst[...] = off if k == 0 else jnp.where(off < worst[...], worst[...], off)
            inverses[k] = inverse
            parts = split(inverse)
            columns = [split(factor[block_index(i, k)]) for i in range(k + 1, 4)]
            lefts = []
            for i in range(k + 1, 4):
                left = dot3(columns[i - k - 1], parts, NN)
                factor[block_index(i, k)] = left
                lefts.append(split(left))
            for j in range(k + 1, 4):
                for i in range(j, 4):
                    factor[block_index(i, j)] -= dot3(lefts[i - k - 1], columns[j - k - 1], NT)

    run(False)

    @pl.when(jnp.logical_not(worst[0, 0] < 1e-6))
    def _():
        run(True)


def factored(weight, gram):
    scalar = pl.BlockSpec(memory_space=pltpu.SMEM)
    array = pl.BlockSpec(memory_space=pltpu.VMEM)
    return pl.pallas_call(
        factor_kernel,
        out_shape=[
            jax.ShapeDtypeStruct((10, PANEL, PANEL), F32),
            jax.ShapeDtypeStruct((4, PANEL, PANEL), F32),
        ],
        in_specs=[scalar, array],
        out_specs=[array, array],
        scratch_shapes=[pltpu.VMEM((PANEL, PANEL), F32), pltpu.VMEM((1, 1), F32)],
        compiler_params=pltpu.CompilerParams(vmem_limit_bytes=VMEM_LIMIT),
        cost_estimate=pl.CostEstimate(flops=9 << 30, bytes_accessed=12 << 20, transcendentals=0),
    )(weight, gram)


def solve_kernel(place, factor, inverses, own, near, across, far, quad, other, high, low, out):
    size = PANEL
    half = LINE // 2
    at = lambda k: slice(k * size, (k + 1) * size)

    def put(step, e, second, value):
        line = (place[0] ^ step) * 2 + (place[1] ^ e)
        out[pl.ds(pl.multiple_of(line * LINE + second * half, half), half), :] = value

    for step, pair in enumerate((own, near, across, far)):
        for e in range(2):
            put(step, e, 0, pair[e])
    for e, lines in enumerate((quad, other)):
        for step in range(4):
            put(step, e, 1, lines[step])
    for k in range(4):
        solved = split(out[:, at(k)])
        for i in range(k + 1, 4):
            out[:, at(i)] -= dot3(solved, split(factor[block_index(i, k)]), NT)
    for k in range(3, -1, -1):
        total = dot3(split(out[:, at(k)]), split(inverses[k]), NN)
        for i in range(k + 1, 4):
            total = total - dot3((high[:, at(i)], low[:, at(i)]), split(factor[block_index(i, k)]), NN)
        high[:, at(k)], low[:, at(k)] = split(total)


def solve(place, factors, sides):
    scalar = pl.BlockSpec(memory_space=pltpu.SMEM)
    array = pl.BlockSpec(memory_space=pltpu.VMEM)
    size = 8 * LINE
    return pl.pallas_call(
        solve_kernel,
        out_shape=[jax.ShapeDtypeStruct((size, 4 * PANEL), BF16)] * 2,
        in_specs=[scalar] + [array] * 8,
        out_specs=[array, array],
        scratch_shapes=[pltpu.VMEM((size, 4 * PANEL), F32)],
        compiler_params=pltpu.CompilerParams(vmem_limit_bytes=VMEM_LIMIT),
        cost_estimate=pl.CostEstimate(flops=9 << 30, bytes_accessed=12 << 20, transcendentals=0),
    )(place, *factors, *sides)


def downdate_kernel(high, low, first, second, base, out):
    lines = split(jnp.concatenate([first[0], second[0]], 0))
    out[...] = base[...] - dot3((high[...], low[...]), lines, NT)


def downdate(solved, gain_cols, base):
    rows, acts = solved[0].shape
    whole = pl.BlockSpec((rows, acts), lambda b: (0, 0))
    line = lambda b: (b % 8) * 2 + b // 8
    block = pl.BlockSpec((rows, 2 * LINE), lambda b: (0, b))
    return pl.pallas_call(
        downdate_kernel,
        grid=(8,),
        in_specs=[
            whole,
            whole,
            pl.BlockSpec((1, LINE, acts), lambda b: (line(2 * b), 0, 0)),
            pl.BlockSpec((1, LINE, acts), lambda b: (line(2 * b + 1), 0, 0)),
            block,
        ],
        out_specs=block,
        out_shape=jax.ShapeDtypeStruct(base.shape, F32),
        compiler_params=pltpu.CompilerParams(vmem_limit_bytes=VMEM_LIMIT),
        cost_estimate=pl.CostEstimate(flops=12 << 30, bytes_accessed=28 << 20, transcendentals=0),
    )(*solved, gain_cols, gain_cols, base)


def stencil_first(field, diagonal):
    centre = field[1:-1]
    side_padded = jnp.pad(centre, ((0, 0), (1, 1), (0, 0)))
    neighbours = field[:-2] + field[2:] + side_padded[:, :-2] + side_padded[:, 2:]
    return diagonal[:, :, None] * centre + COUPLING * neighbours


def plant_kernel(start, last, sides, place, *refs):
    blocks, ends = refs[:9], refs[9 : 9 + sides]
    rows_diag, cols_diag, cost = refs[9 + sides : 12 + sides]
    out = refs[-1]
    b = pl.program_id(0) + start
    rows = out.shape[0]
    lanes = lax.broadcasted_iota(jnp.int32, (1, LINE), 1)
    inner = lax.broadcasted_iota(jnp.int32, (LINE, 1), 0)
    column = lambda k: jnp.concatenate([blocks[3 * k][...], blocks[3 * k + 1][...], blocks[3 * k + 2][...]], 0)
    here = column(1)
    before, after = column(0), column(2)
    if sides:
        before = jnp.where(b == 0, ends[0][...], before)
        after = jnp.where(b == last, ends[1][...], after)
    sides = jnp.where(lanes == 0, 0.0, pltpu.roll(here, 1, 1)) + jnp.where(
        lanes == LINE - 1, 0.0, pltpu.roll(here, LINE - 1, 1)
    )
    field = cols_diag[pl.ds(b, 1), :] * here + COUPLING * (before + after + sides)
    for a in range(rows // LINE):
        line = lambda k: field[(a + k) * LINE : (a + k + 1) * LINE]
        centre = line(1)
        sides = jnp.where(inner == 0, 0.0, pltpu.roll(centre, 1, 0)) + jnp.where(
            inner == LINE - 1, 0.0, pltpu.roll(centre, LINE - 1, 0)
        )
        new = rows_diag[:, a : a + 1] * centre + COUPLING * (line(0) + line(2) + sides)
        on_diagonal = (inner == lanes) & (place[0] + a == place[1] + b)
        out[a * LINE : (a + 1) * LINE, :] = new + jnp.where(on_diagonal, cost[a : a + 1, :], 0.0)


def plant_part(start, count, place, value, above, below, left, right, rows_diag, cols_diag, cost, before):
    rows, cols = value.shape
    last = cols // LINE - 1
    array = pl.BlockSpec(memory_space=pltpu.VMEM)
    blocks, specs = [], []
    for step in (-1, 0, 1):
        index = lambda b, step=step: (0, jnp.clip(b + start + step, 0, last))
        for x in (above, value, below):
            blocks.append(x)
            specs.append(pl.BlockSpec((x.shape[0], LINE), index))
    sides = [] if left is None else [left, right]
    operands = [place, *blocks, *sides, rows_diag, cols_diag, cost]
    specs = [pl.BlockSpec(memory_space=pltpu.SMEM)] + specs + [array] * (3 + len(sides))
    aliases = {}
    if before is not None:
        aliases = {len(operands): 0}
        operands.append(before)
        specs.append(pl.BlockSpec(memory_space=pl.ANY))
    return pl.pallas_call(
        functools.partial(plant_kernel, start, last, len(sides)),
        grid=(count,),
        in_specs=specs,
        out_specs=pl.BlockSpec((rows, LINE), lambda b: (0, b + start)),
        out_shape=jax.ShapeDtypeStruct(value.shape, F32),
        input_output_aliases=aliases,
        compiler_params=pltpu.CompilerParams(vmem_limit_bytes=VMEM_LIMIT),
        cost_estimate=pl.CostEstimate(flops=32 << 20, bytes_accessed=16 << 20, transcendentals=0),
    )(*operands)


def device_of(line):
    chip_row, core, col = line % 8, (line // 8) % 2, line // 16
    return (chip_row * 2 + core) * 8 + col


def local(value_matrix, inputs, plant_diag, state_cost, control_weight):
    row_index = lax.axis_index("row")
    col_index = lax.axis_index("col")
    both = ("row", "col")
    grid_side = plant_diag.shape[0]
    rows_block, cols_block = value_matrix.shape
    actuators = inputs.shape[1]
    lines_rows = rows_block // grid_side
    lines_cols = cols_block // grid_side
    diag_rows = lax.dynamic_slice_in_dim(plant_diag, row_index * lines_rows, lines_rows, 0)
    diag_cols = lax.dynamic_slice_in_dim(plant_diag, col_index * lines_cols, lines_cols, 0)
    me = row_index.astype(jnp.int32).reshape(1)
    trade = [((a * 2 + core) * 8 + b, (b * 2 + core) * 8 + a) for a in range(8) for b in range(8) for core in range(2)]
    mine_inputs = lax.dynamic_slice_in_dim(inputs, col_index * LINE, LINE, 0)
    mine_inputs = lax.ppermute(mine_inputs, both, trade)

    def shifted(x, axis, by):
        count = lax.axis_size(axis)
        return lax.ppermute(x, axis, [(i, i + by) for i in range(count) if 0 <= i + by < count])

    above = shifted(value_matrix[-LINE:], "row", 1)
    below = shifted(value_matrix[:LINE], "row", -1)
    tall = lambda cols: jnp.concatenate([above[:, cols], value_matrix[:, cols], below[:, cols]], 0)
    left = shifted(tall(slice(-LINE, None)), "col", 1)
    right = shifted(tall(slice(None, LINE)), "col", -1)
    operands = (
        jnp.stack([row_index * lines_rows, col_index * lines_cols]).astype(jnp.int32),
        value_matrix,
        above,
        below,
        left,
        right,
        diag_rows.T,
        diag_cols,
        state_cost.reshape(lines_rows, grid_side),
    )
    odd = product_lines(me, value_matrix, inputs, 1)
    even = product_lines(me, value_matrix, inputs, 0)
    held = {}

    def begun(got):
        got, held["above"], held["below"] = tied(got, above, below)
        return got

    def first_wait(c_got, d_got):
        middle = (*operands[:2], held["above"], held["below"], None, None, *operands[6:])
        base = plant_part(4, 4, *middle, None)
        base = plant_part(8, 4, *middle, base)
        c_got, d_got, held["base"] = tied(c_got, d_got, base)
        return c_got, d_got

    def second_wait(came):
        came, held["inputs"] = tied(came, mine_inputs)
        return came

    def third_wait(a_got, b_got):
        a_got, b_got, held["left"], held["right"] = tied(a_got, b_got, left, right)
        return a_got, b_got

    product = scatter_lines(even, odd, begun, first_wait, second_wait, third_wait)
    mine_inputs = held["inputs"]
    operands = (*operands[:2], held["above"], held["below"], held["left"], held["right"], *operands[6:])

    gram = gram_blocks(mine_inputs, product)
    product, gram = tied(product, gram)
    core, x_low, y = row_index & 1, (row_index >> 1) & 1, row_index >> 2
    x_high, z = col_index & 1, col_index >> 1
    x_place = x_high * 2 + x_low

    lines = grid_side
    over = lax.ppermute(product, both, [(device_of(i), device_of(i + 1)) for i in range(lines - 1)])
    under = lax.ppermute(product, both, [(device_of(i + 1), device_of(i)) for i in range(lines - 1)])
    total = sum_start(gram.reshape(10 * PANEL, PANEL), core, z, x_place)
    line = col_index * 16 + line_of(row_index)
    diagonal = lax.dynamic_slice_in_dim(plant_diag, line, 1, 0)
    gain = stencil_first(jnp.stack([over, product, under]), diagonal)[0]
    gain, total = tied(gain, total)
    total = sum_middle(total)
    gain, total = tied(gain, total)
    traded = lax.ppermute(gain, both, trade)
    total = sum_spread(total, x_place, z)
    traded, gain, total = tied(traded, gain, total)

    gain_cols = lax.all_gather(gain, "row", axis=0)
    pair, quad = gather_rows_start(traded)
    total = joined(total, swap(total, CORE), core == 1)
    base = plant_part(0, 4, *operands, held["base"])
    pair, quad, total, base = tied(pair, quad, total, base)
    sides = gather_rows_end(pair, quad)
    factors = factored(control_weight, total.reshape(10, PANEL, PANEL))
    *factors, base = tied(*factors, base)
    base = plant_part(12, 4, *operands, base)
    *sides, base = tied(*sides, base)
    solved = solve(jnp.stack([z, x_high]).astype(jnp.int32), factors, sides)
    return downdate(solved, gain_cols, base)


def solution(mesh):
    in_specs = (P("row", "col"), P("row", None), P(), P("row"), P())
    out_specs = P("row", "col")
    return jax.shard_map(local, mesh=mesh, in_specs=in_specs, out_specs=out_specs, check_vma=False)
```

```python
import functools

import jax
import jax.numpy as jnp
from jax import lax
from jax.experimental import pallas as pl
from jax.experimental.pallas import tpu as pltpu
from jax.sharding import PartitionSpec as P

COUPLING = 0.25
F32 = jnp.float32
BF16 = jnp.bfloat16
NN = (((1,), (0,)), ((), ()))
NT = (((1,), (1,)), ((), ()))
TN = (((0,), (0,)), ((), ()))
LINE = 128
PANEL = 256
VMEM_LIMIT = 56 << 20


def split(x):
    high = x.astype(BF16)
    return high, (x - high.astype(F32)).astype(BF16)


def dot1(a, b, dims):
    return lax.dot_general(a, b, dims, preferred_element_type=F32)


def dot3(a, b, dims):
    (a_high, a_low), (b_high, b_low) = a, b
    return dot1(a_high, b_high, dims) + dot1(a_high, b_low, dims) + dot1(a_low, b_high, dims)


def line_of(device):
    return (device & 1) * 8 + (device >> 1)


def product_kernel(me_ref, first, second, inputs, out, high, low):
    @pl.when(pl.program_id(0) == 0)
    def _():
        high[...], low[...] = split(inputs[...])

    lines = split(jnp.concatenate([first[...], second[...]], 1))
    out[...] = dot3(lines, (high[...], low[...]), TN).reshape(out.shape)


def product_lines(me, value_matrix, inputs, odd):
    rows, acts = inputs.shape
    return pl.pallas_call(
        product_kernel,
        grid_spec=pltpu.PrefetchScalarGridSpec(
            num_scalar_prefetch=1,
            grid=(4,),
            in_specs=[
                pl.BlockSpec((rows, LINE), lambda i, m: (0, line_of(m[0] ^ (4 * i + odd)))),
                pl.BlockSpec((rows, LINE), lambda i, m: (0, line_of(m[0] ^ (4 * i + 2 + odd)))),
                pl.BlockSpec((rows, acts), lambda i, m: (0, 0)),
            ],
            out_specs=pl.BlockSpec((2, LINE, acts), lambda i, m: (i, 0, 0)),
            scratch_shapes=[pltpu.VMEM((rows, acts), BF16)] * 2,
        ),
        out_shape=jax.ShapeDtypeStruct((8, LINE, acts), F32),
        compiler_params=pltpu.CompilerParams(vmem_limit_bytes=VMEM_LIMIT),
        cost_estimate=pl.CostEstimate(flops=1 << 20, bytes_accessed=1 << 20, transcendentals=0),
    )(me, value_matrix, value_matrix, inputs)


def swap(x, mask):
    return lax.ppermute(x, ("row", "col"), [(i, i ^ mask) for i in range(128)])


CORE, X_LOW, X_HIGH = 8, 16, 1
Y = (0, 32, 64, 96)
Z = (0, 2, 4, 6)
X = (0, 16, 1, 17)


def y_first(near, blocks):
    return swap(jnp.stack([blocks[near], blocks[2]]), Y[near])


def y_second(near, blocks, got):
    far = 4 - near
    kept = blocks[far] + got[1]
    return blocks[0] + got[0] + swap(kept, Y[far])


def scatter_lines(even, odd, begun, first_wait, second_wait, third_wait):
    got = begun(swap(odd, CORE))
    quarter = LINE // 4
    cut = lambda i, q: even[i, q * quarter : (q + 1) * quarter] + got[i, q * quarter : (q + 1) * quarter]
    half = lambda i, q: jnp.concatenate([cut(i, q), cut(i, q + 1)], 0)
    pair = lambda m, q: jnp.stack([cut(2 * m, q), cut(2 * m + 1, q)])
    came = swap(jnp.stack([half(2 * m + 1, 0) for m in range(4)]), X_LOW)
    c = [pair(m, 2) for m in range(4)]
    d = [pair(m, 3) for m in range(4)]
    c_got, d_got = first_wait(y_first(1, c), y_first(3, d))
    c, d = y_second(1, c, c_got), y_second(3, d, d_got)
    came = second_wait(came)
    own = [half(2 * m, 0) + came[m] for m in range(4)]
    a = [o[:quarter] for o in own]
    b = [o[quarter:] for o in own]
    a_got, b_got = third_wait(y_first(1, a), y_first(3, b))
    a, b = y_second(1, a, a_got), y_second(3, b, b_got)
    rest = jnp.concatenate([c[0], d[0]], 0) + swap(jnp.concatenate([c[1], d[1]], 0), X_LOW)
    return jnp.concatenate([a, b, rest], 0)


def halves(x, bit):
    count = x.shape[0] // 2
    low, high = x[:count], x[count:]
    return jnp.where(bit, high, low), jnp.where(bit, low, high)


def joined(mine, got, bit):
    return jnp.concatenate([jnp.where(bit, got, mine), jnp.where(bit, mine, got)], 0)


def scatter_four(x, place, masks):
    count = x.shape[0] // 4
    own = lambda m: lax.dynamic_slice_in_dim(x, (place ^ m) * count, count, 0)
    return own(0) + swap(own(1), masks[1]) + swap(own(2), masks[2]) + swap(own(3), masks[3])


def gather_four(x, place, masks):
    parts = jnp.stack([x] + [swap(x, masks[m]) for m in range(1, 4)])
    return jnp.concatenate([lax.dynamic_index_in_dim(parts, place ^ m, 0, False) for m in range(4)], 0)


def tied(*values):
    return lax.optimization_barrier(values)


def sum_cores(x, core):
    keep, send = halves(x, core == 1)
    return keep + swap(send, CORE)


def sum_rest(x, x_place, z):
    x = x + swap(x, Y[1]) + swap(x, Y[2]) + swap(x, Y[3])
    return gather_four(gather_four(x, x_place, X), z, Z)


def gather_rows_start(line):
    first, second = line[: LINE // 2], line[LINE // 2 :]
    pair = jnp.stack([first, swap(first, X_HIGH)])
    quad = jnp.stack([second] + [swap(second, Z[m]) for m in range(1, 4)])
    return pair, quad


def gather_rows_end(pair, quad):
    return [pair] + [swap(pair, Z[m]) for m in range(1, 4)] + [quad, swap(quad, X_HIGH)]


def gram_kernel(inputs, product, out):
    a = split(inputs[...])
    b = split(product[...])
    at = 0
    for k in range(4):
        for i in range(k, 4):
            left = [part[:, i * PANEL : (i + 1) * PANEL] for part in a]
            right = [part[:, k * PANEL : (k + 1) * PANEL] for part in b]
            out[at] = dot3(left, right, TN)
            at += 1


def gram_blocks(inputs, product):
    return pl.pallas_call(
        gram_kernel,
        out_shape=jax.ShapeDtypeStruct((10, PANEL, PANEL), F32),
        compiler_params=pltpu.CompilerParams(vmem_limit_bytes=VMEM_LIMIT),
        cost_estimate=pl.CostEstimate(flops=1 << 20, bytes_accessed=1 << 20, transcendentals=0),
    )(inputs, product)


def block_index(i, k):
    return k * 4 - (k * (k - 1)) // 2 + i - k


def series_inverse(a, eye, mask):
    picked = jnp.where(mask, a, 0.0)
    across = lax.rsqrt(jnp.sum(picked, axis=0, keepdims=True))
    down = lax.rsqrt(jnp.sum(picked, axis=1, keepdims=True))
    error = jnp.where(mask, 0.0, -(a * across * down))
    result = eye + error
    for _ in range(3):
        parts = split(error)
        error = dot3(parts, parts, NN)
        result = result + dot3(split(result), split(error), NN)
    short = error.astype(BF16)
    error = dot1(short, short, NN)
    result = result + dot1(result.astype(BF16), error.astype(BF16), NN)
    return result * across * down, jnp.sum(error * error, keepdims=True)


def pivot_inverse(a, work):
    size = a.shape[0]
    work[...] = a
    lanes = lax.broadcasted_iota(jnp.int32, (1, size), 1)
    rows = lax.broadcasted_iota(jnp.int32, (size, 1), 0)

    def step(p, carry):
        now = work[...]
        across = work[pl.ds(p, 1), :]
        down = jnp.sum(jnp.where(lanes == p, now, 0.0), axis=1, keepdims=True)
        inverse = 1.0 / jnp.sum(jnp.where(lanes == p, across, 0.0), axis=1, keepdims=True)
        new = now - down * (across * inverse)
        new = jnp.where(lanes == p, down * inverse, new)
        new = jnp.where(rows == p, across * inverse, new)
        work[...] = jnp.where((rows == p) & (lanes == p), -inverse, new)
        return carry

    lax.fori_loop(0, size, step, 0)
    return -work[...]


def factor_kernel(weight, gram, factor, inverses, work, worst):
    size = PANEL
    mask = lax.broadcasted_iota(jnp.int32, (size, size), 0) == lax.broadcasted_iota(jnp.int32, (size, size), 1)
    eye = jnp.where(mask, 1.0, 0.0).astype(F32)

    def run(robust):
        for k in range(4):
            for i in range(k, 4):
                here = gram[block_index(i, k)]
                factor[block_index(i, k)] = here + weight[0] * eye if i == k else here
        for k in range(4):
            here = factor[block_index(k, k)]
            if robust:
                inverse = pivot_inverse(here, work)
            else:
                inverse, off = series_inverse(here, eye, mask)
                worst[...] = off if k == 0 else jnp.where(off < worst[...], worst[...], off)
            inverses[k] = inverse
            parts = split(inverse)
            columns = [split(factor[block_index(i, k)]) for i in range(k + 1, 4)]
            lefts = []
            for i in range(k + 1, 4):
                left = dot3(columns[i - k - 1], parts, NN)
                factor[block_index(i, k)] = left
                lefts.append(split(left))
            for j in range(k + 1, 4):
                for i in range(j, 4):
                    factor[block_index(i, j)] -= dot3(lefts[i - k - 1], columns[j - k - 1], NT)

    run(False)

    @pl.when(jnp.logical_not(worst[0, 0] < 1e-6))
    def _():
        run(True)


def factored(weight, gram):
    scalar = pl.BlockSpec(memory_space=pltpu.SMEM)
    array = pl.BlockSpec(memory_space=pltpu.VMEM)
    return pl.pallas_call(
        factor_kernel,
        out_shape=[
            jax.ShapeDtypeStruct((10, PANEL, PANEL), F32),
            jax.ShapeDtypeStruct((4, PANEL, PANEL), F32),
        ],
        in_specs=[scalar, array],
        out_specs=[array, array],
        scratch_shapes=[pltpu.VMEM((PANEL, PANEL), F32), pltpu.VMEM((1, 1), F32)],
        compiler_params=pltpu.CompilerParams(vmem_limit_bytes=VMEM_LIMIT),
        cost_estimate=pl.CostEstimate(flops=9 << 30, bytes_accessed=12 << 20, transcendentals=0),
    )(weight, gram)


def solve_kernel(place, factor, inverses, own, near, across, far, quad, other, high, low, out):
    size = PANEL
    half = LINE // 2
    at = lambda k: slice(k * size, (k + 1) * size)

    def put(step, e, second, value):
        line = (place[0] ^ step) * 2 + (place[1] ^ e)
        out[pl.ds(pl.multiple_of(line * LINE + second * half, half), half), :] = value

    for step, pair in enumerate((own, near, across, far)):
        for e in range(2):
            put(step, e, 0, pair[e])
    for e, lines in enumerate((quad, other)):
        for step in range(4):
            put(step, e, 1, lines[step])
    for k in range(4):
        solved = split(out[:, at(k)])
        for i in range(k + 1, 4):
            out[:, at(i)] -= dot3(solved, split(factor[block_index(i, k)]), NT)
    for k in range(3, -1, -1):
        total = dot3(split(out[:, at(k)]), split(inverses[k]), NN)
        for i in range(k + 1, 4):
            total = total - dot3((high[:, at(i)], low[:, at(i)]), split(factor[block_index(i, k)]), NN)
        high[:, at(k)], low[:, at(k)] = split(total)


def solve(place, factors, sides):
    scalar = pl.BlockSpec(memory_space=pltpu.SMEM)
    array = pl.BlockSpec(memory_space=pltpu.VMEM)
    size = 8 * LINE
    return pl.pallas_call(
        solve_kernel,
        out_shape=[jax.ShapeDtypeStruct((size, 4 * PANEL), BF16)] * 2,
        in_specs=[scalar] + [array] * 8,
        out_specs=[array, array],
        scratch_shapes=[pltpu.VMEM((size, 4 * PANEL), F32)],
        compiler_params=pltpu.CompilerParams(vmem_limit_bytes=VMEM_LIMIT),
        cost_estimate=pl.CostEstimate(flops=9 << 30, bytes_accessed=12 << 20, transcendentals=0),
    )(place, *factors, *sides)


def downdate_kernel(high, low, first, second, base, out):
    lines = split(jnp.concatenate([first[0], second[0]], 0))
    out[...] = base[...] - dot3((high[...], low[...]), lines, NT)


def downdate(solved, gain_cols, base):
    rows, acts = solved[0].shape
    whole = pl.BlockSpec((rows, acts), lambda b: (0, 0))
    line = lambda b: (b % 8) * 2 + b // 8
    block = pl.BlockSpec((rows, 2 * LINE), lambda b: (0, b))
    return pl.pallas_call(
        downdate_kernel,
        grid=(8,),
        in_specs=[
            whole,
            whole,
            pl.BlockSpec((1, LINE, acts), lambda b: (line(2 * b), 0, 0)),
            pl.BlockSpec((1, LINE, acts), lambda b: (line(2 * b + 1), 0, 0)),
            block,
        ],
        out_specs=block,
        out_shape=jax.ShapeDtypeStruct(base.shape, F32),
        compiler_params=pltpu.CompilerParams(vmem_limit_bytes=VMEM_LIMIT),
        cost_estimate=pl.CostEstimate(flops=12 << 30, bytes_accessed=28 << 20, transcendentals=0),
    )(*solved, gain_cols, gain_cols, base)


def stencil_first(field, diagonal):
    centre = field[1:-1]
    side_padded = jnp.pad(centre, ((0, 0), (1, 1), (0, 0)))
    neighbours = field[:-2] + field[2:] + side_padded[:, :-2] + side_padded[:, 2:]
    return diagonal[:, :, None] * centre + COUPLING * neighbours


def plant_kernel(start, sizes, place, *refs):
    columns, at = [], 0
    for size in sizes:
        columns.append(refs[at : at + size])
        at += size
    rows_diag, cols_diag, cost = refs[at : at + 3]
    out, window = refs[-2:]
    step = pl.program_id(0)
    b = step + start
    rows = out.shape[0]
    lanes = lax.broadcasted_iota(jnp.int32, (1, LINE), 1)
    inner = lax.broadcasted_iota(jnp.int32, (LINE, 1), 0)
    column = lambda k: jnp.concatenate([ref[...] for ref in columns[k]], 0)

    @pl.when(step == 0)
    def _():
        window[0] = column(0)
        window[1] = column(1)

    here = window[1]
    after = column(2)
    sides = jnp.where(lanes == 0, 0.0, pltpu.roll(here, 1, 1)) + jnp.where(
        lanes == LINE - 1, 0.0, pltpu.roll(here, LINE - 1, 1)
    )
    field = cols_diag[pl.ds(b, 1), :] * here + COUPLING * (window[0] + after + sides)
    window[0] = here
    window[1] = after
    for a in range(rows // LINE):
        line = lambda k: field[(a + k) * LINE : (a + k + 1) * LINE]
        centre = line(1)
        sides = jnp.where(inner == 0, 0.0, pltpu.roll(centre, 1, 0)) + jnp.where(
            inner == LINE - 1, 0.0, pltpu.roll(centre, LINE - 1, 0)
        )
        here = slice(a * LINE, (a + 1) * LINE)
        out[here, :] = rows_diag[here, :] * centre + COUPLING * (line(0) + line(2) + sides)
    mine = place[1] + b - place[0]

    @pl.when((mine >= 0) & (mine < rows // LINE))
    def _():
        here = pl.ds(pl.multiple_of(mine * LINE, LINE), LINE)
        out[here, :] += jnp.where(inner == lanes, cost[pl.ds(mine, 1), :], 0.0)


def plant_part(start, count, place, value, above, below, left, right, rows_diag, cols_diag, cost, before):
    rows, cols = value.shape
    last = cols // LINE - 1
    array = pl.BlockSpec(memory_space=pltpu.VMEM)
    tall = rows + 2 * LINE

    def column(index):
        blocks = (above, value, below)
        return list(blocks), [pl.BlockSpec((x.shape[0], LINE), index) for x in blocks]

    whole = lambda x: ([x], [pl.BlockSpec((tall, LINE), lambda b: (0, 0))])
    columns = [
        whole(left) if start == 0 else column(lambda b: (0, start - 1)),
        column(lambda b: (0, start)),
        whole(right) if start == last else column(lambda b: (0, b + start + 1)),
    ]
    operands, specs = [place], [pl.BlockSpec(memory_space=pltpu.SMEM)]
    for blocks, block_specs in columns:
        operands += blocks
        specs += block_specs
    operands += [rows_diag, cols_diag, cost]
    specs += [array] * 3
    aliases = {}
    if before is not None:
        aliases = {len(operands): 0}
        operands.append(before)
        specs.append(pl.BlockSpec(memory_space=pl.ANY))
    return pl.pallas_call(
        functools.partial(plant_kernel, start, [len(blocks) for blocks, _ in columns]),
        grid=(count,),
        in_specs=specs,
        out_specs=pl.BlockSpec((rows, LINE), lambda b: (0, b + start)),
        out_shape=jax.ShapeDtypeStruct(value.shape, F32),
        scratch_shapes=[pltpu.VMEM((2, tall, LINE), F32)],
        input_output_aliases=aliases,
        compiler_params=pltpu.CompilerParams(vmem_limit_bytes=VMEM_LIMIT),
        cost_estimate=pl.CostEstimate(flops=32 << 20, bytes_accessed=16 << 20, transcendentals=0),
    )(*operands)


def device_of(line):
    chip_row, core, col = line % 8, (line // 8) % 2, line // 16
    return (chip_row * 2 + core) * 8 + col


def local(value_matrix, inputs, plant_diag, state_cost, control_weight):
    row_index = lax.axis_index("row")
    col_index = lax.axis_index("col")
    both = ("row", "col")
    grid_side = plant_diag.shape[0]
    rows_block, cols_block = value_matrix.shape
    actuators = inputs.shape[1]
    lines_rows = rows_block // grid_side
    lines_cols = cols_block // grid_side
    diag_rows = lax.dynamic_slice_in_dim(plant_diag, row_index * lines_rows, lines_rows, 0)
    diag_cols = lax.dynamic_slice_in_dim(plant_diag, col_index * lines_cols, lines_cols, 0)
    me = row_index.astype(jnp.int32).reshape(1)
    trade = [((a * 2 + core) * 8 + b, (b * 2 + core) * 8 + a) for a in range(8) for b in range(8) for core in range(2)]
    mine_inputs = lax.dynamic_slice_in_dim(inputs, col_index * LINE, LINE, 0)
    mine_inputs = lax.ppermute(mine_inputs, both, trade)

    def shifted(x, axis, by):
        count = lax.axis_size(axis)
        return lax.ppermute(x, axis, [(i, i + by) for i in range(count) if 0 <= i + by < count])

    above = shifted(value_matrix[-LINE:], "row", 1)
    below = shifted(value_matrix[:LINE], "row", -1)
    tall = lambda cols: jnp.concatenate([above[:, cols], value_matrix[:, cols], below[:, cols]], 0)
    left = shifted(tall(slice(-LINE, None)), "col", 1)
    right = shifted(tall(slice(None, LINE)), "col", -1)
    operands = (
        jnp.stack([row_index * lines_rows, col_index * lines_cols]).astype(jnp.int32),
        value_matrix,
        above,
        below,
        left,
        right,
        jnp.broadcast_to(diag_rows.reshape(rows_block, 1), (rows_block, LINE)),
        diag_cols,
        state_cost.reshape(lines_rows, grid_side),
    )
    odd = product_lines(me, value_matrix, inputs, 1)
    even = product_lines(me, value_matrix, inputs, 0)
    held = {}

    def begun(got):
        got, held["above"], held["below"] = tied(got, above, below)
        return got

    def first_wait(c_got, d_got):
        middle = (*operands[:2], held["above"], held["below"], None, None, *operands[6:])
        base = plant_part(1, 7, *middle, None)
        base = plant_part(8, 7, *middle, base)
        c_got, d_got, held["base"] = tied(c_got, d_got, base)
        return c_got, d_got

    def second_wait(came):
        came, held["inputs"] = tied(came, mine_inputs)
        return came

    def third_wait(a_got, b_got):
        a_got, b_got, held["left"], held["right"] = tied(a_got, b_got, left, right)
        return a_got, b_got

    product = scatter_lines(even, odd, begun, first_wait, second_wait, third_wait)
    mine_inputs = held["inputs"]
    operands = (*operands[:2], held["above"], held["below"], held["left"], held["right"], *operands[6:])

    core, x_low, y = row_index & 1, (row_index >> 1) & 1, row_index >> 2
    x_high, z = col_index & 1, col_index >> 1
    x_place = x_high * 2 + x_low

    lines = grid_side
    over = lax.ppermute(product, both, [(device_of(i), device_of(i + 1)) for i in range(lines - 1)])
    under = lax.ppermute(product, both, [(device_of(i + 1), device_of(i)) for i in range(lines - 1)])
    gram = gram_blocks(mine_inputs, product)
    total = sum_cores(gram.reshape(10 * PANEL, PANEL), core)
    line = col_index * 16 + line_of(row_index)
    diagonal = lax.dynamic_slice_in_dim(plant_diag, line, 1, 0)
    over, under, total = tied(over, under, total)
    gain = stencil_first(jnp.stack([over, product, under]), diagonal)[0]
    gain, total = tied(gain, total)

    gain_cols = lax.all_gather(gain, "row", axis=0)
    traded = lax.ppermute(gain, both, trade)
    total = scatter_four(total, z, Z)
    traded, total = tied(traded, total)

    pair, quad = gather_rows_start(traded)
    total = scatter_four(total, x_place, X)
    pair, quad, total = tied(pair, quad, total)

    sides = gather_rows_end(pair, quad)
    total = sum_rest(total, x_place, z)
    *sides, total = tied(*sides, total)
    base = plant_part(0, 1, *operands, held["base"])
    base = plant_part(lines_cols - 1, 1, *operands, base)
    total = joined(total, swap(total, CORE), core == 1)
    total, base = tied(total, base)
    factors = factored(control_weight, total.reshape(10, PANEL, PANEL))
    solved = solve(jnp.stack([z, x_high]).astype(jnp.int32), factors, sides)
    return downdate(solved, gain_cols, base)


def solution(mesh):
    in_specs = (P("row", "col"), P("row", None), P(), P("row"), P())
    out_specs = P("row", "col")
    return jax.shard_map(local, mesh=mesh, in_specs=in_specs, out_specs=out_specs, check_vma=False)
```

```python
import functools

import jax
import jax.numpy as jnp
from jax import lax
from jax.experimental import pallas as pl
from jax.experimental.pallas import tpu as pltpu
from jax.sharding import PartitionSpec as P

COUPLING = 0.25
F32 = jnp.float32
BF16 = jnp.bfloat16
NN = (((1,), (0,)), ((), ()))
NT = (((1,), (1,)), ((), ()))
TN = (((0,), (0,)), ((), ()))
LINE = 128
PANEL = 256
VMEM_LIMIT = 56 << 20


def split(x):
    high = x.astype(BF16)
    return high, (x - high.astype(F32)).astype(BF16)


def dot1(a, b, dims):
    return lax.dot_general(a, b, dims, preferred_element_type=F32)


def dot3(a, b, dims):
    (a_high, a_low), (b_high, b_low) = a, b
    return dot1(a_high, b_high, dims) + dot1(a_high, b_low, dims) + dot1(a_low, b_high, dims)


def line_of(device):
    return (device & 1) * 8 + (device >> 1)


def product_kernel(me_ref, first, second, inputs, out, high, low):
    @pl.when(pl.program_id(0) == 0)
    def _():
        high[...], low[...] = split(inputs[...])

    lines = split(jnp.concatenate([first[...], second[...]], 1))
    out[...] = dot3(lines, (high[...], low[...]), TN).reshape(out.shape)


def product_lines(me, value_matrix, inputs, odd):
    rows, acts = inputs.shape
    return pl.pallas_call(
        product_kernel,
        grid_spec=pltpu.PrefetchScalarGridSpec(
            num_scalar_prefetch=1,
            grid=(4,),
            in_specs=[
                pl.BlockSpec((rows, LINE), lambda i, m: (0, line_of(m[0] ^ (4 * i + odd)))),
                pl.BlockSpec((rows, LINE), lambda i, m: (0, line_of(m[0] ^ (4 * i + 2 + odd)))),
                pl.BlockSpec((rows, acts), lambda i, m: (0, 0)),
            ],
            out_specs=pl.BlockSpec((2, LINE, acts), lambda i, m: (i, 0, 0)),
            scratch_shapes=[pltpu.VMEM((rows, acts), BF16)] * 2,
        ),
        out_shape=jax.ShapeDtypeStruct((8, LINE, acts), F32),
        compiler_params=pltpu.CompilerParams(vmem_limit_bytes=VMEM_LIMIT),
        cost_estimate=pl.CostEstimate(flops=1 << 20, bytes_accessed=1 << 20, transcendentals=0),
    )(me, value_matrix, value_matrix, inputs)


def swap(x, mask):
    return lax.ppermute(x, ("row", "col"), [(i, i ^ mask) for i in range(128)])


CORE, X_LOW, X_HIGH = 8, 16, 1
Y = (0, 32, 64, 96)
Z = (0, 2, 4, 6)
X = (0, 16, 1, 17)


def y_first(near, blocks):
    return swap(jnp.stack([blocks[near], blocks[2]]), Y[near])


def y_second(near, blocks, got):
    far = 4 - near
    kept = blocks[far] + got[1]
    return blocks[0] + got[0] + swap(kept, Y[far])


def scatter_lines(even, odd, begun, first_wait, third_wait):
    got = begun(swap(odd, CORE))
    quarter = LINE // 4
    cut = lambda i, q: even[i, q * quarter : (q + 1) * quarter] + got[i, q * quarter : (q + 1) * quarter]
    half = lambda i, q: jnp.concatenate([cut(i, q), cut(i, q + 1)], 0)
    pair = lambda m, q: jnp.stack([cut(2 * m, q), cut(2 * m + 1, q)])
    came = swap(jnp.stack([half(2 * m + 1, 0) for m in range(4)]), X_LOW)
    c = [pair(m, 2) for m in range(4)]
    d = [pair(m, 3) for m in range(4)]
    c_got, d_got = first_wait(y_first(1, c), y_first(3, d))
    c, d = y_second(1, c, c_got), y_second(3, d, d_got)
    own = [half(2 * m, 0) + came[m] for m in range(4)]
    a = [o[:quarter] for o in own]
    b = [o[quarter:] for o in own]
    a_got, b_got = third_wait(y_first(1, a), y_first(3, b))
    a, b = y_second(1, a, a_got), y_second(3, b, b_got)
    rest = jnp.concatenate([c[0], d[0]], 0) + swap(jnp.concatenate([c[1], d[1]], 0), X_LOW)
    return jnp.concatenate([a, b, rest], 0)


def halves(x, bit):
    count = x.shape[0] // 2
    low, high = x[:count], x[count:]
    return jnp.where(bit, high, low), jnp.where(bit, low, high)


def joined(mine, got, bit):
    return jnp.concatenate([jnp.where(bit, got, mine), jnp.where(bit, mine, got)], 0)


def scatter_four(x, place, masks):
    count = x.shape[0] // 4
    own = lambda m: lax.dynamic_slice_in_dim(x, (place ^ m) * count, count, 0)
    return own(0) + swap(own(1), masks[1]) + swap(own(2), masks[2]) + swap(own(3), masks[3])


def gather_four(x, place, masks):
    parts = jnp.stack([x] + [swap(x, masks[m]) for m in range(1, 4)])
    return jnp.concatenate([lax.dynamic_index_in_dim(parts, place ^ m, 0, False) for m in range(4)], 0)


def tied(*values):
    return lax.optimization_barrier(values)


def sum_cores(x, core):
    keep, send = halves(x, core == 1)
    return keep + swap(send, CORE)


def gather_rows_start(line):
    first, second = line[: LINE // 2], line[LINE // 2 :]
    pair = jnp.stack([first, swap(first, X_HIGH)])
    quad = jnp.stack([second] + [swap(second, Z[m]) for m in range(1, 4)])
    return pair, quad


def gather_rows_end(pair, quad):
    return [pair] + [swap(pair, Z[m]) for m in range(1, 4)] + [quad, swap(quad, X_HIGH)]


def gram_kernel(inputs, product, out):
    a = split(inputs[...])
    b = split(product[...])
    at = 0
    for k in range(4):
        for i in range(k, 4):
            left = [part[:, i * PANEL : (i + 1) * PANEL] for part in a]
            right = [part[:, k * PANEL : (k + 1) * PANEL] for part in b]
            out[at] = dot3(left, right, TN)
            at += 1


def gram_blocks(inputs, product):
    return pl.pallas_call(
        gram_kernel,
        out_shape=jax.ShapeDtypeStruct((10, PANEL, PANEL), F32),
        compiler_params=pltpu.CompilerParams(vmem_limit_bytes=VMEM_LIMIT),
        cost_estimate=pl.CostEstimate(flops=1 << 20, bytes_accessed=1 << 20, transcendentals=0),
    )(inputs, product)


def block_index(i, k):
    return k * 4 - (k * (k - 1)) // 2 + i - k


def series_inverse(a, eye, mask):
    picked = jnp.where(mask, a, 0.0)
    across = lax.rsqrt(jnp.sum(picked, axis=0, keepdims=True))
    down = lax.rsqrt(jnp.sum(picked, axis=1, keepdims=True))
    error = jnp.where(mask, 0.0, -(a * across * down))
    result = eye + error
    for _ in range(3):
        parts = split(error)
        error = dot3(parts, parts, NN)
        result = result + dot3(split(result), split(error), NN)
    short = error.astype(BF16)
    error = dot1(short, short, NN)
    result = result + dot1(result.astype(BF16), error.astype(BF16), NN)
    return result * across * down, jnp.sum(error * error, keepdims=True)


def pivot_inverse(a, work):
    size = a.shape[0]
    work[...] = a
    lanes = lax.broadcasted_iota(jnp.int32, (1, size), 1)
    rows = lax.broadcasted_iota(jnp.int32, (size, 1), 0)

    def step(p, carry):
        now = work[...]
        across = work[pl.ds(p, 1), :]
        down = jnp.sum(jnp.where(lanes == p, now, 0.0), axis=1, keepdims=True)
        inverse = 1.0 / jnp.sum(jnp.where(lanes == p, across, 0.0), axis=1, keepdims=True)
        new = now - down * (across * inverse)
        new = jnp.where(lanes == p, down * inverse, new)
        new = jnp.where(rows == p, across * inverse, new)
        work[...] = jnp.where((rows == p) & (lanes == p), -inverse, new)
        return carry

    lax.fori_loop(0, size, step, 0)
    return -work[...]


def factor_kernel(weight, gram, factor, inverses, work, worst):
    size = PANEL
    mask = lax.broadcasted_iota(jnp.int32, (size, size), 0) == lax.broadcasted_iota(jnp.int32, (size, size), 1)
    eye = jnp.where(mask, 1.0, 0.0).astype(F32)

    def run(robust):
        for k in range(4):
            for i in range(k, 4):
                here = gram[block_index(i, k)]
                factor[block_index(i, k)] = here + weight[0] * eye if i == k else here
        for k in range(4):
            here = factor[block_index(k, k)]
            if robust:
                inverse = pivot_inverse(here, work)
            else:
                inverse, off = series_inverse(here, eye, mask)
                worst[...] = off if k == 0 else jnp.where(off < worst[...], worst[...], off)
            inverses[k] = inverse
            parts = split(inverse)
            columns = [split(factor[block_index(i, k)]) for i in range(k + 1, 4)]
            lefts = []
            for i in range(k + 1, 4):
                left = dot3(columns[i - k - 1], parts, NN)
                factor[block_index(i, k)] = left
                lefts.append(split(left))
            for j in range(k + 1, 4):
                for i in range(j, 4):
                    factor[block_index(i, j)] -= dot3(lefts[i - k - 1], columns[j - k - 1], NT)

    run(False)

    @pl.when(jnp.logical_not(worst[0, 0] < 1e-6))
    def _():
        run(True)


def factored(weight, gram):
    scalar = pl.BlockSpec(memory_space=pltpu.SMEM)
    array = pl.BlockSpec(memory_space=pltpu.VMEM)
    return pl.pallas_call(
        factor_kernel,
        out_shape=[
            jax.ShapeDtypeStruct((10, PANEL, PANEL), F32),
            jax.ShapeDtypeStruct((4, PANEL, PANEL), F32),
        ],
        in_specs=[scalar, array],
        out_specs=[array, array],
        scratch_shapes=[pltpu.VMEM((PANEL, PANEL), F32), pltpu.VMEM((1, 1), F32)],
        compiler_params=pltpu.CompilerParams(vmem_limit_bytes=VMEM_LIMIT),
        cost_estimate=pl.CostEstimate(flops=9 << 30, bytes_accessed=12 << 20, transcendentals=0),
    )(weight, gram)


def solve_kernel(place, factor, inverses, own, near, across, far, quad, other, high, low, out):
    size = PANEL
    half = LINE // 2
    at = lambda k: slice(k * size, (k + 1) * size)

    def put(step, e, second, value):
        line = (place[0] ^ step) * 2 + (place[1] ^ e)
        out[pl.ds(pl.multiple_of(line * LINE + second * half, half), half), :] = value

    for step, pair in enumerate((own, near, across, far)):
        for e in range(2):
            put(step, e, 0, pair[e])
    for e, lines in enumerate((quad, other)):
        for step in range(4):
            put(step, e, 1, lines[step])
    for k in range(4):
        solved = split(out[:, at(k)])
        for i in range(k + 1, 4):
            out[:, at(i)] -= dot3(solved, split(factor[block_index(i, k)]), NT)
    for k in range(3, -1, -1):
        total = dot3(split(out[:, at(k)]), split(inverses[k]), NN)
        for i in range(k + 1, 4):
            total = total - dot3((high[:, at(i)], low[:, at(i)]), split(factor[block_index(i, k)]), NN)
        high[:, at(k)], low[:, at(k)] = split(total)


def solve(place, factors, sides):
    scalar = pl.BlockSpec(memory_space=pltpu.SMEM)
    array = pl.BlockSpec(memory_space=pltpu.VMEM)
    size = 8 * LINE
    return pl.pallas_call(
        solve_kernel,
        out_shape=[jax.ShapeDtypeStruct((size, 4 * PANEL), BF16)] * 2,
        in_specs=[scalar] + [array] * 8,
        out_specs=[array, array],
        scratch_shapes=[pltpu.VMEM((size, 4 * PANEL), F32)],
        compiler_params=pltpu.CompilerParams(vmem_limit_bytes=VMEM_LIMIT),
        cost_estimate=pl.CostEstimate(flops=9 << 30, bytes_accessed=12 << 20, transcendentals=0),
    )(place, *factors, *sides)


def downdate_kernel(high, low, first, second, base, out):
    lines = split(jnp.concatenate([first[0], second[0]], 0))
    out[...] = base[...] - dot3((high[...], low[...]), lines, NT)


def downdate(solved, gain_cols, base):
    rows, acts = solved[0].shape
    whole = pl.BlockSpec((rows, acts), lambda b: (0, 0))
    line = lambda b: (b % 8) * 2 + b // 8
    block = pl.BlockSpec((rows, 2 * LINE), lambda b: (0, b))
    return pl.pallas_call(
        downdate_kernel,
        grid=(8,),
        in_specs=[
            whole,
            whole,
            pl.BlockSpec((1, LINE, acts), lambda b: (line(2 * b), 0, 0)),
            pl.BlockSpec((1, LINE, acts), lambda b: (line(2 * b + 1), 0, 0)),
            block,
        ],
        out_specs=block,
        out_shape=jax.ShapeDtypeStruct(base.shape, F32),
        compiler_params=pltpu.CompilerParams(vmem_limit_bytes=VMEM_LIMIT),
        cost_estimate=pl.CostEstimate(flops=12 << 30, bytes_accessed=28 << 20, transcendentals=0),
    )(*solved, gain_cols, gain_cols, base)


def stencil_first(field, diagonal):
    centre = field[1:-1]
    side_padded = jnp.pad(centre, ((0, 0), (1, 1), (0, 0)))
    neighbours = field[:-2] + field[2:] + side_padded[:, :-2] + side_padded[:, 2:]
    return diagonal[:, :, None] * centre + COUPLING * neighbours


def plant_kernel(start, sizes, place, *refs):
    columns, at = [], 0
    for size in sizes:
        columns.append(refs[at : at + size])
        at += size
    rows_diag, cols_diag, cost = refs[at : at + 3]
    out, window = refs[-2:]
    step = pl.program_id(0)
    b = step + start
    rows = out.shape[0]
    lanes = lax.broadcasted_iota(jnp.int32, (1, LINE), 1)
    inner = lax.broadcasted_iota(jnp.int32, (LINE, 1), 0)
    column = lambda k: jnp.concatenate([ref[...] for ref in columns[k]], 0)

    @pl.when(step == 0)
    def _():
        window[0] = column(0)
        window[1] = column(1)

    here = window[1]
    after = column(2)
    sides = jnp.where(lanes == 0, 0.0, pltpu.roll(here, 1, 1)) + jnp.where(
        lanes == LINE - 1, 0.0, pltpu.roll(here, LINE - 1, 1)
    )
    field = cols_diag[pl.ds(b, 1), :] * here + COUPLING * (window[0] + after + sides)
    window[0] = here
    window[1] = after
    for a in range(rows // LINE):
        line = lambda k: field[(a + k) * LINE : (a + k + 1) * LINE]
        centre = line(1)
        sides = jnp.where(inner == 0, 0.0, pltpu.roll(centre, 1, 0)) + jnp.where(
            inner == LINE - 1, 0.0, pltpu.roll(centre, LINE - 1, 0)
        )
        here = slice(a * LINE, (a + 1) * LINE)
        out[here, :] = rows_diag[here, :] * centre + COUPLING * (line(0) + line(2) + sides)
    mine = place[1] + b - place[0]

    @pl.when((mine >= 0) & (mine < rows // LINE))
    def _():
        here = pl.ds(pl.multiple_of(mine * LINE, LINE), LINE)
        out[here, :] += jnp.where(inner == lanes, cost[pl.ds(mine, 1), :], 0.0)


def plant_part(start, count, place, value, above, below, left, right, rows_diag, cols_diag, cost, before):
    rows, cols = value.shape
    last = cols // LINE - 1
    array = pl.BlockSpec(memory_space=pltpu.VMEM)
    tall = rows + 2 * LINE

    def column(index):
        blocks = (above, value, below)
        return list(blocks), [pl.BlockSpec((x.shape[0], LINE), index) for x in blocks]

    whole = lambda x: ([x], [pl.BlockSpec((tall, LINE), lambda b: (0, 0))])
    columns = [
        whole(left) if start == 0 else column(lambda b: (0, start - 1)),
        column(lambda b: (0, start)),
        whole(right) if start == last else column(lambda b: (0, b + start + 1)),
    ]
    operands, specs = [place], [pl.BlockSpec(memory_space=pltpu.SMEM)]
    for blocks, block_specs in columns:
        operands += blocks
        specs += block_specs
    operands += [rows_diag, cols_diag, cost]
    specs += [array] * 3
    aliases = {}
    if before is not None:
        aliases = {len(operands): 0}
        operands.append(before)
        specs.append(pl.BlockSpec(memory_space=pl.ANY))
    return pl.pallas_call(
        functools.partial(plant_kernel, start, [len(blocks) for blocks, _ in columns]),
        grid=(count,),
        in_specs=specs,
        out_specs=pl.BlockSpec((rows, LINE), lambda b: (0, b + start)),
        out_shape=jax.ShapeDtypeStruct(value.shape, F32),
        scratch_shapes=[pltpu.VMEM((2, tall, LINE), F32)],
        input_output_aliases=aliases,
        compiler_params=pltpu.CompilerParams(vmem_limit_bytes=VMEM_LIMIT),
        cost_estimate=pl.CostEstimate(flops=32 << 20, bytes_accessed=16 << 20, transcendentals=0),
    )(*operands)


def local(value_matrix, inputs, plant_diag, state_cost, control_weight):
    row_index = lax.axis_index("row")
    col_index = lax.axis_index("col")
    both = ("row", "col")
    grid_side = plant_diag.shape[0]
    rows_block, cols_block = value_matrix.shape
    actuators = inputs.shape[1]
    lines_rows = rows_block // grid_side
    lines_cols = cols_block // grid_side
    diag_rows = lax.dynamic_slice_in_dim(plant_diag, row_index * lines_rows, lines_rows, 0)
    diag_cols = lax.dynamic_slice_in_dim(plant_diag, col_index * lines_cols, lines_cols, 0)
    me = row_index.astype(jnp.int32).reshape(1)
    trade = [((a * 2 + core) * 8 + b, (b * 2 + core) * 8 + a) for a in range(8) for b in range(8) for core in range(2)]

    def shifted(x, axis, by):
        count = lax.axis_size(axis)
        return lax.ppermute(x, axis, [(i, i + by) for i in range(count) if 0 <= i + by < count])

    above = shifted(value_matrix[-LINE:], "row", 1)
    below = shifted(value_matrix[:LINE], "row", -1)
    operands = (
        jnp.stack([row_index * lines_rows, col_index * lines_cols]).astype(jnp.int32),
        value_matrix,
        above,
        below,
        None,
        None,
        jnp.broadcast_to(diag_rows.reshape(rows_block, 1), (rows_block, LINE)),
        diag_cols,
        state_cost.reshape(lines_rows, grid_side),
    )
    odd = product_lines(me, value_matrix, inputs, 1)
    even = product_lines(me, value_matrix, inputs, 0)
    held = {}

    def begun(got):
        got, held["above"], held["below"] = tied(got, above, below)
        return got

    def first_wait(c_got, d_got):
        middle = (*operands[:2], held["above"], held["below"], *operands[4:])
        base = plant_part(1, 7, *middle, None)
        base = plant_part(8, 7, *middle, base)
        c_got, d_got, held["base"], above, below = tied(c_got, d_got, base, held["above"], held["below"])
        tall = lambda cols: jnp.concatenate([above[:, cols], value_matrix[:, cols], below[:, cols]], 0)
        held["left"] = shifted(tall(slice(-LINE, None)), "col", 1)
        held["right"] = shifted(tall(slice(None, LINE)), "col", -1)
        return c_got, d_got

    def third_wait(a_got, b_got):
        a_got, b_got, held["left"], held["right"] = tied(a_got, b_got, held["left"], held["right"])
        return a_got, b_got

    product = scatter_lines(even, odd, begun, first_wait, third_wait)
    operands = (*operands[:2], held["above"], held["below"], held["left"], held["right"], *operands[6:])

    core, x_low, y = row_index & 1, (row_index >> 1) & 1, row_index >> 2
    x_high, z = col_index & 1, col_index >> 1
    x_place = x_high * 2 + x_low

    product = lax.ppermute(product, both, trade)
    count = grid_side
    over = lax.ppermute(product, both, [(i, i + 1) for i in range(count - 1)])
    under = lax.ppermute(product, both, [(i + 1, i) for i in range(count - 1)])
    mine_inputs = lax.dynamic_slice_in_dim(inputs, col_index * LINE, LINE, 0)
    gram = gram_blocks(mine_inputs, product)
    total = sum_cores(gram.reshape(10 * PANEL, PANEL), core)
    total = scatter_four(total, z, Z)
    over, under, total = tied(over, under, total)
    diagonal = lax.dynamic_slice_in_dim(plant_diag, row_index * 8 + col_index, 1, 0)
    gain = stencil_first(jnp.stack([over, product, under]), diagonal)[0]
    gain, total = tied(gain, total)

    back = lax.ppermute(gain, both, trade)
    total = scatter_four(total, x_place, X)
    total = total + swap(total, Y[1]) + swap(total, Y[2]) + swap(total, Y[3])
    back, gain, total = tied(back, gain, total)

    gain_cols = lax.all_gather(back, "row", axis=0)
    pair, quad = gather_rows_start(gain)
    total = gather_four(gather_four(total, x_place, X), z, Z)
    pair, quad, total = tied(pair, quad, total)
    sides = gather_rows_end(pair, quad)
    total = joined(total, swap(total, CORE), core == 1)
    factors = factored(control_weight, total.reshape(10, PANEL, PANEL))
    *factors, base = tied(*factors, held["base"])
    base = plant_part(0, 1, *operands, base)
    base = plant_part(lines_cols - 1, 1, *operands, base)
    *sides, base = tied(*sides, base)
    solved = solve(jnp.stack([z, x_high]).astype(jnp.int32), factors, sides)
    return downdate(solved, gain_cols, base)


def solution(mesh):
    in_specs = (P("row", "col"), P("row", None), P(), P("row"), P())
    out_specs = P("row", "col")
    return jax.shard_map(local, mesh=mesh, in_specs=in_specs, out_specs=out_specs, check_vma=False)
```

```python
import functools

import jax
import jax.numpy as jnp
from jax import lax
from jax.experimental import pallas as pl
from jax.experimental.pallas import tpu as pltpu
from jax.sharding import PartitionSpec as P

COUPLING = 0.25
F32 = jnp.float32
BF16 = jnp.bfloat16
NN = (((1,), (0,)), ((), ()))
NT = (((1,), (1,)), ((), ()))
TN = (((0,), (0,)), ((), ()))
LINE = 128
PANEL = 256
VMEM_LIMIT = 56 << 20


def split(x):
    high = x.astype(BF16)
    return high, (x - high.astype(F32)).astype(BF16)


def dot1(a, b, dims):
    return lax.dot_general(a, b, dims, preferred_element_type=F32)


def dot3(a, b, dims):
    (a_high, a_low), (b_high, b_low) = a, b
    return dot1(a_high, b_high, dims) + dot1(a_high, b_low, dims) + dot1(a_low, b_high, dims)


def line_of(device):
    return (device & 1) * 8 + (device >> 1)


def product_kernel(me_ref, first, second, inputs, out, high, low):
    @pl.when(pl.program_id(0) == 0)
    def _():
        high[...], low[...] = split(inputs[...])

    lines = split(jnp.concatenate([first[...], second[...]], 1))
    out[...] = dot3(lines, (high[...], low[...]), TN).reshape(out.shape)


def product_lines(me, value_matrix, inputs, odd):
    rows, acts = inputs.shape
    return pl.pallas_call(
        product_kernel,
        grid_spec=pltpu.PrefetchScalarGridSpec(
            num_scalar_prefetch=1,
            grid=(4,),
            in_specs=[
                pl.BlockSpec((rows, LINE), lambda i, m: (0, line_of(m[0] ^ (4 * i + odd)))),
                pl.BlockSpec((rows, LINE), lambda i, m: (0, line_of(m[0] ^ (4 * i + 2 + odd)))),
                pl.BlockSpec((rows, acts), lambda i, m: (0, 0)),
            ],
            out_specs=pl.BlockSpec((2, LINE, acts), lambda i, m: (i, 0, 0)),
            scratch_shapes=[pltpu.VMEM((rows, acts), BF16)] * 2,
        ),
        out_shape=jax.ShapeDtypeStruct((8, LINE, acts), F32),
        compiler_params=pltpu.CompilerParams(vmem_limit_bytes=VMEM_LIMIT),
        cost_estimate=pl.CostEstimate(flops=1 << 20, bytes_accessed=1 << 20, transcendentals=0),
    )(me, value_matrix, value_matrix, inputs)


def swap(x, mask):
    return lax.ppermute(x, ("row", "col"), [(i, i ^ mask) for i in range(128)])


CORE, X_LOW, X_HIGH = 8, 16, 1
Y = (0, 32, 64, 96)
Z = (0, 2, 4, 6)
X = (0, 16, 1, 17)


def y_first(near, blocks):
    return swap(jnp.stack([blocks[near], blocks[2]]), Y[near])


def y_second(near, blocks, got):
    far = 4 - near
    kept = blocks[far] + got[1]
    return blocks[0] + got[0] + swap(kept, Y[far])


def scatter_lines(even, odd):
    got = swap(odd, CORE)
    quarter = LINE // 4
    cut = lambda i, q: even[i, q * quarter : (q + 1) * quarter] + got[i, q * quarter : (q + 1) * quarter]
    half = lambda i, q: jnp.concatenate([cut(i, q), cut(i, q + 1)], 0)
    pair = lambda m, q: jnp.stack([cut(2 * m, q), cut(2 * m + 1, q)])
    came = swap(jnp.stack([half(2 * m + 1, 0) for m in range(4)]), X_LOW)
    c = [pair(m, 2) for m in range(4)]
    d = [pair(m, 3) for m in range(4)]
    c, d = y_second(1, c, y_first(1, c)), y_second(3, d, y_first(3, d))
    own = [half(2 * m, 0) + came[m] for m in range(4)]
    a = [o[:quarter] for o in own]
    b = [o[quarter:] for o in own]
    a, b = y_second(1, a, y_first(1, a)), y_second(3, b, y_first(3, b))
    rest = jnp.concatenate([c[0], d[0]], 0) + swap(jnp.concatenate([c[1], d[1]], 0), X_LOW)
    return jnp.concatenate([a, b, rest], 0)


def halves(x, bit):
    count = x.shape[0] // 2
    low, high = x[:count], x[count:]
    return jnp.where(bit, high, low), jnp.where(bit, low, high)


def joined(mine, got, bit):
    return jnp.concatenate([jnp.where(bit, got, mine), jnp.where(bit, mine, got)], 0)


def scatter_four(x, place, masks):
    count = x.shape[0] // 4
    own = lambda m: lax.dynamic_slice_in_dim(x, (place ^ m) * count, count, 0)
    return own(0) + swap(own(1), masks[1]) + swap(own(2), masks[2]) + swap(own(3), masks[3])


def gather_four(x, place, masks):
    parts = jnp.stack([x] + [swap(x, masks[m]) for m in range(1, 4)])
    return jnp.concatenate([lax.dynamic_index_in_dim(parts, place ^ m, 0, False) for m in range(4)], 0)


def tied(*values):
    return lax.optimization_barrier(values)


def sum_cores(x, core):
    keep, send = halves(x, core == 1)
    return keep + swap(send, CORE)


def gram_kernel(inputs, product, out):
    a = split(inputs[...])
    b = split(product[...])
    at = 0
    for k in range(4):
        for i in range(k, 4):
            left = [part[:, i * PANEL : (i + 1) * PANEL] for part in a]
            right = [part[:, k * PANEL : (k + 1) * PANEL] for part in b]
            out[at] = dot3(left, right, TN)
            at += 1


def gram_blocks(inputs, product):
    return pl.pallas_call(
        gram_kernel,
        out_shape=jax.ShapeDtypeStruct((10, PANEL, PANEL), F32),
        compiler_params=pltpu.CompilerParams(vmem_limit_bytes=VMEM_LIMIT),
        cost_estimate=pl.CostEstimate(flops=1 << 20, bytes_accessed=1 << 20, transcendentals=0),
    )(inputs, product)


def block_index(i, k):
    return k * 4 - (k * (k - 1)) // 2 + i - k


def series_inverse(a, eye, mask):
    picked = jnp.where(mask, a, 0.0)
    across = lax.rsqrt(jnp.sum(picked, axis=0, keepdims=True))
    down = lax.rsqrt(jnp.sum(picked, axis=1, keepdims=True))
    error = jnp.where(mask, 0.0, -(a * across * down))
    result = eye + error
    for _ in range(3):
        parts = split(error)
        error = dot3(parts, parts, NN)
        result = result + dot3(split(result), split(error), NN)
    short = error.astype(BF16)
    error = dot1(short, short, NN)
    result = result + dot1(result.astype(BF16), error.astype(BF16), NN)
    return result * across * down, jnp.sum(error * error, keepdims=True)


def pivot_inverse(a, work):
    size = a.shape[0]
    work[...] = a
    lanes = lax.broadcasted_iota(jnp.int32, (1, size), 1)
    rows = lax.broadcasted_iota(jnp.int32, (size, 1), 0)

    def step(p, carry):
        now = work[...]
        across = work[pl.ds(p, 1), :]
        down = jnp.sum(jnp.where(lanes == p, now, 0.0), axis=1, keepdims=True)
        inverse = 1.0 / jnp.sum(jnp.where(lanes == p, across, 0.0), axis=1, keepdims=True)
        new = now - down * (across * inverse)
        new = jnp.where(lanes == p, down * inverse, new)
        new = jnp.where(rows == p, across * inverse, new)
        work[...] = jnp.where((rows == p) & (lanes == p), -inverse, new)
        return carry

    lax.fori_loop(0, size, step, 0)
    return -work[...]


def factor_kernel(weight, gram, factor, inverses, work, worst):
    size = PANEL
    mask = lax.broadcasted_iota(jnp.int32, (size, size), 0) == lax.broadcasted_iota(jnp.int32, (size, size), 1)
    eye = jnp.where(mask, 1.0, 0.0).astype(F32)

    def run(robust):
        for k in range(4):
            for i in range(k, 4):
                here = gram[block_index(i, k)]
                factor[block_index(i, k)] = here + weight[0] * eye if i == k else here
        for k in range(4):
            here = factor[block_index(k, k)]
            if robust:
                inverse = pivot_inverse(here, work)
            else:
                inverse, off = series_inverse(here, eye, mask)
                worst[...] = off if k == 0 else jnp.where(off < worst[...], worst[...], off)
            inverses[k] = inverse
            parts = split(inverse)
            columns = [split(factor[block_index(i, k)]) for i in range(k + 1, 4)]
            lefts = []
            for i in range(k + 1, 4):
                left = dot3(columns[i - k - 1], parts, NN)
                factor[block_index(i, k)] = left
                lefts.append(split(left))
            for j in range(k + 1, 4):
                for i in range(j, 4):
                    factor[block_index(i, j)] -= dot3(lefts[i - k - 1], columns[j - k - 1], NT)

    run(False)

    @pl.when(jnp.logical_not(worst[0, 0] < 1e-6))
    def _():
        run(True)


def factored(weight, gram):
    scalar = pl.BlockSpec(memory_space=pltpu.SMEM)
    array = pl.BlockSpec(memory_space=pltpu.VMEM)
    return pl.pallas_call(
        factor_kernel,
        out_shape=[
            jax.ShapeDtypeStruct((10, PANEL, PANEL), F32),
            jax.ShapeDtypeStruct((4, PANEL, PANEL), F32),
        ],
        in_specs=[scalar, array],
        out_specs=[array, array],
        scratch_shapes=[pltpu.VMEM((PANEL, PANEL), F32), pltpu.VMEM((1, 1), F32)],
        compiler_params=pltpu.CompilerParams(vmem_limit_bytes=VMEM_LIMIT),
        cost_estimate=pl.CostEstimate(flops=9 << 30, bytes_accessed=12 << 20, transcendentals=0),
    )(weight, gram)


def solve_kernel(z, factor, inverses, first, first_near, first_far, second, second_near, second_far, high, low, out):
    size = PANEL
    at = lambda k: slice(k * size, (k + 1) * size)

    def put(step, x_high, value):
        line = (z[0] ^ step) * 2 + x_high
        out[pl.ds(pl.multiple_of(line * LINE, LINE), LINE), :] = value

    put(0, 0, first[...])
    put(1, 0, first_near[...])
    put(3, 0, first_far[0])
    put(2, 0, first_far[1])
    put(0, 1, second[...])
    put(3, 1, second_near[...])
    put(1, 1, second_far[0])
    put(2, 1, second_far[1])
    for k in range(4):
        solved = split(out[:, at(k)])
        for i in range(k + 1, 4):
            out[:, at(i)] -= dot3(solved, split(factor[block_index(i, k)]), NT)
    for k in range(3, -1, -1):
        total = dot3(split(out[:, at(k)]), split(inverses[k]), NN)
        for i in range(k + 1, 4):
            total = total - dot3((high[:, at(i)], low[:, at(i)]), split(factor[block_index(i, k)]), NN)
        high[:, at(k)], low[:, at(k)] = split(total)


def solve(z, factors, sides):
    scalar = pl.BlockSpec(memory_space=pltpu.SMEM)
    array = pl.BlockSpec(memory_space=pltpu.VMEM)
    size = 8 * LINE
    return pl.pallas_call(
        solve_kernel,
        out_shape=[jax.ShapeDtypeStruct((size, 4 * PANEL), BF16)] * 2,
        in_specs=[scalar] + [array] * 8,
        out_specs=[array, array],
        scratch_shapes=[pltpu.VMEM((size, 4 * PANEL), F32)],
        compiler_params=pltpu.CompilerParams(vmem_limit_bytes=VMEM_LIMIT),
        cost_estimate=pl.CostEstimate(flops=9 << 30, bytes_accessed=12 << 20, transcendentals=0),
    )(z, *factors, *sides)


def downdate_kernel(high, low, first, second, base, out):
    lines = split(jnp.concatenate([first[0], second[0]], 0))
    out[...] = base[...] - dot3((high[...], low[...]), lines, NT)


def downdate(solved, gain_cols, base):
    rows, acts = solved[0].shape
    whole = pl.BlockSpec((rows, acts), lambda b: (0, 0))
    line = lambda b: (b % 8) * 2 + b // 8
    block = pl.BlockSpec((rows, 2 * LINE), lambda b: (0, b))
    return pl.pallas_call(
        downdate_kernel,
        grid=(8,),
        in_specs=[
            whole,
            whole,
            pl.BlockSpec((1, LINE, acts), lambda b: (line(2 * b), 0, 0)),
            pl.BlockSpec((1, LINE, acts), lambda b: (line(2 * b + 1), 0, 0)),
            block,
        ],
        out_specs=block,
        out_shape=jax.ShapeDtypeStruct(base.shape, F32),
        compiler_params=pltpu.CompilerParams(vmem_limit_bytes=VMEM_LIMIT),
        cost_estimate=pl.CostEstimate(flops=12 << 30, bytes_accessed=28 << 20, transcendentals=0),
    )(*solved, gain_cols, gain_cols, base)


def stencil_first(field, diagonal):
    centre = field[1:-1]
    side_padded = jnp.pad(centre, ((0, 0), (1, 1), (0, 0)))
    neighbours = field[:-2] + field[2:] + side_padded[:, :-2] + side_padded[:, 2:]
    return diagonal[:, :, None] * centre + COUPLING * neighbours


def plant_kernel(start, sizes, place, *refs):
    columns, at = [], 0
    for size in sizes:
        columns.append(refs[at : at + size])
        at += size
    rows_diag, cols_diag, cost = refs[at : at + 3]
    out, window = refs[-2:]
    step = pl.program_id(0)
    b = step + start
    rows = out.shape[0]
    lanes = lax.broadcasted_iota(jnp.int32, (1, LINE), 1)
    inner = lax.broadcasted_iota(jnp.int32, (LINE, 1), 0)
    column = lambda k: jnp.concatenate([ref[...] for ref in columns[k]], 0)

    @pl.when(step == 0)
    def _():
        window[0] = column(0)
        window[1] = column(1)

    here = window[1]
    after = column(2)
    sides = jnp.where(lanes == 0, 0.0, pltpu.roll(here, 1, 1)) + jnp.where(
        lanes == LINE - 1, 0.0, pltpu.roll(here, LINE - 1, 1)
    )
    field = cols_diag[pl.ds(b, 1), :] * here + COUPLING * (window[0] + after + sides)
    window[0] = here
    window[1] = after
    for a in range(rows // LINE):
        line = lambda k: field[(a + k) * LINE : (a + k + 1) * LINE]
        centre = line(1)
        sides = jnp.where(inner == 0, 0.0, pltpu.roll(centre, 1, 0)) + jnp.where(
            inner == LINE - 1, 0.0, pltpu.roll(centre, LINE - 1, 0)
        )
        here = slice(a * LINE, (a + 1) * LINE)
        out[here, :] = rows_diag[here, :] * centre + COUPLING * (line(0) + line(2) + sides)
    mine = place[1] + b - place[0]

    @pl.when((mine >= 0) & (mine < rows // LINE))
    def _():
        here = pl.ds(pl.multiple_of(mine * LINE, LINE), LINE)
        out[here, :] += jnp.where(inner == lanes, cost[pl.ds(mine, 1), :], 0.0)


def plant_part(start, count, place, value, above, below, left, right, rows_diag, cols_diag, cost, before):
    rows, cols = value.shape
    last = cols // LINE - 1
    array = pl.BlockSpec(memory_space=pltpu.VMEM)
    tall = rows + 2 * LINE

    def column(index):
        blocks = (above, value, below)
        return list(blocks), [pl.BlockSpec((x.shape[0], LINE), index) for x in blocks]

    whole = lambda x: ([x], [pl.BlockSpec((tall, LINE), lambda b: (0, 0))])
    columns = [
        whole(left) if start == 0 else column(lambda b: (0, start - 1)),
        column(lambda b: (0, start)),
        whole(right) if start == last else column(lambda b: (0, b + start + 1)),
    ]
    operands, specs = [place], [pl.BlockSpec(memory_space=pltpu.SMEM)]
    for blocks, block_specs in columns:
        operands += blocks
        specs += block_specs
    operands += [rows_diag, cols_diag, cost]
    specs += [array] * 3
    aliases = {}
    if before is not None:
        aliases = {len(operands): 0}
        operands.append(before)
        specs.append(pl.BlockSpec(memory_space=pl.ANY))
    return pl.pallas_call(
        functools.partial(plant_kernel, start, [len(blocks) for blocks, _ in columns]),
        grid=(count,),
        in_specs=specs,
        out_specs=pl.BlockSpec((rows, LINE), lambda b: (0, b + start)),
        out_shape=jax.ShapeDtypeStruct(value.shape, F32),
        scratch_shapes=[pltpu.VMEM((2, tall, LINE), F32)],
        input_output_aliases=aliases,
        compiler_params=pltpu.CompilerParams(vmem_limit_bytes=VMEM_LIMIT),
        cost_estimate=pl.CostEstimate(flops=32 << 20, bytes_accessed=16 << 20, transcendentals=0),
    )(*operands)


def local(value_matrix, inputs, plant_diag, state_cost, control_weight):
    row_index = lax.axis_index("row")
    col_index = lax.axis_index("col")
    both = ("row", "col")
    grid_side = plant_diag.shape[0]
    rows_block, cols_block = value_matrix.shape
    actuators = inputs.shape[1]
    lines_rows = rows_block // grid_side
    lines_cols = cols_block // grid_side
    diag_rows = lax.dynamic_slice_in_dim(plant_diag, row_index * lines_rows, lines_rows, 0)
    diag_cols = lax.dynamic_slice_in_dim(plant_diag, col_index * lines_cols, lines_cols, 0)
    me = row_index.astype(jnp.int32).reshape(1)
    trade = [((a * 2 + core) * 8 + b, (b * 2 + core) * 8 + a) for a in range(8) for b in range(8) for core in range(2)]

    def shifted(x, axis, by):
        count = lax.axis_size(axis)
        return lax.ppermute(x, axis, [(i, i + by) for i in range(count) if 0 <= i + by < count])

    above = shifted(value_matrix[-LINE:], "row", 1)
    below = shifted(value_matrix[:LINE], "row", -1)
    operands = (
        jnp.stack([row_index * lines_rows, col_index * lines_cols]).astype(jnp.int32),
        value_matrix,
        jnp.broadcast_to(diag_rows.reshape(rows_block, 1), (rows_block, LINE)),
        diag_cols,
        state_cost.reshape(lines_rows, grid_side),
    )
    odd = product_lines(me, value_matrix, inputs, 1)
    even = product_lines(me, value_matrix, inputs, 0)
    tall = lambda cols: jnp.concatenate([above[:, cols], value_matrix[:, cols], below[:, cols]], 0)
    left = shifted(tall(slice(-LINE, None)), "col", 1)
    right = shifted(tall(slice(None, LINE)), "col", -1)
    product = scatter_lines(even, odd)

    core, x_low, y = row_index & 1, (row_index >> 1) & 1, row_index >> 2
    x_high, z = col_index & 1, col_index >> 1
    x_place = x_high * 2 + x_low

    product, above, below, left, right = tied(product, above, below, left, right)
    product = lax.ppermute(product, both, trade)
    around = (*operands[:2], above, below, left, right, *operands[2:])
    base = None
    for start, count in ((1, 7), (8, 7), (0, 1), (lines_cols - 1, 1)):
        base = plant_part(start, count, *around, base)
    product, base = tied(product, base)

    count = grid_side
    over = lax.ppermute(product, both, [(i, i + 1) for i in range(count - 1)])
    under = lax.ppermute(product, both, [(i + 1, i) for i in range(count - 1)])
    mine_inputs = lax.dynamic_slice_in_dim(inputs, col_index * LINE, LINE, 0)
    gram = gram_blocks(mine_inputs, product)
    total = sum_cores(gram.reshape(10 * PANEL, PANEL), core)
    over, under, total = tied(over, under, total)
    diagonal = lax.dynamic_slice_in_dim(plant_diag, row_index * 8 + col_index, 1, 0)
    gain = stencil_first(jnp.stack([over, product, under]), diagonal)[0]
    gain, total = tied(gain, total)

    pair = joined(gain, swap(gain, X_HIGH), x_high == 1)
    total = scatter_four(total, z, Z)
    pair, total = tied(pair, total)

    back = lax.ppermute(gain, both, trade)
    first, second = pair[:LINE], pair[LINE:]
    first_near, second_near = swap(first, Z[1]), swap(second, Z[3])
    total = scatter_four(total, x_place, X)
    first_near, second_near, total = tied(first_near, second_near, total)

    first_far = swap(jnp.stack([first, first_near]), Z[3])
    second_far = swap(jnp.stack([second, second_near]), Z[1])
    total = total + swap(total, Y[1]) + swap(total, Y[2]) + swap(total, Y[3])
    back, total = tied(back, total)
    gain_cols = lax.all_gather(back, "row", axis=0)
    total = gather_four(total, x_place, X)
    first_far, second_far, total = tied(first_far, second_far, total)
    total = gather_four(total, z, Z)
    total = joined(total, swap(total, CORE), core == 1)

    factors = factored(control_weight, total.reshape(10, PANEL, PANEL))
    sides = (first, first_near, first_far, second, second_near, second_far)
    solved = solve(z.astype(jnp.int32).reshape(1), factors, sides)
    return downdate(solved, gain_cols, base)


def solution(mesh):
    in_specs = (P("row", "col"), P("row", None), P(), P("row"), P())
    out_specs = P("row", "col")
    return jax.shard_map(local, mesh=mesh, in_specs=in_specs, out_specs=out_specs, check_vma=False)
```

```python
import functools

import jax
import jax.numpy as jnp
from jax import lax
from jax.experimental import pallas as pl
from jax.experimental.pallas import tpu as pltpu
from jax.sharding import PartitionSpec as P

COUPLING = 0.25
F32 = jnp.float32
BF16 = jnp.bfloat16
NN = (((1,), (0,)), ((), ()))
NT = (((1,), (1,)), ((), ()))
TN = (((0,), (0,)), ((), ()))
LINE = 128
PANEL = 256
VMEM_LIMIT = 56 << 20


def split(x):
    high = x.astype(BF16)
    return high, (x - high.astype(F32)).astype(BF16)


def dot1(a, b, dims):
    return lax.dot_general(a, b, dims, preferred_element_type=F32)


def dot3(a, b, dims):
    (a_high, a_low), (b_high, b_low) = a, b
    return dot1(a_high, b_high, dims) + dot1(a_high, b_low, dims) + dot1(a_low, b_high, dims)


def product_kernel(me_ref, first, second, inputs, out, high, low):
    @pl.when(pl.program_id(0) == 0)
    def _():
        high[...], low[...] = split(inputs[...])

    lines = split(jnp.concatenate([first[...], second[...]], 1))
    out[...] = dot3(lines, (high[...], low[...]), TN).reshape(out.shape)


def product_lines(me, value_matrix, inputs, odd):
    rows, acts = inputs.shape
    return pl.pallas_call(
        product_kernel,
        grid_spec=pltpu.PrefetchScalarGridSpec(
            num_scalar_prefetch=1,
            grid=(4,),
            in_specs=[
                pl.BlockSpec((rows, LINE), lambda i, m: (0, m[0] ^ (4 * i + odd))),
                pl.BlockSpec((rows, LINE), lambda i, m: (0, m[0] ^ (4 * i + 2 + odd))),
                pl.BlockSpec((rows, acts), lambda i, m: (0, 0)),
            ],
            out_specs=pl.BlockSpec((2, LINE, acts), lambda i, m: (i, 0, 0)),
            scratch_shapes=[pltpu.VMEM((rows, acts), BF16)] * 2,
        ),
        out_shape=jax.ShapeDtypeStruct((8, LINE, acts), F32),
        compiler_params=pltpu.CompilerParams(vmem_limit_bytes=VMEM_LIMIT),
        cost_estimate=pl.CostEstimate(flops=1 << 20, bytes_accessed=1 << 20, transcendentals=0),
    )(me, value_matrix, value_matrix, inputs)


def swap(x, mask):
    return lax.ppermute(x, ("row", "col"), [(i, i ^ mask) for i in range(128)])


CORE, X_LOW, X_HIGH = 8, 16, 1
Y = (0, 32, 64, 96)
Z = (0, 2, 4, 6)
X = (0, 16, 1, 17)


def y_first(near, blocks):
    return swap(jnp.stack([blocks[near], blocks[2]]), Y[near])


def y_second(near, blocks, got):
    far = 4 - near
    kept = blocks[far] + got[1]
    return blocks[0] + got[0] + swap(kept, Y[far])


def scatter_lines(even, odd, wait):
    got = swap(odd, CORE)
    quarter = LINE // 4
    cut = lambda i, q: even[i, q * quarter : (q + 1) * quarter] + got[i, q * quarter : (q + 1) * quarter]
    half = lambda i, q: jnp.concatenate([cut(i, q), cut(i, q + 1)], 0)
    pair = lambda m, q: jnp.stack([cut(2 * m, q), cut(2 * m + 1, q)])
    came = swap(jnp.stack([half(2 * m + 1, 0) for m in range(4)]), X_LOW)
    c = [pair(m, 2) for m in range(4)]
    d = [pair(m, 3) for m in range(4)]
    c, d = y_second(1, c, y_first(1, c)), y_second(3, d, y_first(3, d))
    came = wait(came)
    own = [half(2 * m, 0) + came[m] for m in range(4)]
    a = [o[:quarter] for o in own]
    b = [o[quarter:] for o in own]
    a, b = y_second(1, a, y_first(1, a)), y_second(3, b, y_first(3, b))
    rest = jnp.concatenate([c[0], d[0]], 0) + swap(jnp.concatenate([c[1], d[1]], 0), X_LOW)
    return jnp.concatenate([a, b, rest], 0)


def halves(x, bit):
    count = x.shape[0] // 2
    low, high = x[:count], x[count:]
    return jnp.where(bit, high, low), jnp.where(bit, low, high)


def joined(mine, got, bit):
    return jnp.concatenate([jnp.where(bit, got, mine), jnp.where(bit, mine, got)], 0)


def scatter_four(x, place, masks):
    count = x.shape[0] // 4
    own = lambda m: lax.dynamic_slice_in_dim(x, (place ^ m) * count, count, 0)
    return own(0) + swap(own(1), masks[1]) + swap(own(2), masks[2]) + swap(own(3), masks[3])


def gather_four(x, place, masks):
    parts = jnp.stack([x] + [swap(x, masks[m]) for m in range(1, 4)])
    return jnp.concatenate([lax.dynamic_index_in_dim(parts, place ^ m, 0, False) for m in range(4)], 0)


def tied(*values):
    return lax.optimization_barrier(values)


def sum_cores(x, core):
    keep, send = halves(x, core == 1)
    return keep + swap(send, CORE)


def gram_kernel(inputs, product, out):
    a = split(inputs[...])
    b = split(product[...])
    at = 0
    for k in range(4):
        for i in range(k, 4):
            left = [part[:, i * PANEL : (i + 1) * PANEL] for part in a]
            right = [part[:, k * PANEL : (k + 1) * PANEL] for part in b]
            out[at] = dot3(left, right, TN)
            at += 1


def gram_blocks(inputs, product):
    return pl.pallas_call(
        gram_kernel,
        out_shape=jax.ShapeDtypeStruct((10, PANEL, PANEL), F32),
        compiler_params=pltpu.CompilerParams(vmem_limit_bytes=VMEM_LIMIT),
        cost_estimate=pl.CostEstimate(flops=1 << 20, bytes_accessed=1 << 20, transcendentals=0),
    )(inputs, product)


def block_index(i, k):
    return k * 4 - (k * (k - 1)) // 2 + i - k


def series_inverse(a, eye, mask):
    picked = jnp.where(mask, a, 0.0)
    across = lax.rsqrt(jnp.sum(picked, axis=0, keepdims=True))
    down = lax.rsqrt(jnp.sum(picked, axis=1, keepdims=True))
    error = jnp.where(mask, 0.0, -(a * across * down))
    result = eye + error
    for _ in range(3):
        parts = split(error)
        error = dot3(parts, parts, NN)
        result = result + dot3(split(result), split(error), NN)
    short = error.astype(BF16)
    error = dot1(short, short, NN)
    result = result + dot1(result.astype(BF16), error.astype(BF16), NN)
    return result * across * down, jnp.sum(error * error, keepdims=True)


def pivot_inverse(a, work):
    size = a.shape[0]
    work[...] = a
    lanes = lax.broadcasted_iota(jnp.int32, (1, size), 1)
    rows = lax.broadcasted_iota(jnp.int32, (size, 1), 0)

    def step(p, carry):
        now = work[...]
        across = work[pl.ds(p, 1), :]
        down = jnp.sum(jnp.where(lanes == p, now, 0.0), axis=1, keepdims=True)
        inverse = 1.0 / jnp.sum(jnp.where(lanes == p, across, 0.0), axis=1, keepdims=True)
        new = now - down * (across * inverse)
        new = jnp.where(lanes == p, down * inverse, new)
        new = jnp.where(rows == p, across * inverse, new)
        work[...] = jnp.where((rows == p) & (lanes == p), -inverse, new)
        return carry

    lax.fori_loop(0, size, step, 0)
    return -work[...]


def factor_kernel(weight, gram, factor, inverses, work, worst):
    size = PANEL
    mask = lax.broadcasted_iota(jnp.int32, (size, size), 0) == lax.broadcasted_iota(jnp.int32, (size, size), 1)
    eye = jnp.where(mask, 1.0, 0.0).astype(F32)

    def run(robust):
        for k in range(4):
            for i in range(k, 4):
                here = gram[block_index(i, k)]
                factor[block_index(i, k)] = here + weight[0] * eye if i == k else here
        for k in range(4):
            here = factor[block_index(k, k)]
            if robust:
                inverse = pivot_inverse(here, work)
            else:
                inverse, off = series_inverse(here, eye, mask)
                worst[...] = off if k == 0 else jnp.where(off < worst[...], worst[...], off)
            inverses[k] = inverse
            parts = split(inverse)
            columns = [split(factor[block_index(i, k)]) for i in range(k + 1, 4)]
            lefts = []
            for i in range(k + 1, 4):
                left = dot3(columns[i - k - 1], parts, NN)
                factor[block_index(i, k)] = left
                lefts.append(split(left))
            for j in range(k + 1, 4):
                for i in range(j, 4):
                    factor[block_index(i, j)] -= dot3(lefts[i - k - 1], columns[j - k - 1], NT)

    run(False)

    @pl.when(jnp.logical_not(worst[0, 0] < 1e-6))
    def _():
        run(True)


def factored(weight, gram):
    scalar = pl.BlockSpec(memory_space=pltpu.SMEM)
    array = pl.BlockSpec(memory_space=pltpu.VMEM)
    return pl.pallas_call(
        factor_kernel,
        out_shape=[
            jax.ShapeDtypeStruct((10, PANEL, PANEL), F32),
            jax.ShapeDtypeStruct((4, PANEL, PANEL), F32),
        ],
        in_specs=[scalar, array],
        out_specs=[array, array],
        scratch_shapes=[pltpu.VMEM((PANEL, PANEL), F32), pltpu.VMEM((1, 1), F32)],
        compiler_params=pltpu.CompilerParams(vmem_limit_bytes=VMEM_LIMIT),
        cost_estimate=pl.CostEstimate(flops=9 << 30, bytes_accessed=12 << 20, transcendentals=0),
    )(weight, gram)


def solve_kernel(z, factor, inverses, first, first_near, first_far, second, second_near, second_far, high, low, out):
    size = PANEL
    at = lambda k: slice(k * size, (k + 1) * size)

    def put(step, x_high, value):
        line = (z[0] ^ step) * 2 + x_high
        out[pl.ds(pl.multiple_of(line * LINE, LINE), LINE), :] = value

    put(0, 0, first[...])
    put(1, 0, first_near[...])
    put(3, 0, first_far[0])
    put(2, 0, first_far[1])
    put(0, 1, second[...])
    put(3, 1, second_near[...])
    put(1, 1, second_far[0])
    put(2, 1, second_far[1])
    for k in range(4):
        solved = split(out[:, at(k)])
        for i in range(k + 1, 4):
            out[:, at(i)] -= dot3(solved, split(factor[block_index(i, k)]), NT)
    for k in range(3, -1, -1):
        total = dot3(split(out[:, at(k)]), split(inverses[k]), NN)
        for i in range(k + 1, 4):
            total = total - dot3((high[:, at(i)], low[:, at(i)]), split(factor[block_index(i, k)]), NN)
        high[:, at(k)], low[:, at(k)] = split(total)


def solve(z, factors, sides):
    scalar = pl.BlockSpec(memory_space=pltpu.SMEM)
    array = pl.BlockSpec(memory_space=pltpu.VMEM)
    size = 8 * LINE
    return pl.pallas_call(
        solve_kernel,
        out_shape=[jax.ShapeDtypeStruct((size, 4 * PANEL), BF16)] * 2,
        in_specs=[scalar] + [array] * 8,
        out_specs=[array, array],
        scratch_shapes=[pltpu.VMEM((size, 4 * PANEL), F32)],
        compiler_params=pltpu.CompilerParams(vmem_limit_bytes=VMEM_LIMIT),
        cost_estimate=pl.CostEstimate(flops=9 << 30, bytes_accessed=12 << 20, transcendentals=0),
    )(z, *factors, *sides)


def downdate_kernel(high, low, first, second, base, out):
    lines = split(jnp.concatenate([first[0], second[0]], 0))
    out[...] = base[...] - dot3((high[...], low[...]), lines, NT)


def downdate(solved, gain_cols, base):
    rows, acts = solved[0].shape
    whole = pl.BlockSpec((rows, acts), lambda b: (0, 0))
    block = pl.BlockSpec((rows, 2 * LINE), lambda b: (0, b))
    return pl.pallas_call(
        downdate_kernel,
        grid=(8,),
        in_specs=[
            whole,
            whole,
            pl.BlockSpec((1, LINE, acts), lambda b: (2 * b, 0, 0)),
            pl.BlockSpec((1, LINE, acts), lambda b: (2 * b + 1, 0, 0)),
            block,
        ],
        out_specs=block,
        out_shape=jax.ShapeDtypeStruct(base.shape, F32),
        compiler_params=pltpu.CompilerParams(vmem_limit_bytes=VMEM_LIMIT),
        cost_estimate=pl.CostEstimate(flops=12 << 30, bytes_accessed=28 << 20, transcendentals=0),
    )(*solved, gain_cols, gain_cols, base)


def stencil_first(field, diagonal):
    centre = field[1:-1]
    side_padded = jnp.pad(centre, ((0, 0), (1, 1), (0, 0)))
    neighbours = field[:-2] + field[2:] + side_padded[:, :-2] + side_padded[:, 2:]
    return diagonal[:, :, None] * centre + COUPLING * neighbours


def plant_kernel(start, sizes, place, *refs):
    columns, at = [], 0
    for size in sizes:
        columns.append(refs[at : at + size])
        at += size
    rows_diag, cols_diag, cost = refs[at : at + 3]
    out, window = refs[-2:]
    step = pl.program_id(0)
    b = step + start
    rows = out.shape[0]
    lanes = lax.broadcasted_iota(jnp.int32, (1, LINE), 1)
    inner = lax.broadcasted_iota(jnp.int32, (LINE, 1), 0)
    column = lambda k: jnp.concatenate([ref[...] for ref in columns[k]], 0)

    @pl.when(step == 0)
    def _():
        window[0] = column(0)
        window[1] = column(1)

    here = window[1]
    after = column(2)
    sides = jnp.where(lanes == 0, 0.0, pltpu.roll(here, 1, 1)) + jnp.where(
        lanes == LINE - 1, 0.0, pltpu.roll(here, LINE - 1, 1)
    )
    field = cols_diag[pl.ds(b, 1), :] * here + COUPLING * (window[0] + after + sides)
    window[0] = here
    window[1] = after
    for a in range(rows // LINE):
        line = lambda k: field[(a + k) * LINE : (a + k + 1) * LINE]
        centre = line(1)
        sides = jnp.where(inner == 0, 0.0, pltpu.roll(centre, 1, 0)) + jnp.where(
            inner == LINE - 1, 0.0, pltpu.roll(centre, LINE - 1, 0)
        )
        here = slice(a * LINE, (a + 1) * LINE)
        out[here, :] = rows_diag[here, :] * centre + COUPLING * (line(0) + line(2) + sides)
    mine = place[1] + b - place[0]

    @pl.when((mine >= 0) & (mine < rows // LINE))
    def _():
        here = pl.ds(pl.multiple_of(mine * LINE, LINE), LINE)
        out[here, :] += jnp.where(inner == lanes, cost[pl.ds(mine, 1), :], 0.0)


def plant_part(start, count, place, value, above, below, left, right, rows_diag, cols_diag, cost, before):
    rows, cols = value.shape
    last = cols // LINE - 1
    array = pl.BlockSpec(memory_space=pltpu.VMEM)
    tall = rows + 2 * LINE

    def column(index):
        blocks = (above, value, below)
        return list(blocks), [pl.BlockSpec((x.shape[0], LINE), index) for x in blocks]

    whole = lambda x: ([x], [pl.BlockSpec((tall, LINE), lambda b: (0, 0))])
    columns = [
        whole(left) if start == 0 else column(lambda b: (0, start - 1)),
        column(lambda b: (0, start)),
        whole(right) if start == last else column(lambda b: (0, b + start + 1)),
    ]
    operands, specs = [place], [pl.BlockSpec(memory_space=pltpu.SMEM)]
    for blocks, block_specs in columns:
        operands += blocks
        specs += block_specs
    operands += [rows_diag, cols_diag, cost]
    specs += [array] * 3
    aliases = {}
    if before is not None:
        aliases = {len(operands): 0}
        operands.append(before)
        specs.append(pl.BlockSpec(memory_space=pl.ANY))
    return pl.pallas_call(
        functools.partial(plant_kernel, start, [len(blocks) for blocks, _ in columns]),
        grid=(count,),
        in_specs=specs,
        out_specs=pl.BlockSpec((rows, LINE), lambda b: (0, b + start)),
        out_shape=jax.ShapeDtypeStruct(value.shape, F32),
        scratch_shapes=[pltpu.VMEM((2, tall, LINE), F32)],
        input_output_aliases=aliases,
        compiler_params=pltpu.CompilerParams(vmem_limit_bytes=VMEM_LIMIT),
        cost_estimate=pl.CostEstimate(flops=32 << 20, bytes_accessed=16 << 20, transcendentals=0),
    )(*operands)


def local(value_matrix, inputs, plant_diag, state_cost, control_weight):
    row_index = lax.axis_index("row")
    col_index = lax.axis_index("col")
    both = ("row", "col")
    grid_side = plant_diag.shape[0]
    rows_block, cols_block = value_matrix.shape
    actuators = inputs.shape[1]
    lines_rows = rows_block // grid_side
    lines_cols = cols_block // grid_side
    diag_rows = lax.dynamic_slice_in_dim(plant_diag, row_index * lines_rows, lines_rows, 0)
    diag_cols = lax.dynamic_slice_in_dim(plant_diag, col_index * lines_cols, lines_cols, 0)
    me = row_index.astype(jnp.int32).reshape(1)
    trade = [(r * 8 + c, (2 * c + r // 8) * 8 + r % 8) for r in range(16) for c in range(8)]
    mine_inputs = lax.dynamic_slice_in_dim(inputs, col_index * LINE, LINE, 0)
    mine_inputs = lax.ppermute(mine_inputs, both, [(b, a) for a, b in trade])

    def shifted(x, axis, by):
        count = lax.axis_size(axis)
        return lax.ppermute(x, axis, [(i, i + by) for i in range(count) if 0 <= i + by < count])

    above = shifted(value_matrix[-LINE:], "row", 1)
    below = shifted(value_matrix[:LINE], "row", -1)
    operands = (
        jnp.stack([row_index * lines_rows, col_index * lines_cols]).astype(jnp.int32),
        value_matrix,
        jnp.broadcast_to(diag_rows.reshape(rows_block, 1), (rows_block, LINE)),
        diag_cols,
        state_cost.reshape(lines_rows, grid_side),
    )
    odd = product_lines(me, value_matrix, inputs, 1)
    even = product_lines(me, value_matrix, inputs, 0)
    held = {}

    def wait(came):
        came, held["inputs"], *held["rows"] = tied(came, mine_inputs, above, below)
        return came

    product = scatter_lines(even, odd, wait)
    above, below = held["rows"]
    tall = lambda cols: jnp.concatenate([above[:, cols], value_matrix[:, cols], below[:, cols]], 0)
    left = shifted(tall(slice(-LINE, None)), "col", 1)
    right = shifted(tall(slice(None, LINE)), "col", -1)

    core, x_low, y = row_index & 1, (row_index >> 1) & 1, row_index >> 2
    x_high, z = col_index & 1, col_index >> 1
    x_place = x_high * 2 + x_low

    count = grid_side
    device_of = lambda line: (line % 16) * 8 + line // 16
    over = lax.ppermute(product, both, [(device_of(i), device_of(i + 1)) for i in range(count - 1)])
    under = lax.ppermute(product, both, [(device_of(i + 1), device_of(i)) for i in range(count - 1)])
    gram = gram_blocks(held["inputs"], product)
    total = sum_cores(gram.reshape(10 * PANEL, PANEL), core)
    over, under, total = tied(over, under, total)
    diagonal = lax.dynamic_slice_in_dim(plant_diag, col_index * 16 + row_index, 1, 0)
    gain = stencil_first(jnp.stack([over, product, under]), diagonal)[0]
    gain, total = tied(gain, total)

    gain_cols = lax.all_gather(gain, "row", axis=0)
    total = scatter_four(scatter_four(total, z, Z), x_place, X)
    total = total + swap(total, Y[1]) + swap(total, Y[2]) + swap(total, Y[3])
    total = gather_four(gather_four(total, x_place, X), z, Z)

    gain, total = tied(gain, total)
    traded = lax.ppermute(gain, both, trade)
    total = joined(total, swap(total, CORE), core == 1)
    factors = factored(control_weight, total.reshape(10, PANEL, PANEL))
    around = (*operands[:2], above, below, left, right, *operands[2:])
    *factors, value = tied(*factors, value_matrix)
    base = plant_part(1, 7, around[0], value, *around[2:], None)
    traded, base, left, right = tied(traded, base, left, right)
    around = (*operands[:2], above, below, left, right, *operands[2:])

    pair = joined(traded, swap(traded, X_HIGH), x_high == 1)
    base = plant_part(8, 7, *around, base)
    pair, base, gain_cols = tied(pair, base, gain_cols)
    first, second = pair[:LINE], pair[LINE:]
    first_near, second_near = swap(first, Z[1]), swap(second, Z[3])
    base = plant_part(0, 1, *around, base)
    base = plant_part(lines_cols - 1, 1, *around, base)
    first_near, second_near, base = tied(first_near, second_near, base)
    first_far = swap(jnp.stack([first, first_near]), Z[3])
    second_far = swap(jnp.stack([second, second_near]), Z[1])

    sides = (first, first_near, first_far, second, second_near, second_far)
    solved = solve(z.astype(jnp.int32).reshape(1), factors, sides)
    return downdate(solved, gain_cols, base)


def solution(mesh):
    in_specs = (P("row", "col"), P("row", None), P(), P("row"), P())
    out_specs = P("row", "col")
    return jax.shard_map(local, mesh=mesh, in_specs=in_specs, out_specs=out_specs, check_vma=False)
```

```python
import functools

import jax
import jax.numpy as jnp
from jax import lax
from jax.experimental import pallas as pl
from jax.experimental.pallas import tpu as pltpu
from jax.sharding import PartitionSpec as P

COUPLING = 0.25
F32 = jnp.float32
BF16 = jnp.bfloat16
NN = (((1,), (0,)), ((), ()))
NT = (((1,), (1,)), ((), ()))
TN = (((0,), (0,)), ((), ()))
LINE = 128
PANEL = 256
VMEM_LIMIT = 56 << 20


def split(x):
    high = x.astype(BF16)
    return high, (x - high.astype(F32)).astype(BF16)


def dot1(a, b, dims):
    return lax.dot_general(a, b, dims, preferred_element_type=F32)


def dot3(a, b, dims):
    (a_high, a_low), (b_high, b_low) = a, b
    return dot1(a_high, b_high, dims) + dot1(a_high, b_low, dims) + dot1(a_low, b_high, dims)


def product_kernel(me_ref, first, second, inputs, out, high, low):
    @pl.when(pl.program_id(0) == 0)
    def _():
        high[...], low[...] = split(inputs[...])

    lines = split(jnp.concatenate([first[...], second[...]], 1))
    out[...] = dot3(lines, (high[...], low[...]), TN).reshape(out.shape)


def product_lines(me, value_matrix, inputs, odd):
    rows, acts = inputs.shape
    return pl.pallas_call(
        product_kernel,
        grid_spec=pltpu.PrefetchScalarGridSpec(
            num_scalar_prefetch=1,
            grid=(4,),
            in_specs=[
                pl.BlockSpec((rows, LINE), lambda i, m: (0, m[0] ^ (4 * i + odd))),
                pl.BlockSpec((rows, LINE), lambda i, m: (0, m[0] ^ (4 * i + 2 + odd))),
                pl.BlockSpec((rows, acts), lambda i, m: (0, 0)),
            ],
            out_specs=pl.BlockSpec((2, LINE, acts), lambda i, m: (i, 0, 0)),
            scratch_shapes=[pltpu.VMEM((rows, acts), BF16)] * 2,
        ),
        out_shape=jax.ShapeDtypeStruct((8, LINE, acts), F32),
        compiler_params=pltpu.CompilerParams(vmem_limit_bytes=VMEM_LIMIT),
        cost_estimate=pl.CostEstimate(flops=1 << 20, bytes_accessed=1 << 20, transcendentals=0),
    )(me, value_matrix, value_matrix, inputs)


def swap(x, mask):
    return lax.ppermute(x, ("row", "col"), [(i, i ^ mask) for i in range(128)])


CORE, X_LOW, X_HIGH = 8, 16, 1
Y = (0, 32, 64, 96)
Z = (0, 2, 4, 6)
X = (0, 16, 1, 17)


def y_first(near, blocks):
    return swap(jnp.stack([blocks[near], blocks[2]]), Y[near])


def y_second(near, blocks, got):
    far = 4 - near
    kept = blocks[far] + got[1]
    return blocks[0] + got[0] + swap(kept, Y[far])


def scatter_lines(even, odd, wait):
    got = swap(odd, CORE)
    quarter = LINE // 4
    cut = lambda i, q: even[i, q * quarter : (q + 1) * quarter] + got[i, q * quarter : (q + 1) * quarter]
    half = lambda i, q: jnp.concatenate([cut(i, q), cut(i, q + 1)], 0)
    pair = lambda m, q: jnp.stack([cut(2 * m, q), cut(2 * m + 1, q)])
    came = swap(jnp.stack([half(2 * m + 1, 0) for m in range(4)]), X_LOW)
    c = [pair(m, 2) for m in range(4)]
    d = [pair(m, 3) for m in range(4)]
    c, d = y_second(1, c, y_first(1, c)), y_second(3, d, y_first(3, d))
    came = wait(came)
    own = [half(2 * m, 0) + came[m] for m in range(4)]
    a = [o[:quarter] for o in own]
    b = [o[quarter:] for o in own]
    a, b = y_second(1, a, y_first(1, a)), y_second(3, b, y_first(3, b))
    rest = jnp.concatenate([c[0], d[0]], 0) + swap(jnp.concatenate([c[1], d[1]], 0), X_LOW)
    return jnp.concatenate([a, b, rest], 0)


def halves(x, bit):
    count = x.shape[0] // 2
    low, high = x[:count], x[count:]
    return jnp.where(bit, high, low), jnp.where(bit, low, high)


def joined(mine, got, bit):
    return jnp.concatenate([jnp.where(bit, got, mine), jnp.where(bit, mine, got)], 0)


def scatter_four(x, place, masks):
    count = x.shape[0] // 4
    own = lambda m: lax.dynamic_slice_in_dim(x, (place ^ m) * count, count, 0)
    return own(0) + swap(own(1), masks[1]) + swap(own(2), masks[2]) + swap(own(3), masks[3])


def gather_four(x, place, masks):
    parts = jnp.stack([x] + [swap(x, masks[m]) for m in range(1, 4)])
    return jnp.concatenate([lax.dynamic_index_in_dim(parts, place ^ m, 0, False) for m in range(4)], 0)


def tied(*values):
    return lax.optimization_barrier(values)


def sum_cores(x, core):
    keep, send = halves(x, core == 1)
    return keep + swap(send, CORE)


def gram_kernel(inputs, product, out):
    a = split(inputs[...])
    b = split(product[...])
    at = 0
    for k in range(4):
        for i in range(k, 4):
            left = [part[:, i * PANEL : (i + 1) * PANEL] for part in a]
            right = [part[:, k * PANEL : (k + 1) * PANEL] for part in b]
            out[at] = dot3(left, right, TN)
            at += 1


def gram_blocks(inputs, product):
    return pl.pallas_call(
        gram_kernel,
        out_shape=jax.ShapeDtypeStruct((10, PANEL, PANEL), F32),
        compiler_params=pltpu.CompilerParams(vmem_limit_bytes=VMEM_LIMIT),
        cost_estimate=pl.CostEstimate(flops=1 << 20, bytes_accessed=1 << 20, transcendentals=0),
    )(inputs, product)


def block_index(i, k):
    return k * 4 - (k * (k - 1)) // 2 + i - k


def series_inverse(a, eye, mask):
    picked = jnp.where(mask, a, 0.0)
    across = lax.rsqrt(jnp.sum(picked, axis=0, keepdims=True))
    down = lax.rsqrt(jnp.sum(picked, axis=1, keepdims=True))
    error = jnp.where(mask, 0.0, -(a * across * down))
    result = eye + error
    for _ in range(3):
        parts = split(error)
        error = dot3(parts, parts, NN)
        result = result + dot3(split(result), split(error), NN)
    short = error.astype(BF16)
    error = dot1(short, short, NN)
    result = result + dot1(result.astype(BF16), error.astype(BF16), NN)
    return result * across * down, jnp.sum(error * error, keepdims=True)


def pivot_inverse(a, work):
    size = a.shape[0]
    work[...] = a
    lanes = lax.broadcasted_iota(jnp.int32, (1, size), 1)
    rows = lax.broadcasted_iota(jnp.int32, (size, 1), 0)

    def step(p, carry):
        now = work[...]
        across = work[pl.ds(p, 1), :]
        down = jnp.sum(jnp.where(lanes == p, now, 0.0), axis=1, keepdims=True)
        inverse = 1.0 / jnp.sum(jnp.where(lanes == p, across, 0.0), axis=1, keepdims=True)
        new = now - down * (across * inverse)
        new = jnp.where(lanes == p, down * inverse, new)
        new = jnp.where(rows == p, across * inverse, new)
        work[...] = jnp.where((rows == p) & (lanes == p), -inverse, new)
        return carry

    lax.fori_loop(0, size, step, 0)
    return -work[...]


def factor_kernel(weight, gram, factor, inverses, work, worst):
    size = PANEL
    mask = lax.broadcasted_iota(jnp.int32, (size, size), 0) == lax.broadcasted_iota(jnp.int32, (size, size), 1)
    eye = jnp.where(mask, 1.0, 0.0).astype(F32)

    def run(robust):
        for k in range(4):
            for i in range(k, 4):
                here = gram[block_index(i, k)]
                factor[block_index(i, k)] = here + weight[0] * eye if i == k else here
        for k in range(4):
            here = factor[block_index(k, k)]
            if robust:
                inverse = pivot_inverse(here, work)
            else:
                inverse, off = series_inverse(here, eye, mask)
                worst[...] = off if k == 0 else jnp.where(off < worst[...], worst[...], off)
            inverses[k] = inverse
            parts = split(inverse)
            columns = [split(factor[block_index(i, k)]) for i in range(k + 1, 4)]
            lefts = []
            for i in range(k + 1, 4):
                left = dot3(columns[i - k - 1], parts, NN)
                factor[block_index(i, k)] = left
                lefts.append(split(left))
            for j in range(k + 1, 4):
                for i in range(j, 4):
                    factor[block_index(i, j)] -= dot3(lefts[i - k - 1], columns[j - k - 1], NT)

    run(False)

    @pl.when(jnp.logical_not(worst[0, 0] < 1e-6))
    def _():
        run(True)


def factored(weight, gram):
    scalar = pl.BlockSpec(memory_space=pltpu.SMEM)
    array = pl.BlockSpec(memory_space=pltpu.VMEM)
    return pl.pallas_call(
        factor_kernel,
        out_shape=[
            jax.ShapeDtypeStruct((10, PANEL, PANEL), F32),
            jax.ShapeDtypeStruct((4, PANEL, PANEL), F32),
        ],
        in_specs=[scalar, array],
        out_specs=[array, array],
        scratch_shapes=[pltpu.VMEM((PANEL, PANEL), F32), pltpu.VMEM((1, 1), F32)],
        compiler_params=pltpu.CompilerParams(vmem_limit_bytes=VMEM_LIMIT),
        cost_estimate=pl.CostEstimate(flops=9 << 30, bytes_accessed=12 << 20, transcendentals=0),
    )(weight, gram)


def solve_kernel(
    z, factor, inverses, first, first_near, first_far, second, second_near, second_far, over, under, diag, high, low, raw, out
):
    size = PANEL
    at = lambda k: slice(k * size, (k + 1) * size)

    def put(step, x_high, value):
        line = (z[0] ^ step) * 2 + x_high
        raw[pl.ds(pl.multiple_of(line * LINE, LINE), LINE), :] = value

    put(0, 0, first[...])
    put(1, 0, first_near[...])
    put(3, 0, first_far[0])
    put(2, 0, first_far[1])
    put(0, 1, second[...])
    put(3, 1, second_near[...])
    put(1, 1, second_far[0])
    put(2, 1, second_far[1])
    for a in range(8):
        line = lambda k: slice((a + k) * LINE, (a + k + 1) * LINE)
        before = raw[line(-1), :] if a > 0 else over[...]
        after = raw[line(1), :] if a < 7 else under[...]
        out[line(0), :] = plant_line(before, raw[line(0), :], after, diag[line(0), :1])
    for k in range(4):
        solved = split(out[:, at(k)])
        for i in range(k + 1, 4):
            out[:, at(i)] -= dot3(solved, split(factor[block_index(i, k)]), NT)
    for k in range(3, -1, -1):
        total = dot3(split(out[:, at(k)]), split(inverses[k]), NN)
        for i in range(k + 1, 4):
            total = total - dot3((high[:, at(i)], low[:, at(i)]), split(factor[block_index(i, k)]), NN)
        high[:, at(k)], low[:, at(k)] = split(total)


def solve(z, factors, sides):
    scalar = pl.BlockSpec(memory_space=pltpu.SMEM)
    array = pl.BlockSpec(memory_space=pltpu.VMEM)
    size = 8 * LINE
    return pl.pallas_call(
        solve_kernel,
        out_shape=[jax.ShapeDtypeStruct((size, 4 * PANEL), BF16)] * 2,
        in_specs=[scalar] + [array] * 11,
        out_specs=[array, array],
        scratch_shapes=[pltpu.VMEM((size, 4 * PANEL), F32)] * 2,
        compiler_params=pltpu.CompilerParams(vmem_limit_bytes=VMEM_LIMIT),
        cost_estimate=pl.CostEstimate(flops=9 << 30, bytes_accessed=12 << 20, transcendentals=0),
    )(z, *factors, *sides)


def downdate_kernel(high, low, before, first, second, after, over, under, diag, base, out):
    b = pl.program_id(0)
    before = jnp.where(b == 0, over[...], before[0])
    after = jnp.where(b == pl.num_programs(0) - 1, under[...], after[0])
    first, second = first[0], second[0]
    upper = plant_line(before, first, second, diag[0][:, :1])
    lower = plant_line(first, second, after, diag[1][:, :1])
    lines = split(jnp.concatenate([upper, lower], 0))
    out[...] = base[...] - dot3((high[...], low[...]), lines, NT)


def downdate(solved, lines, over, under, diag, base):
    rows, acts = solved[0].shape
    last = lines.shape[0] - 1
    whole = lambda x: pl.BlockSpec(x.shape, lambda b: (0, 0))
    block = pl.BlockSpec((rows, 2 * LINE), lambda b: (0, b))
    line = lambda k: pl.BlockSpec((1, LINE, acts), lambda b: (jnp.clip(2 * b + k, 0, last), 0, 0))
    return pl.pallas_call(
        downdate_kernel,
        grid=(8,),
        in_specs=[whole(solved[0]), whole(solved[1])]
        + [line(k) for k in (-1, 0, 1, 2)]
        + [whole(over), whole(under), pl.BlockSpec((2, LINE, LINE), lambda b: (b, 0, 0)), block],
        out_specs=block,
        out_shape=jax.ShapeDtypeStruct(base.shape, F32),
        compiler_params=pltpu.CompilerParams(vmem_limit_bytes=VMEM_LIMIT),
        cost_estimate=pl.CostEstimate(flops=12 << 30, bytes_accessed=28 << 20, transcendentals=0),
    )(*solved, lines, lines, lines, lines, over, under, diag, base)


def plant_line(before, here, after, diagonal):
    inner = lax.broadcasted_iota(jnp.int32, (LINE, 1), 0)
    sides = jnp.where(inner == 0, 0.0, pltpu.roll(here, 1, 0)) + jnp.where(
        inner == LINE - 1, 0.0, pltpu.roll(here, LINE - 1, 0)
    )
    return diagonal * here + COUPLING * (before + after + sides)


def plant_kernel(start, sizes, place, *refs):
    columns, at = [], 0
    for size in sizes:
        columns.append(refs[at : at + size])
        at += size
    rows_diag, cols_diag, cost = refs[at : at + 3]
    out, window = refs[-2:]
    step = pl.program_id(0)
    b = step + start
    rows = out.shape[0]
    lanes = lax.broadcasted_iota(jnp.int32, (1, LINE), 1)
    inner = lax.broadcasted_iota(jnp.int32, (LINE, 1), 0)
    column = lambda k: jnp.concatenate([ref[...] for ref in columns[k]], 0)

    @pl.when(step == 0)
    def _():
        window[0] = column(0)
        window[1] = column(1)

    here = window[1]
    after = column(2)
    sides = jnp.where(lanes == 0, 0.0, pltpu.roll(here, 1, 1)) + jnp.where(
        lanes == LINE - 1, 0.0, pltpu.roll(here, LINE - 1, 1)
    )
    field = cols_diag[pl.ds(b, 1), :] * here + COUPLING * (window[0] + after + sides)
    window[0] = here
    window[1] = after
    for a in range(rows // LINE):
        line = lambda k: field[(a + k) * LINE : (a + k + 1) * LINE]
        centre = line(1)
        sides = jnp.where(inner == 0, 0.0, pltpu.roll(centre, 1, 0)) + jnp.where(
            inner == LINE - 1, 0.0, pltpu.roll(centre, LINE - 1, 0)
        )
        here = slice(a * LINE, (a + 1) * LINE)
        out[here, :] = rows_diag[here, :] * centre + COUPLING * (line(0) + line(2) + sides)
    mine = place[1] + b - place[0]

    @pl.when((mine >= 0) & (mine < rows // LINE))
    def _():
        here = pl.ds(pl.multiple_of(mine * LINE, LINE), LINE)
        out[here, :] += jnp.where(inner == lanes, cost[pl.ds(mine, 1), :], 0.0)


def plant_part(start, count, place, value, above, below, left, right, rows_diag, cols_diag, cost, before):
    rows, cols = value.shape
    last = cols // LINE - 1
    array = pl.BlockSpec(memory_space=pltpu.VMEM)
    tall = rows + 2 * LINE

    def column(index):
        blocks = (above, value, below)
        return list(blocks), [pl.BlockSpec((x.shape[0], LINE), index) for x in blocks]

    whole = lambda x: ([x], [pl.BlockSpec((tall, LINE), lambda b: (0, 0))])
    columns = [
        whole(left) if start == 0 else column(lambda b: (0, start - 1)),
        column(lambda b: (0, start)),
        whole(right) if start == last else column(lambda b: (0, b + start + 1)),
    ]
    operands, specs = [place], [pl.BlockSpec(memory_space=pltpu.SMEM)]
    for blocks, block_specs in columns:
        operands += blocks
        specs += block_specs
    operands += [rows_diag, cols_diag, cost]
    specs += [array] * 3
    aliases = {}
    if before is not None:
        aliases = {len(operands): 0}
        operands.append(before)
        specs.append(pl.BlockSpec(memory_space=pl.ANY))
    return pl.pallas_call(
        functools.partial(plant_kernel, start, [len(blocks) for blocks, _ in columns]),
        grid=(count,),
        in_specs=specs,
        out_specs=pl.BlockSpec((rows, LINE), lambda b: (0, b + start)),
        out_shape=jax.ShapeDtypeStruct(value.shape, F32),
        scratch_shapes=[pltpu.VMEM((2, tall, LINE), F32)],
        input_output_aliases=aliases,
        compiler_params=pltpu.CompilerParams(vmem_limit_bytes=VMEM_LIMIT),
        cost_estimate=pl.CostEstimate(flops=32 << 20, bytes_accessed=16 << 20, transcendentals=0),
    )(*operands)


def local(value_matrix, inputs, plant_diag, state_cost, control_weight):
    row_index = lax.axis_index("row")
    col_index = lax.axis_index("col")
    both = ("row", "col")
    grid_side = plant_diag.shape[0]
    rows_block, cols_block = value_matrix.shape
    actuators = inputs.shape[1]
    lines_rows = rows_block // grid_side
    lines_cols = cols_block // grid_side
    diag_rows = lax.dynamic_slice_in_dim(plant_diag, row_index * lines_rows, lines_rows, 0)
    diag_cols = lax.dynamic_slice_in_dim(plant_diag, col_index * lines_cols, lines_cols, 0)
    me = row_index.astype(jnp.int32).reshape(1)
    trade = [(r * 8 + c, (2 * c + r // 8) * 8 + r % 8) for r in range(16) for c in range(8)]

    def shifted(x, axis, by):
        count = lax.axis_size(axis)
        return lax.ppermute(x, axis, [(i, i + by) for i in range(count) if 0 <= i + by < count])

    above = shifted(value_matrix[-LINE:], "row", 1)
    below = shifted(value_matrix[:LINE], "row", -1)
    operands = (
        jnp.stack([row_index * lines_rows, col_index * lines_cols]).astype(jnp.int32),
        value_matrix,
        jnp.broadcast_to(diag_rows.reshape(rows_block, 1), (rows_block, LINE)),
        diag_cols,
        state_cost.reshape(lines_rows, grid_side),
    )
    odd = product_lines(me, value_matrix, inputs, 1)
    even = product_lines(me, value_matrix, inputs, 0)
    rows = []

    def wait(came):
        came, *rows[:] = tied(came, above, below)
        return came

    product = scatter_lines(even, odd, wait)
    above, below = rows
    tall = lambda cols: jnp.concatenate([above[:, cols], value_matrix[:, cols], below[:, cols]], 0)
    left = shifted(tall(slice(-LINE, None)), "col", 1)
    right = shifted(tall(slice(None, LINE)), "col", -1)

    core, x_low, y = row_index & 1, (row_index >> 1) & 1, row_index >> 2
    x_high, z = col_index & 1, col_index >> 1
    x_place = x_high * 2 + x_low

    product, above, below = tied(product, above, below)
    lines = lax.all_gather(product, "row", axis=0)
    product = lax.ppermute(product, both, trade)
    around = (*operands[:2], above, below, left, right, *operands[2:])
    base = None
    for start, count in ((1, 7), (8, 7), (0, 1), (lines_cols - 1, 1)):
        base = plant_part(start, count, *around, base)
    product, base = tied(product, base)

    mine_inputs = lax.dynamic_slice_in_dim(inputs, col_index * LINE, LINE, 0)
    pair = joined(product, swap(product, X_HIGH), x_high == 1)
    gram = gram_blocks(mine_inputs, product)
    total = sum_cores(gram.reshape(10 * PANEL, PANEL), core)
    pair, total = tied(pair, total)

    first, second = pair[:LINE], pair[LINE:]
    first_near, second_near = swap(first, Z[1]), swap(second, Z[3])
    total = scatter_four(total, z, Z)
    first_near, second_near, total = tied(first_near, second_near, total)

    first_far = swap(jnp.stack([first, first_near]), Z[3])
    second_far = swap(jnp.stack([second, second_near]), Z[1])
    total = scatter_four(total, x_place, X)
    total = total + swap(total, Y[1]) + swap(total, Y[2]) + swap(total, Y[3])
    total = gather_four(total, x_place, X)
    first_far, second_far, total, lines = tied(first_far, second_far, total, lines)

    pick = lambda k, x: jnp.where(k < 2, jnp.where(k == 0, x[0], x[1]), jnp.where(k == 2, x[2], x[3]))
    head = pick(z, (first, first_near, first_far[1], first_far[0]))
    tail = pick(z ^ 3, (second, second_far[0], second_far[1], second_near))
    row_over, row_under = shifted(tail, "row", 1), shifted(head, "row", -1)
    col_over, col_under = shifted(lines[-1], "col", 1), shifted(lines[0], "col", -1)
    total = gather_four(total, z, Z)
    row_over, row_under, col_over, col_under, total = tied(row_over, row_under, col_over, col_under, total)

    total = joined(total, swap(total, CORE), core == 1)
    factors = factored(control_weight, total.reshape(10, PANEL, PANEL))
    sides = (first, first_near, first_far, second, second_near, second_far, row_over, row_under, operands[2])
    solved = solve(z.astype(jnp.int32).reshape(1), factors, sides)
    wide_diag = jnp.broadcast_to(diag_cols[:, :, None], (lines_cols, LINE, LINE))
    return downdate(solved, lines, col_over, col_under, wide_diag, base)


def solution(mesh):
    in_specs = (P("row", "col"), P("row", None), P(), P("row"), P())
    out_specs = P("row", "col")
    return jax.shard_map(local, mesh=mesh, in_specs=in_specs, out_specs=out_specs, check_vma=False)
```

```python
import functools

import jax
import jax.numpy as jnp
from jax import lax
from jax.experimental import pallas as pl
from jax.experimental.pallas import tpu as pltpu
from jax.sharding import PartitionSpec as P

COUPLING = 0.25
F32 = jnp.float32
BF16 = jnp.bfloat16
NN = (((1,), (0,)), ((), ()))
NT = (((1,), (1,)), ((), ()))
TN = (((0,), (0,)), ((), ()))
LINE = 128
PANEL = 256
VMEM_LIMIT = 56 << 20


def split(x):
    high = x.astype(BF16)
    return high, (x - high.astype(F32)).astype(BF16)


def dot1(a, b, dims):
    return lax.dot_general(a, b, dims, preferred_element_type=F32)


def dot3(a, b, dims):
    (a_high, a_low), (b_high, b_low) = a, b
    return dot1(a_high, b_high, dims) + dot1(a_high, b_low, dims) + dot1(a_low, b_high, dims)


def product_kernel(me_ref, first, second, inputs, out, high, low):
    @pl.when(pl.program_id(0) == 0)
    def _():
        high[...], low[...] = split(inputs[...])

    lines = split(jnp.concatenate([first[...], second[...]], 1))
    out[...] = dot3(lines, (high[...], low[...]), TN).reshape(out.shape)


def product_lines(me, value_matrix, inputs, odd):
    rows, acts = inputs.shape
    return pl.pallas_call(
        product_kernel,
        grid_spec=pltpu.PrefetchScalarGridSpec(
            num_scalar_prefetch=1,
            grid=(4,),
            in_specs=[
                pl.BlockSpec((rows, LINE), lambda i, m: (0, m[0] ^ (4 * i + odd))),
                pl.BlockSpec((rows, LINE), lambda i, m: (0, m[0] ^ (4 * i + 2 + odd))),
                pl.BlockSpec((rows, acts), lambda i, m: (0, 0)),
            ],
            out_specs=pl.BlockSpec((2, LINE, acts), lambda i, m: (i, 0, 0)),
            scratch_shapes=[pltpu.VMEM((rows, acts), BF16)] * 2,
        ),
        out_shape=jax.ShapeDtypeStruct((8, LINE, acts), F32),
        compiler_params=pltpu.CompilerParams(vmem_limit_bytes=VMEM_LIMIT),
        cost_estimate=pl.CostEstimate(flops=1 << 20, bytes_accessed=1 << 20, transcendentals=0),
    )(me, value_matrix, value_matrix, inputs)


def swap(x, mask):
    return lax.ppermute(x, ("row", "col"), [(i, i ^ mask) for i in range(128)])


CORE, X_LOW, X_HIGH = 8, 16, 1
Y = (0, 32, 64, 96)
Z = (0, 2, 4, 6)
X = (0, 16, 1, 17)


def y_first(near, blocks):
    return swap(jnp.stack([blocks[near], blocks[2]]), Y[near])


def y_second(near, blocks, got):
    far = 4 - near
    kept = blocks[far] + got[1]
    return blocks[0] + got[0] + swap(kept, Y[far])


def scatter_lines(even, odd, wait):
    got = swap(odd, CORE)
    quarter = LINE // 4
    cut = lambda i, q: even[i, q * quarter : (q + 1) * quarter] + got[i, q * quarter : (q + 1) * quarter]
    half = lambda i, q: jnp.concatenate([cut(i, q), cut(i, q + 1)], 0)
    pair = lambda m, q: jnp.stack([cut(2 * m, q), cut(2 * m + 1, q)])
    came = swap(jnp.stack([half(2 * m + 1, 0) for m in range(4)]), X_LOW)
    c = [pair(m, 2) for m in range(4)]
    d = [pair(m, 3) for m in range(4)]
    c, d = y_second(1, c, y_first(1, c)), y_second(3, d, y_first(3, d))
    came = wait(came)
    own = [half(2 * m, 0) + came[m] for m in range(4)]
    a = [o[:quarter] for o in own]
    b = [o[quarter:] for o in own]
    a, b = y_second(1, a, y_first(1, a)), y_second(3, b, y_first(3, b))
    rest = jnp.concatenate([c[0], d[0]], 0) + swap(jnp.concatenate([c[1], d[1]], 0), X_LOW)
    return jnp.concatenate([a, b, rest], 0)


def halves(x, bit):
    count = x.shape[0] // 2
    low, high = x[:count], x[count:]
    return jnp.where(bit, high, low), jnp.where(bit, low, high)


def joined(mine, got, bit):
    return jnp.concatenate([jnp.where(bit, got, mine), jnp.where(bit, mine, got)], 0)


def scatter_four(x, place, masks):
    count = x.shape[0] // 4
    own = lambda m: lax.dynamic_slice_in_dim(x, (place ^ m) * count, count, 0)
    return own(0) + swap(own(1), masks[1]) + swap(own(2), masks[2]) + swap(own(3), masks[3])


def gather_four(x, place, masks):
    parts = jnp.stack([x] + [swap(x, masks[m]) for m in range(1, 4)])
    return jnp.concatenate([lax.dynamic_index_in_dim(parts, place ^ m, 0, False) for m in range(4)], 0)


def tied(*values):
    return lax.optimization_barrier(values)


def sum_cores(x, core):
    keep, send = halves(x, core == 1)
    return keep + swap(send, CORE)


def gram_kernel(inputs, product, out):
    a = split(inputs[...])
    b = split(product[...])
    at = 0
    for k in range(4):
        for i in range(k, 4):
            left = [part[:, i * PANEL : (i + 1) * PANEL] for part in a]
            right = [part[:, k * PANEL : (k + 1) * PANEL] for part in b]
            out[at] = dot3(left, right, TN)
            at += 1


def gram_blocks(inputs, product):
    return pl.pallas_call(
        gram_kernel,
        out_shape=jax.ShapeDtypeStruct((10, PANEL, PANEL), F32),
        compiler_params=pltpu.CompilerParams(vmem_limit_bytes=VMEM_LIMIT),
        cost_estimate=pl.CostEstimate(flops=1 << 20, bytes_accessed=1 << 20, transcendentals=0),
    )(inputs, product)


def block_index(i, k):
    return k * 4 - (k * (k - 1)) // 2 + i - k


def series_inverse(a, eye, mask):
    picked = jnp.where(mask, a, 0.0)
    across = lax.rsqrt(jnp.sum(picked, axis=0, keepdims=True))
    down = lax.rsqrt(jnp.sum(picked, axis=1, keepdims=True))
    error = jnp.where(mask, 0.0, -(a * across * down))
    result = eye + error
    for _ in range(3):
        parts = split(error)
        error = dot3(parts, parts, NN)
        result = result + dot3(split(result), split(error), NN)
    short = error.astype(BF16)
    error = dot1(short, short, NN)
    result = result + dot1(result.astype(BF16), error.astype(BF16), NN)
    return result * across * down, jnp.sum(error * error, keepdims=True)


def pivot_inverse(a, work):
    size = a.shape[0]
    work[...] = a
    lanes = lax.broadcasted_iota(jnp.int32, (1, size), 1)
    rows = lax.broadcasted_iota(jnp.int32, (size, 1), 0)

    def step(p, carry):
        now = work[...]
        across = work[pl.ds(p, 1), :]
        down = jnp.sum(jnp.where(lanes == p, now, 0.0), axis=1, keepdims=True)
        inverse = 1.0 / jnp.sum(jnp.where(lanes == p, across, 0.0), axis=1, keepdims=True)
        new = now - down * (across * inverse)
        new = jnp.where(lanes == p, down * inverse, new)
        new = jnp.where(rows == p, across * inverse, new)
        work[...] = jnp.where((rows == p) & (lanes == p), -inverse, new)
        return carry

    lax.fori_loop(0, size, step, 0)
    return -work[...]


def factor_kernel(weight, gram, factor, inverses, work, worst):
    size = PANEL
    mask = lax.broadcasted_iota(jnp.int32, (size, size), 0) == lax.broadcasted_iota(jnp.int32, (size, size), 1)
    eye = jnp.where(mask, 1.0, 0.0).astype(F32)

    def run(robust):
        for k in range(4):
            for i in range(k, 4):
                here = gram[block_index(i, k)]
                factor[block_index(i, k)] = here + weight[0] * eye if i == k else here
        for k in range(4):
            here = factor[block_index(k, k)]
            if robust:
                inverse = pivot_inverse(here, work)
            else:
                inverse, off = series_inverse(here, eye, mask)
                worst[...] = off if k == 0 else jnp.where(off < worst[...], worst[...], off)
            inverses[k] = inverse
            parts = split(inverse)
            columns = [split(factor[block_index(i, k)]) for i in range(k + 1, 4)]
            lefts = []
            for i in range(k + 1, 4):
                left = dot3(columns[i - k - 1], parts, NN)
                factor[block_index(i, k)] = left
                lefts.append(split(left))
            for j in range(k + 1, 4):
                for i in range(j, 4):
                    factor[block_index(i, j)] -= dot3(lefts[i - k - 1], columns[j - k - 1], NT)

    run(False)

    @pl.when(jnp.logical_not(worst[0, 0] < 1e-6))
    def _():
        run(True)


def factored(weight, gram):
    scalar = pl.BlockSpec(memory_space=pltpu.SMEM)
    array = pl.BlockSpec(memory_space=pltpu.VMEM)
    return pl.pallas_call(
        factor_kernel,
        out_shape=[
            jax.ShapeDtypeStruct((10, PANEL, PANEL), F32),
            jax.ShapeDtypeStruct((4, PANEL, PANEL), F32),
        ],
        in_specs=[scalar, array],
        out_specs=[array, array],
        scratch_shapes=[pltpu.VMEM((PANEL, PANEL), F32), pltpu.VMEM((1, 1), F32)],
        compiler_params=pltpu.CompilerParams(vmem_limit_bytes=VMEM_LIMIT),
        cost_estimate=pl.CostEstimate(flops=9 << 30, bytes_accessed=12 << 20, transcendentals=0),
    )(weight, gram)


def solve_kernel(
    z, factor, inverses, first, first_near, first_far, second, second_near, second_far, over, under, diag, high, low, raw, out
):
    size = PANEL
    at = lambda k: slice(k * size, (k + 1) * size)

    def put(step, x_high, value):
        line = (z[0] ^ step) * 2 + x_high
        raw[pl.ds(pl.multiple_of(line * LINE, LINE), LINE), :] = value

    put(0, 0, first[...])
    put(1, 0, first_near[...])
    put(3, 0, first_far[0])
    put(2, 0, first_far[1])
    put(0, 1, second[...])
    put(3, 1, second_near[...])
    put(1, 1, second_far[0])
    put(2, 1, second_far[1])
    for a in range(8):
        line = lambda k: slice((a + k) * LINE, (a + k + 1) * LINE)
        before = raw[line(-1), :] if a > 0 else over[...]
        after = raw[line(1), :] if a < 7 else under[...]
        out[line(0), :] = plant_line(before, raw[line(0), :], after, diag[line(0), :1])
    for k in range(4):
        solved = split(out[:, at(k)])
        for i in range(k + 1, 4):
            out[:, at(i)] -= dot3(solved, split(factor[block_index(i, k)]), NT)
    for k in range(3, -1, -1):
        total = dot3(split(out[:, at(k)]), split(inverses[k]), NN)
        for i in range(k + 1, 4):
            total = total - dot3((high[:, at(i)], low[:, at(i)]), split(factor[block_index(i, k)]), NN)
        high[:, at(k)], low[:, at(k)] = split(total)


def solve(z, factors, sides):
    scalar = pl.BlockSpec(memory_space=pltpu.SMEM)
    array = pl.BlockSpec(memory_space=pltpu.VMEM)
    size = 8 * LINE
    return pl.pallas_call(
        solve_kernel,
        out_shape=[jax.ShapeDtypeStruct((size, 4 * PANEL), BF16)] * 2,
        in_specs=[scalar] + [array] * 11,
        out_specs=[array, array],
        scratch_shapes=[pltpu.VMEM((size, 4 * PANEL), F32)] * 2,
        compiler_params=pltpu.CompilerParams(vmem_limit_bytes=VMEM_LIMIT),
        cost_estimate=pl.CostEstimate(flops=9 << 30, bytes_accessed=12 << 20, transcendentals=0),
    )(z, *factors, *sides)


def downdate_kernel(high, low, before, first, second, after, over, under, diag, base, out):
    b = pl.program_id(0)
    before = jnp.where(b == 0, over[...], before[0])
    after = jnp.where(b == pl.num_programs(0) - 1, under[...], after[0])
    first, second = first[0], second[0]
    upper = plant_line(before, first, second, diag[0][:, :1])
    lower = plant_line(first, second, after, diag[1][:, :1])
    lines = split(jnp.concatenate([upper, lower], 0))
    out[...] = base[...] - dot3((high[...], low[...]), lines, NT)


def downdate(solved, lines, over, under, diag, base):
    rows, acts = solved[0].shape
    last = lines.shape[0] - 1
    whole = lambda x: pl.BlockSpec(x.shape, lambda b: (0, 0))
    block = pl.BlockSpec((rows, 2 * LINE), lambda b: (0, b))
    line = lambda k: pl.BlockSpec((1, LINE, acts), lambda b: (jnp.clip(2 * b + k, 0, last), 0, 0))
    return pl.pallas_call(
        downdate_kernel,
        grid=(8,),
        in_specs=[whole(solved[0]), whole(solved[1])]
        + [line(k) for k in (-1, 0, 1, 2)]
        + [whole(over), whole(under), pl.BlockSpec((2, LINE, LINE), lambda b: (b, 0, 0)), block],
        out_specs=block,
        out_shape=jax.ShapeDtypeStruct(base.shape, F32),
        compiler_params=pltpu.CompilerParams(vmem_limit_bytes=VMEM_LIMIT),
        cost_estimate=pl.CostEstimate(flops=12 << 30, bytes_accessed=28 << 20, transcendentals=0),
    )(*solved, lines, lines, lines, lines, over, under, diag, base)


def plant_line(before, here, after, diagonal):
    inner = lax.broadcasted_iota(jnp.int32, (LINE, 1), 0)
    sides = jnp.where(inner == 0, 0.0, pltpu.roll(here, 1, 0)) + jnp.where(
        inner == LINE - 1, 0.0, pltpu.roll(here, LINE - 1, 0)
    )
    return diagonal * here + COUPLING * (before + after + sides)


def plant_kernel(start, sizes, place, *refs):
    columns, at = [], 0
    for size in sizes:
        columns.append(refs[at : at + size])
        at += size
    rows_diag, cols_diag, cost = refs[at : at + 3]
    out, window = refs[-2:]
    step = pl.program_id(0)
    b = step + start
    rows = out.shape[0]
    lanes = lax.broadcasted_iota(jnp.int32, (1, LINE), 1)
    inner = lax.broadcasted_iota(jnp.int32, (LINE, 1), 0)
    column = lambda k: jnp.concatenate([ref[...] for ref in columns[k]], 0)

    @pl.when(step == 0)
    def _():
        window[0] = column(0)
        window[1] = column(1)

    here = window[1]
    after = column(2)
    sides = jnp.where(lanes == 0, 0.0, pltpu.roll(here, 1, 1)) + jnp.where(
        lanes == LINE - 1, 0.0, pltpu.roll(here, LINE - 1, 1)
    )
    field = cols_diag[pl.ds(b, 1), :] * here + COUPLING * (window[0] + after + sides)
    window[0] = here
    window[1] = after
    for a in range(rows // LINE):
        line = lambda k: field[(a + k) * LINE : (a + k + 1) * LINE]
        centre = line(1)
        sides = jnp.where(inner == 0, 0.0, pltpu.roll(centre, 1, 0)) + jnp.where(
            inner == LINE - 1, 0.0, pltpu.roll(centre, LINE - 1, 0)
        )
        here = slice(a * LINE, (a + 1) * LINE)
        out[here, :] = rows_diag[here, :] * centre + COUPLING * (line(0) + line(2) + sides)
    mine = place[1] + b - place[0]

    @pl.when((mine >= 0) & (mine < rows // LINE))
    def _():
        here = pl.ds(pl.multiple_of(mine * LINE, LINE), LINE)
        out[here, :] += jnp.where(inner == lanes, cost[pl.ds(mine, 1), :], 0.0)


def plant_part(start, count, place, value, above, below, left, right, rows_diag, cols_diag, cost, before):
    rows, cols = value.shape
    last = cols // LINE - 1
    array = pl.BlockSpec(memory_space=pltpu.VMEM)
    tall = rows + 2 * LINE

    def column(index):
        blocks = (above, value, below)
        return list(blocks), [pl.BlockSpec((x.shape[0], LINE), index) for x in blocks]

    whole = lambda x: ([x], [pl.BlockSpec((tall, LINE), lambda b: (0, 0))])
    columns = [
        whole(left) if start == 0 else column(lambda b: (0, start - 1)),
        column(lambda b: (0, start)),
        whole(right) if start == last else column(lambda b: (0, b + start + 1)),
    ]
    operands, specs = [place], [pl.BlockSpec(memory_space=pltpu.SMEM)]
    for blocks, block_specs in columns:
        operands += blocks
        specs += block_specs
    operands += [rows_diag, cols_diag, cost]
    specs += [array] * 3
    aliases = {}
    if before is not None:
        aliases = {len(operands): 0}
        operands.append(before)
        specs.append(pl.BlockSpec(memory_space=pl.ANY))
    return pl.pallas_call(
        functools.partial(plant_kernel, start, [len(blocks) for blocks, _ in columns]),
        grid=(count,),
        in_specs=specs,
        out_specs=pl.BlockSpec((rows, LINE), lambda b: (0, b + start)),
        out_shape=jax.ShapeDtypeStruct(value.shape, F32),
        scratch_shapes=[pltpu.VMEM((2, tall, LINE), F32)],
        input_output_aliases=aliases,
        compiler_params=pltpu.CompilerParams(vmem_limit_bytes=VMEM_LIMIT),
        cost_estimate=pl.CostEstimate(flops=32 << 20, bytes_accessed=16 << 20, transcendentals=0),
    )(*operands)


def local(value_matrix, inputs, plant_diag, state_cost, control_weight):
    row_index = lax.axis_index("row")
    col_index = lax.axis_index("col")
    both = ("row", "col")
    grid_side = plant_diag.shape[0]
    rows_block, cols_block = value_matrix.shape
    actuators = inputs.shape[1]
    lines_rows = rows_block // grid_side
    lines_cols = cols_block // grid_side
    diag_rows = lax.dynamic_slice_in_dim(plant_diag, row_index * lines_rows, lines_rows, 0)
    diag_cols = lax.dynamic_slice_in_dim(plant_diag, col_index * lines_cols, lines_cols, 0)
    me = row_index.astype(jnp.int32).reshape(1)
    trade = [(r * 8 + c, (2 * c + r // 8) * 8 + r % 8) for r in range(16) for c in range(8)]

    def shifted(x, axis, by):
        count = lax.axis_size(axis)
        return lax.ppermute(x, axis, [(i, i + by) for i in range(count) if 0 <= i + by < count])

    above = shifted(value_matrix[-LINE:], "row", 1)
    below = shifted(value_matrix[:LINE], "row", -1)
    operands = (
        jnp.stack([row_index * lines_rows, col_index * lines_cols]).astype(jnp.int32),
        value_matrix,
        jnp.broadcast_to(diag_rows.reshape(rows_block, 1), (rows_block, LINE)),
        diag_cols,
        state_cost.reshape(lines_rows, grid_side),
    )
    odd = product_lines(me, value_matrix, inputs, 1)
    even = product_lines(me, value_matrix, inputs, 0)
    rows = []

    def wait(came):
        came, *rows[:] = tied(came, above, below)
        return came

    product = scatter_lines(even, odd, wait)
    above, below = rows
    tall = lambda cols: jnp.concatenate([above[:, cols], value_matrix[:, cols], below[:, cols]], 0)
    left = shifted(tall(slice(-LINE, None)), "col", 1)
    right = shifted(tall(slice(None, LINE)), "col", -1)

    core, x_low, y = row_index & 1, (row_index >> 1) & 1, row_index >> 2
    x_high, z = col_index & 1, col_index >> 1
    x_place = x_high * 2 + x_low

    product, above, below = tied(product, above, below)
    traded = lax.ppermute(product, both, trade)
    around = (*operands[:2], above, below, left, right, *operands[2:])
    base = plant_part(1, 7, *around, None)
    base = plant_part(8, 7, *around, base)
    traded, product, base = tied(traded, product, base)
    lines = lax.all_gather(product, "row", axis=0)

    mine_inputs = lax.dynamic_slice_in_dim(inputs, col_index * LINE, LINE, 0)
    pair = joined(traded, swap(traded, X_HIGH), x_high == 1)
    gram = gram_blocks(mine_inputs, traded)
    total = sum_cores(gram.reshape(10 * PANEL, PANEL), core)
    pair, total, left, right = tied(pair, total, left, right)

    first, second = pair[:LINE], pair[LINE:]
    first_near, second_near = swap(first, Z[1]), swap(second, Z[3])
    total = scatter_four(total, z, Z)
    around = (*operands[:2], above, below, left, right, *operands[2:])
    for start in (0, lines_cols - 1):
        base = plant_part(start, 1, *around, base)
    first_near, second_near, total, base = tied(first_near, second_near, total, base)

    first_far = swap(jnp.stack([first, first_near]), Z[3])
    second_far = swap(jnp.stack([second, second_near]), Z[1])
    total = scatter_four(total, x_place, X)
    total = total + swap(total, Y[1]) + swap(total, Y[2]) + swap(total, Y[3])
    total = gather_four(total, x_place, X)
    first_far, second_far, total, lines = tied(first_far, second_far, total, lines)

    pick = lambda k, x: jnp.where(k < 2, jnp.where(k == 0, x[0], x[1]), jnp.where(k == 2, x[2], x[3]))
    head = pick(z, (first, first_near, first_far[1], first_far[0]))
    tail = pick(z ^ 3, (second, second_far[0], second_far[1], second_near))
    row_over, row_under = shifted(tail, "row", 1), shifted(head, "row", -1)
    col_over, col_under = shifted(lines[-1], "col", 1), shifted(lines[0], "col", -1)
    total = gather_four(total, z, Z)
    total = joined(total, swap(total, CORE), core == 1)
    factors = factored(control_weight, total.reshape(10, PANEL, PANEL))
    sides = (first, first_near, first_far, second, second_near, second_far, row_over, row_under, operands[2])
    solved = solve(z.astype(jnp.int32).reshape(1), factors, sides)
    wide_diag = jnp.broadcast_to(diag_cols[:, :, None], (lines_cols, LINE, LINE))
    return downdate(solved, lines, col_over, col_under, wide_diag, base)


def solution(mesh):
    in_specs = (P("row", "col"), P("row", None), P(), P("row"), P())
    out_specs = P("row", "col")
    return jax.shard_map(local, mesh=mesh, in_specs=in_specs, out_specs=out_specs, check_vma=False)
```

```python
import functools

import jax
import jax.numpy as jnp
from jax import lax
from jax.experimental import pallas as pl
from jax.experimental.pallas import tpu as pltpu
from jax.sharding import PartitionSpec as P

COUPLING = 0.25
F32 = jnp.float32
BF16 = jnp.bfloat16
NN = (((1,), (0,)), ((), ()))
NT = (((1,), (1,)), ((), ()))
TN = (((0,), (0,)), ((), ()))
LINE = 128
PANEL = 256
VMEM_LIMIT = 56 << 20


def split(x):
    high = x.astype(BF16)
    return high, (x - high.astype(F32)).astype(BF16)


def dot1(a, b, dims):
    return lax.dot_general(a, b, dims, preferred_element_type=F32)


def dot3(a, b, dims):
    (a_high, a_low), (b_high, b_low) = a, b
    return dot1(a_high, b_high, dims) + dot1(a_high, b_low, dims) + dot1(a_low, b_high, dims)


def product_kernel(me_ref, first, second, inputs, out, high, low):
    @pl.when(pl.program_id(0) == 0)
    def _():
        high[...], low[...] = split(inputs[...])

    lines = split(jnp.concatenate([first[...], second[...]], 1))
    out[...] = dot3(lines, (high[...], low[...]), TN).reshape(out.shape)


def product_lines(me, value_matrix, inputs, odd):
    rows, acts = inputs.shape
    return pl.pallas_call(
        product_kernel,
        grid_spec=pltpu.PrefetchScalarGridSpec(
            num_scalar_prefetch=1,
            grid=(4,),
            in_specs=[
                pl.BlockSpec((rows, LINE), lambda i, m: (0, m[0] ^ (4 * i + odd))),
                pl.BlockSpec((rows, LINE), lambda i, m: (0, m[0] ^ (4 * i + 2 + odd))),
                pl.BlockSpec((rows, acts), lambda i, m: (0, 0)),
            ],
            out_specs=pl.BlockSpec((2, LINE, acts), lambda i, m: (i, 0, 0)),
            scratch_shapes=[pltpu.VMEM((rows, acts), BF16)] * 2,
        ),
        out_shape=jax.ShapeDtypeStruct((8, LINE, acts), F32),
        compiler_params=pltpu.CompilerParams(vmem_limit_bytes=VMEM_LIMIT),
        cost_estimate=pl.CostEstimate(flops=1 << 20, bytes_accessed=1 << 20, transcendentals=0),
    )(me, value_matrix, value_matrix, inputs)


def swap(x, mask):
    return lax.ppermute(x, ("row", "col"), [(i, i ^ mask) for i in range(128)])


CORE, X_LOW, X_HIGH = 8, 16, 1
Y = (0, 32, 64, 96)
Z = (0, 2, 4, 6)
X = (0, 16, 1, 17)


def y_first(near, blocks):
    return swap(jnp.stack([blocks[near], blocks[2]]), Y[near])


def y_second(near, blocks, got):
    far = 4 - near
    kept = blocks[far] + got[1]
    return blocks[0] + got[0] + swap(kept, Y[far])


def scatter_lines(even, odd, wait):
    got = swap(odd, CORE)
    quarter = LINE // 4
    cut = lambda i, q: even[i, q * quarter : (q + 1) * quarter] + got[i, q * quarter : (q + 1) * quarter]
    half = lambda i, q: jnp.concatenate([cut(i, q), cut(i, q + 1)], 0)
    pair = lambda m, q: jnp.stack([cut(2 * m, q), cut(2 * m + 1, q)])
    came = swap(jnp.stack([half(2 * m + 1, 0) for m in range(4)]), X_LOW)
    c = [pair(m, 2) for m in range(4)]
    d = [pair(m, 3) for m in range(4)]
    c, d = y_second(1, c, y_first(1, c)), y_second(3, d, y_first(3, d))
    came = wait(came)
    own = [half(2 * m, 0) + came[m] for m in range(4)]
    a = [o[:quarter] for o in own]
    b = [o[quarter:] for o in own]
    a, b = y_second(1, a, y_first(1, a)), y_second(3, b, y_first(3, b))
    rest = jnp.concatenate([c[0], d[0]], 0) + swap(jnp.concatenate([c[1], d[1]], 0), X_LOW)
    return jnp.concatenate([a, b, rest], 0)


def halves(x, bit):
    count = x.shape[0] // 2
    low, high = x[:count], x[count:]
    return jnp.where(bit, high, low), jnp.where(bit, low, high)


def joined(mine, got, bit):
    return jnp.concatenate([jnp.where(bit, got, mine), jnp.where(bit, mine, got)], 0)


def scatter_four(x, place, masks):
    count = x.shape[0] // 4
    own = lambda m: lax.dynamic_slice_in_dim(x, (place ^ m) * count, count, 0)
    return own(0) + swap(own(1), masks[1]) + swap(own(2), masks[2]) + swap(own(3), masks[3])


def gather_four(x, place, masks):
    parts = jnp.stack([x] + [swap(x, masks[m]) for m in range(1, 4)])
    return jnp.concatenate([lax.dynamic_index_in_dim(parts, place ^ m, 0, False) for m in range(4)], 0)


def tied(*values):
    return lax.optimization_barrier(values)


def sum_cores(x, core):
    keep, send = halves(x, core == 1)
    return keep + swap(send, CORE)


def gram_kernel(inputs, product, out):
    a = split(inputs[...])
    b = split(product[...])
    at = 0
    for k in range(4):
        for i in range(k, 4):
            left = [part[:, i * PANEL : (i + 1) * PANEL] for part in a]
            right = [part[:, k * PANEL : (k + 1) * PANEL] for part in b]
            out[at] = dot3(left, right, TN)
            at += 1


def gram_blocks(inputs, product):
    return pl.pallas_call(
        gram_kernel,
        out_shape=jax.ShapeDtypeStruct((10, PANEL, PANEL), F32),
        compiler_params=pltpu.CompilerParams(vmem_limit_bytes=VMEM_LIMIT),
        cost_estimate=pl.CostEstimate(flops=1 << 20, bytes_accessed=1 << 20, transcendentals=0),
    )(inputs, product)


def block_index(i, k):
    return k * 4 - (k * (k - 1)) // 2 + i - k


def series_inverse(a, eye, mask):
    picked = jnp.where(mask, a, 0.0)
    across = lax.rsqrt(jnp.sum(picked, axis=0, keepdims=True))
    down = lax.rsqrt(jnp.sum(picked, axis=1, keepdims=True))
    error = jnp.where(mask, 0.0, -(a * across * down))
    result = eye + error
    for _ in range(3):
        parts = split(error)
        error = dot3(parts, parts, NN)
        result = result + dot3(split(result), split(error), NN)
    short = error.astype(BF16)
    error = dot1(short, short, NN)
    result = result + dot1(result.astype(BF16), error.astype(BF16), NN)
    return result * across * down, jnp.sum(error * error, keepdims=True)


def pivot_inverse(a, work):
    size = a.shape[0]
    work[...] = a
    lanes = lax.broadcasted_iota(jnp.int32, (1, size), 1)
    rows = lax.broadcasted_iota(jnp.int32, (size, 1), 0)

    def step(p, carry):
        now = work[...]
        across = work[pl.ds(p, 1), :]
        down = jnp.sum(jnp.where(lanes == p, now, 0.0), axis=1, keepdims=True)
        inverse = 1.0 / jnp.sum(jnp.where(lanes == p, across, 0.0), axis=1, keepdims=True)
        new = now - down * (across * inverse)
        new = jnp.where(lanes == p, down * inverse, new)
        new = jnp.where(rows == p, across * inverse, new)
        work[...] = jnp.where((rows == p) & (lanes == p), -inverse, new)
        return carry

    lax.fori_loop(0, size, step, 0)
    return -work[...]


def factor_kernel(weight, gram, factor, inverses, work, worst):
    size = PANEL
    mask = lax.broadcasted_iota(jnp.int32, (size, size), 0) == lax.broadcasted_iota(jnp.int32, (size, size), 1)
    eye = jnp.where(mask, 1.0, 0.0).astype(F32)

    def run(robust):
        for k in range(4):
            for i in range(k, 4):
                here = gram[block_index(i, k)]
                factor[block_index(i, k)] = here + weight[0] * eye if i == k else here
        for k in range(4):
            here = factor[block_index(k, k)]
            if robust:
                inverse = pivot_inverse(here, work)
            else:
                inverse, off = series_inverse(here, eye, mask)
                worst[...] = off if k == 0 else jnp.where(off < worst[...], worst[...], off)
            inverses[k] = inverse
            parts = split(inverse)
            columns = [split(factor[block_index(i, k)]) for i in range(k + 1, 4)]
            lefts = []
            for i in range(k + 1, 4):
                left = dot3(columns[i - k - 1], parts, NN)
                factor[block_index(i, k)] = left
                lefts.append(split(left))
            for j in range(k + 1, 4):
                for i in range(j, 4):
                    factor[block_index(i, j)] -= dot3(lefts[i - k - 1], columns[j - k - 1], NT)

    run(False)

    @pl.when(jnp.logical_not(worst[0, 0] < 1e-6))
    def _():
        run(True)


def factored(weight, gram):
    scalar = pl.BlockSpec(memory_space=pltpu.SMEM)
    array = pl.BlockSpec(memory_space=pltpu.VMEM)
    return pl.pallas_call(
        factor_kernel,
        out_shape=[
            jax.ShapeDtypeStruct((10, PANEL, PANEL), F32),
            jax.ShapeDtypeStruct((4, PANEL, PANEL), F32),
        ],
        in_specs=[scalar, array],
        out_specs=[array, array],
        scratch_shapes=[pltpu.VMEM((PANEL, PANEL), F32), pltpu.VMEM((1, 1), F32)],
        compiler_params=pltpu.CompilerParams(vmem_limit_bytes=VMEM_LIMIT),
        cost_estimate=pl.CostEstimate(flops=9 << 30, bytes_accessed=12 << 20, transcendentals=0),
    )(weight, gram)


def solve_kernel(
    z, factor, inverses, first, first_near, first_far, second, second_near, second_far, over, under, diag, high, low, raw, out
):
    size = PANEL
    at = lambda k: slice(k * size, (k + 1) * size)

    def put(step, x_high, value):
        line = (z[0] ^ step) * 2 + x_high
        raw[pl.ds(pl.multiple_of(line * LINE, LINE), LINE), :] = value

    put(0, 0, first[...])
    put(1, 0, first_near[...])
    put(3, 0, first_far[0])
    put(2, 0, first_far[1])
    put(0, 1, second[...])
    put(3, 1, second_near[...])
    put(1, 1, second_far[0])
    put(2, 1, second_far[1])
    for a in range(8):
        line = lambda k: slice((a + k) * LINE, (a + k + 1) * LINE)
        before = raw[line(-1), :] if a > 0 else over[...]
        after = raw[line(1), :] if a < 7 else under[...]
        out[line(0), :] = plant_line(before, raw[line(0), :], after, diag[line(0), :1])
    for k in range(4):
        solved = split(out[:, at(k)])
        for i in range(k + 1, 4):
            out[:, at(i)] -= dot3(solved, split(factor[block_index(i, k)]), NT)
    for k in range(3, -1, -1):
        total = dot3(split(out[:, at(k)]), split(inverses[k]), NN)
        for i in range(k + 1, 4):
            total = total - dot3((high[:, at(i)], low[:, at(i)]), split(factor[block_index(i, k)]), NN)
        high[:, at(k)], low[:, at(k)] = split(total)


def solve(z, factors, sides):
    scalar = pl.BlockSpec(memory_space=pltpu.SMEM)
    array = pl.BlockSpec(memory_space=pltpu.VMEM)
    size = 8 * LINE
    return pl.pallas_call(
        solve_kernel,
        out_shape=[jax.ShapeDtypeStruct((size, 4 * PANEL), BF16)] * 2,
        in_specs=[scalar] + [array] * 11,
        out_specs=[array, array],
        scratch_shapes=[pltpu.VMEM((size, 4 * PANEL), F32)] * 2,
        compiler_params=pltpu.CompilerParams(vmem_limit_bytes=VMEM_LIMIT),
        cost_estimate=pl.CostEstimate(flops=9 << 30, bytes_accessed=12 << 20, transcendentals=0),
    )(z, *factors, *sides)


def downdate_kernel(high, low, before, first, second, after, over, under, diag, base, out):
    b = pl.program_id(0)
    before = jnp.where(b == 0, over[...], before[0])
    after = jnp.where(b == pl.num_programs(0) - 1, under[...], after[0])
    first, second = first[0], second[0]
    upper = plant_line(before, first, second, diag[0][:, :1])
    lower = plant_line(first, second, after, diag[1][:, :1])
    lines = split(jnp.concatenate([upper, lower], 0))
    out[...] = base[...] - dot3((high[...], low[...]), lines, NT)


def downdate(solved, lines, over, under, diag, base):
    rows, acts = solved[0].shape
    last = lines.shape[0] - 1
    whole = lambda x: pl.BlockSpec(x.shape, lambda b: (0, 0))
    block = pl.BlockSpec((rows, 2 * LINE), lambda b: (0, b))
    line = lambda k: pl.BlockSpec((1, LINE, acts), lambda b: (jnp.clip(2 * b + k, 0, last), 0, 0))
    return pl.pallas_call(
        downdate_kernel,
        grid=(8,),
        in_specs=[whole(solved[0]), whole(solved[1])]
        + [line(k) for k in (-1, 0, 1, 2)]
        + [whole(over), whole(under), pl.BlockSpec((2, LINE, LINE), lambda b: (b, 0, 0)), block],
        out_specs=block,
        out_shape=jax.ShapeDtypeStruct(base.shape, F32),
        compiler_params=pltpu.CompilerParams(vmem_limit_bytes=VMEM_LIMIT),
        cost_estimate=pl.CostEstimate(flops=12 << 30, bytes_accessed=28 << 20, transcendentals=0),
    )(*solved, lines, lines, lines, lines, over, under, diag, base)


def plant_line(before, here, after, diagonal):
    inner = lax.broadcasted_iota(jnp.int32, (LINE, 1), 0)
    sides = jnp.where(inner == 0, 0.0, pltpu.roll(here, 1, 0)) + jnp.where(
        inner == LINE - 1, 0.0, pltpu.roll(here, LINE - 1, 0)
    )
    return diagonal * here + COUPLING * (before + after + sides)


def plant_kernel(start, sizes, place, *refs):
    columns, at = [], 0
    for size in sizes:
        columns.append(refs[at : at + size])
        at += size
    rows_diag, cols_diag, cost = refs[at : at + 3]
    out, window = refs[-2:]
    step = pl.program_id(0)
    b = step + start
    rows = out.shape[0]
    lanes = lax.broadcasted_iota(jnp.int32, (1, LINE), 1)
    inner = lax.broadcasted_iota(jnp.int32, (LINE, 1), 0)
    column = lambda k: jnp.concatenate([ref[...] for ref in columns[k]], 0)

    @pl.when(step == 0)
    def _():
        window[0] = column(0)
        window[1] = column(1)

    here = window[1]
    after = column(2)
    sides = jnp.where(lanes == 0, 0.0, pltpu.roll(here, 1, 1)) + jnp.where(
        lanes == LINE - 1, 0.0, pltpu.roll(here, LINE - 1, 1)
    )
    field = cols_diag[pl.ds(b, 1), :] * here + COUPLING * (window[0] + after + sides)
    window[0] = here
    window[1] = after
    for a in range(rows // LINE):
        line = lambda k: field[(a + k) * LINE : (a + k + 1) * LINE]
        centre = line(1)
        sides = jnp.where(inner == 0, 0.0, pltpu.roll(centre, 1, 0)) + jnp.where(
            inner == LINE - 1, 0.0, pltpu.roll(centre, LINE - 1, 0)
        )
        here = slice(a * LINE, (a + 1) * LINE)
        out[here, :] = rows_diag[here, :] * centre + COUPLING * (line(0) + line(2) + sides)
    mine = place[1] + b - place[0]

    @pl.when((mine >= 0) & (mine < rows // LINE))
    def _():
        here = pl.ds(pl.multiple_of(mine * LINE, LINE), LINE)
        out[here, :] += jnp.where(inner == lanes, cost[pl.ds(mine, 1), :], 0.0)


def plant_part(start, count, place, value, above, below, left, right, rows_diag, cols_diag, cost, before):
    rows, cols = value.shape
    last = cols // LINE - 1
    array = pl.BlockSpec(memory_space=pltpu.VMEM)
    tall = rows + 2 * LINE

    def column(index):
        blocks = (above, value, below)
        return list(blocks), [pl.BlockSpec((x.shape[0], LINE), index) for x in blocks]

    whole = lambda x: ([x], [pl.BlockSpec((tall, LINE), lambda b: (0, 0))])
    columns = [
        whole(left) if start == 0 else column(lambda b: (0, start - 1)),
        column(lambda b: (0, start)),
        whole(right) if start == last else column(lambda b: (0, b + start + 1)),
    ]
    operands, specs = [place], [pl.BlockSpec(memory_space=pltpu.SMEM)]
    for blocks, block_specs in columns:
        operands += blocks
        specs += block_specs
    operands += [rows_diag, cols_diag, cost]
    specs += [array] * 3
    aliases = {}
    if before is not None:
        aliases = {len(operands): 0}
        operands.append(before)
        specs.append(pl.BlockSpec(memory_space=pl.ANY))
    return pl.pallas_call(
        functools.partial(plant_kernel, start, [len(blocks) for blocks, _ in columns]),
        grid=(count,),
        in_specs=specs,
        out_specs=pl.BlockSpec((rows, LINE), lambda b: (0, b + start)),
        out_shape=jax.ShapeDtypeStruct(value.shape, F32),
        scratch_shapes=[pltpu.VMEM((2, tall, LINE), F32)],
        input_output_aliases=aliases,
        compiler_params=pltpu.CompilerParams(vmem_limit_bytes=VMEM_LIMIT),
        cost_estimate=pl.CostEstimate(flops=32 << 20, bytes_accessed=16 << 20, transcendentals=0),
    )(*operands)


def local(value_matrix, inputs, plant_diag, state_cost, control_weight):
    row_index = lax.axis_index("row")
    col_index = lax.axis_index("col")
    both = ("row", "col")
    grid_side = plant_diag.shape[0]
    rows_block, cols_block = value_matrix.shape
    actuators = inputs.shape[1]
    lines_rows = rows_block // grid_side
    lines_cols = cols_block // grid_side
    diag_rows = lax.dynamic_slice_in_dim(plant_diag, row_index * lines_rows, lines_rows, 0)
    diag_cols = lax.dynamic_slice_in_dim(plant_diag, col_index * lines_cols, lines_cols, 0)
    me = row_index.astype(jnp.int32).reshape(1)
    trade = [(r * 8 + c, (2 * c + r // 8) * 8 + r % 8) for r in range(16) for c in range(8)]

    def shifted(x, axis, by):
        count = lax.axis_size(axis)
        return lax.ppermute(x, axis, [(i, i + by) for i in range(count) if 0 <= i + by < count])

    above = shifted(value_matrix[-LINE:], "row", 1)
    below = shifted(value_matrix[:LINE], "row", -1)
    operands = (
        jnp.stack([row_index * lines_rows, col_index * lines_cols]).astype(jnp.int32),
        value_matrix,
        jnp.broadcast_to(diag_rows.reshape(rows_block, 1), (rows_block, LINE)),
        diag_cols,
        state_cost.reshape(lines_rows, grid_side),
    )
    odd = product_lines(me, value_matrix, inputs, 1)
    even = product_lines(me, value_matrix, inputs, 0)
    rows = []

    def wait(came):
        came, *rows[:] = tied(came, above, below)
        return came

    product = scatter_lines(even, odd, wait)
    above, below = rows
    tall = lambda cols: jnp.concatenate([above[:, cols], value_matrix[:, cols], below[:, cols]], 0)
    left = shifted(tall(slice(-LINE, None)), "col", 1)
    right = shifted(tall(slice(None, LINE)), "col", -1)

    core, x_low, y = row_index & 1, (row_index >> 1) & 1, row_index >> 2
    x_high, z = col_index & 1, col_index >> 1
    x_place = x_high * 2 + x_low

    product, above, below = tied(product, above, below)
    traded = lax.ppermute(product, both, trade)
    around = (*operands[:2], above, below, left, right, *operands[2:])
    base = None
    for start, count in ((1, 7), (8, 7), (0, 1), (lines_cols - 1, 1)):
        base = plant_part(start, count, *around, base)
    traded, product, base = tied(traded, product, base)
    lines = lax.all_gather(product, "row", axis=0)

    mine_inputs = lax.dynamic_slice_in_dim(inputs, col_index * LINE, LINE, 0)
    pair = joined(traded, swap(traded, X_HIGH), x_high == 1)
    gram = gram_blocks(mine_inputs, traded)
    total = sum_cores(gram.reshape(10 * PANEL, PANEL), core)
    pair, total = tied(pair, total)

    first, second = pair[:LINE], pair[LINE:]
    first_near, second_near = swap(first, Z[1]), swap(second, Z[3])
    total = scatter_four(total, z, Z)
    first_near, second_near, total = tied(first_near, second_near, total)

    first_far = swap(jnp.stack([first, first_near]), Z[3])
    second_far = swap(jnp.stack([second, second_near]), Z[1])
    total = scatter_four(total, x_place, X)
    total = total + swap(total, Y[1]) + swap(total, Y[2]) + swap(total, Y[3])
    total = gather_four(total, x_place, X)
    first_far, second_far, total, lines = tied(first_far, second_far, total, lines)

    pick = lambda k, x: jnp.where(k < 2, jnp.where(k == 0, x[0], x[1]), jnp.where(k == 2, x[2], x[3]))
    head = pick(z, (first, first_near, first_far[1], first_far[0]))
    tail = pick(z ^ 3, (second, second_far[0], second_far[1], second_near))
    row_over, row_under = shifted(tail, "row", 1), shifted(head, "row", -1)
    col_over, col_under = shifted(lines[-1], "col", 1), shifted(lines[0], "col", -1)
    total = gather_four(total, z, Z)
    total = joined(total, swap(total, CORE), core == 1)
    factors = factored(control_weight, total.reshape(10, PANEL, PANEL))
    sides = (first, first_near, first_far, second, second_near, second_far, row_over, row_under, operands[2])
    solved = solve(z.astype(jnp.int32).reshape(1), factors, sides)
    wide_diag = jnp.broadcast_to(diag_cols[:, :, None], (lines_cols, LINE, LINE))
    return downdate(solved, lines, col_over, col_under, wide_diag, base)


def solution(mesh):
    in_specs = (P("row", "col"), P("row", None), P(), P("row"), P())
    out_specs = P("row", "col")
    return jax.shard_map(local, mesh=mesh, in_specs=in_specs, out_specs=out_specs, check_vma=False)
```

```python
import functools

import jax
import jax.numpy as jnp
from jax import lax
from jax.experimental import pallas as pl
from jax.experimental.pallas import tpu as pltpu
from jax.sharding import PartitionSpec as P

COUPLING = 0.25
F32 = jnp.float32
BF16 = jnp.bfloat16
NN = (((1,), (0,)), ((), ()))
NT = (((1,), (1,)), ((), ()))
TN = (((0,), (0,)), ((), ()))
LINE = 128
PANEL = 256
VMEM_LIMIT = 56 << 20


def split(x):
    high = x.astype(BF16)
    return high, (x - high.astype(F32)).astype(BF16)


def dot1(a, b, dims):
    return lax.dot_general(a, b, dims, preferred_element_type=F32)


def dot3(a, b, dims):
    (a_high, a_low), (b_high, b_low) = a, b
    return dot1(a_high, b_high, dims) + dot1(a_high, b_low, dims) + dot1(a_low, b_high, dims)


def line_of(device):
    return (device & 1) * 8 + (device >> 1)


def product_kernel(me_ref, first, second, inputs, out, high, low):
    @pl.when(pl.program_id(0) == 0)
    def _():
        high[...], low[...] = split(inputs[...])

    lines = split(jnp.concatenate([first[...], second[...]], 1))
    out[...] = dot3(lines, (high[...], low[...]), TN).reshape(out.shape)


def product_lines(me, value_matrix, inputs, odd):
    rows, acts = inputs.shape
    return pl.pallas_call(
        product_kernel,
        grid_spec=pltpu.PrefetchScalarGridSpec(
            num_scalar_prefetch=1,
            grid=(4,),
            in_specs=[
                pl.BlockSpec((rows, LINE), lambda i, m: (0, line_of(m[0] ^ (4 * i + odd)))),
                pl.BlockSpec((rows, LINE), lambda i, m: (0, line_of(m[0] ^ (4 * i + 2 + odd)))),
                pl.BlockSpec((rows, acts), lambda i, m: (0, 0)),
            ],
            out_specs=pl.BlockSpec((2, LINE, acts), lambda i, m: (i, 0, 0)),
            scratch_shapes=[pltpu.VMEM((rows, acts), BF16)] * 2,
        ),
        out_shape=jax.ShapeDtypeStruct((8, LINE, acts), F32),
        compiler_params=pltpu.CompilerParams(vmem_limit_bytes=VMEM_LIMIT),
        cost_estimate=pl.CostEstimate(flops=1 << 20, bytes_accessed=1 << 20, transcendentals=0),
    )(me, value_matrix, value_matrix, inputs)


def swap(x, mask):
    return lax.ppermute(x, ("row", "col"), [(i, i ^ mask) for i in range(128)])


CORE, X_LOW, X_HIGH = 8, 16, 1
Y = (0, 32, 64, 96)
Z = (0, 2, 4, 6)
X = (0, 16, 1, 17)


def y_first(near, blocks):
    return swap(jnp.stack([blocks[near], blocks[2]]), Y[near])


def y_second(near, blocks, got):
    far = 4 - near
    kept = blocks[far] + got[1]
    return blocks[0] + got[0] + swap(kept, Y[far])


def scatter_lines(even, odd, begun, first_wait, second_wait, third_wait):
    got = begun(swap(odd, CORE))
    quarter = LINE // 4
    cut = lambda i, q: even[i, q * quarter : (q + 1) * quarter] + got[i, q * quarter : (q + 1) * quarter]
    half = lambda i, q: jnp.concatenate([cut(i, q), cut(i, q + 1)], 0)
    pair = lambda m, q: jnp.stack([cut(2 * m, q), cut(2 * m + 1, q)])
    came = swap(jnp.stack([half(2 * m + 1, 0) for m in range(4)]), X_LOW)
    c = [pair(m, 2) for m in range(4)]
    d = [pair(m, 3) for m in range(4)]
    c_got, d_got = first_wait(y_first(1, c), y_first(3, d))
    c, d = y_second(1, c, c_got), y_second(3, d, d_got)
    came = second_wait(came)
    own = [half(2 * m, 0) + came[m] for m in range(4)]
    a = [o[:quarter] for o in own]
    b = [o[quarter:] for o in own]
    a_got, b_got = third_wait(y_first(1, a), y_first(3, b))
    a, b = y_second(1, a, a_got), y_second(3, b, b_got)
    rest = jnp.concatenate([c[0], d[0]], 0) + swap(jnp.concatenate([c[1], d[1]], 0), X_LOW)
    return jnp.concatenate([a, b, rest], 0)


def halves(x, bit):
    count = x.shape[0] // 2
    low, high = x[:count], x[count:]
    return jnp.where(bit, high, low), jnp.where(bit, low, high)


def joined(mine, got, bit):
    return jnp.concatenate([jnp.where(bit, got, mine), jnp.where(bit, mine, got)], 0)


def scatter_four(x, place, masks):
    count = x.shape[0] // 4
    own = lambda m: lax.dynamic_slice_in_dim(x, (place ^ m) * count, count, 0)
    return own(0) + swap(own(1), masks[1]) + swap(own(2), masks[2]) + swap(own(3), masks[3])


def gather_four(x, place, masks):
    parts = jnp.stack([x] + [swap(x, masks[m]) for m in range(1, 4)])
    return jnp.concatenate([lax.dynamic_index_in_dim(parts, place ^ m, 0, False) for m in range(4)], 0)


def tied(*values):
    return lax.optimization_barrier(values)


def sum_start(x, core, z, x_place):
    keep, send = halves(x, core == 1)
    x = keep + swap(send, CORE)
    return scatter_four(scatter_four(x, z, Z), x_place, X)


def sum_middle(x):
    return x + swap(x, Y[1]) + swap(x, Y[2]) + swap(x, Y[3])


def gather_rows_start(line):
    first, second = line[: LINE // 2], line[LINE // 2 :]
    pair = jnp.stack([first, swap(first, X_HIGH)])
    quad = jnp.stack([second] + [swap(second, Z[m]) for m in range(1, 4)])
    return pair, quad


def gather_rows_end(pair, quad):
    return [pair] + [swap(pair, Z[m]) for m in range(1, 4)] + [quad, swap(quad, X_HIGH)]


def gram_kernel(inputs, product, out):
    a = split(inputs[...])
    b = split(product[...])
    at = 0
    for k in range(4):
        for i in range(k, 4):
            left = [part[:, i * PANEL : (i + 1) * PANEL] for part in a]
            right = [part[:, k * PANEL : (k + 1) * PANEL] for part in b]
            out[at] = dot3(left, right, TN)
            at += 1


def gram_blocks(inputs, product):
    return pl.pallas_call(
        gram_kernel,
        out_shape=jax.ShapeDtypeStruct((10, PANEL, PANEL), F32),
        compiler_params=pltpu.CompilerParams(vmem_limit_bytes=VMEM_LIMIT),
    )(inputs, product)


def block_index(i, k):
    return k * 4 - (k * (k - 1)) // 2 + i - k


def series_inverse(a, eye, mask):
    picked = jnp.where(mask, a, 0.0)
    across = lax.rsqrt(jnp.sum(picked, axis=0, keepdims=True))
    down = lax.rsqrt(jnp.sum(picked, axis=1, keepdims=True))
    error = jnp.where(mask, 0.0, -(a * across * down))
    result = eye + error
    for _ in range(3):
        parts = split(error)
        error = dot3(parts, parts, NN)
        result = result + dot3(split(result), split(error), NN)
    short = error.astype(BF16)
    error = dot1(short, short, NN)
    result = result + dot1(result.astype(BF16), error.astype(BF16), NN)
    return result * across * down, jnp.sum(error * error, keepdims=True)


def pivot_inverse(a, work):
    size = a.shape[0]
    work[...] = a
    lanes = lax.broadcasted_iota(jnp.int32, (1, size), 1)
    rows = lax.broadcasted_iota(jnp.int32, (size, 1), 0)

    def step(p, carry):
        now = work[...]
        across = work[pl.ds(p, 1), :]
        down = jnp.sum(jnp.where(lanes == p, now, 0.0), axis=1, keepdims=True)
        inverse = 1.0 / jnp.sum(jnp.where(lanes == p, across, 0.0), axis=1, keepdims=True)
        new = now - down * (across * inverse)
        new = jnp.where(lanes == p, down * inverse, new)
        new = jnp.where(rows == p, across * inverse, new)
        work[...] = jnp.where((rows == p) & (lanes == p), -inverse, new)
        return carry

    lax.fori_loop(0, size, step, 0)
    return -work[...]


def factor_kernel(weight, gram, factor, inverses, work, worst):
    size = PANEL
    mask = lax.broadcasted_iota(jnp.int32, (size, size), 0) == lax.broadcasted_iota(jnp.int32, (size, size), 1)
    eye = jnp.where(mask, 1.0, 0.0).astype(F32)

    def run(robust):
        for k in range(4):
            for i in range(k, 4):
                here = gram[block_index(i, k)]
                factor[block_index(i, k)] = here + weight[0] * eye if i == k else here
        for k in range(4):
            here = factor[block_index(k, k)]
            if robust:
                inverse = pivot_inverse(here, work)
            else:
                inverse, off = series_inverse(here, eye, mask)
                worst[...] = off if k == 0 else jnp.where(off < worst[...], worst[...], off)
            inverses[k] = inverse
            parts = split(inverse)
            columns = [split(factor[block_index(i, k)]) for i in range(k + 1, 4)]
            lefts = []
            for i in range(k + 1, 4):
                left = dot3(columns[i - k - 1], parts, NN)
                factor[block_index(i, k)] = left
                lefts.append(split(left))
            for j in range(k + 1, 4):
                for i in range(j, 4):
                    factor[block_index(i, j)] -= dot3(lefts[i - k - 1], columns[j - k - 1], NT)

    run(False)

    @pl.when(jnp.logical_not(worst[0, 0] < 1e-6))
    def _():
        run(True)


def factored(weight, gram):
    scalar = pl.BlockSpec(memory_space=pltpu.SMEM)
    array = pl.BlockSpec(memory_space=pltpu.VMEM)
    return pl.pallas_call(
        factor_kernel,
        out_shape=[
            jax.ShapeDtypeStruct((10, PANEL, PANEL), F32),
            jax.ShapeDtypeStruct((4, PANEL, PANEL), F32),
        ],
        in_specs=[scalar, array],
        out_specs=[array, array],
        scratch_shapes=[pltpu.VMEM((PANEL, PANEL), F32), pltpu.VMEM((1, 1), F32)],
        compiler_params=pltpu.CompilerParams(vmem_limit_bytes=VMEM_LIMIT),
        cost_estimate=pl.CostEstimate(flops=9 << 30, bytes_accessed=12 << 20, transcendentals=0),
    )(weight, gram)


def solve_kernel(place, factor, inverses, own, near, across, far, quad, other, high, low, out):
    size = PANEL
    half = LINE // 2
    at = lambda k: slice(k * size, (k + 1) * size)

    def put(step, e, second, value):
        line = (place[0] ^ step) * 2 + (place[1] ^ e)
        out[pl.ds(pl.multiple_of(line * LINE + second * half, half), half), :] = value

    for step, pair in enumerate((own, near, across, far)):
        for e in range(2):
            put(step, e, 0, pair[e])
    for e, lines in enumerate((quad, other)):
        for step in range(4):
            put(step, e, 1, lines[step])
    for k in range(4):
        solved = split(out[:, at(k)])
        for i in range(k + 1, 4):
            out[:, at(i)] -= dot3(solved, split(factor[block_index(i, k)]), NT)
    for k in range(3, -1, -1):
        total = dot3(split(out[:, at(k)]), split(inverses[k]), NN)
        for i in range(k + 1, 4):
            total = total - dot3((high[:, at(i)], low[:, at(i)]), split(factor[block_index(i, k)]), NN)
        high[:, at(k)], low[:, at(k)] = split(total)


def solve(place, factors, sides):
    scalar = pl.BlockSpec(memory_space=pltpu.SMEM)
    array = pl.BlockSpec(memory_space=pltpu.VMEM)
    size = 8 * LINE
    return pl.pallas_call(
        solve_kernel,
        out_shape=[jax.ShapeDtypeStruct((size, 4 * PANEL), BF16)] * 2,
        in_specs=[scalar] + [array] * 8,
        out_specs=[array, array],
        scratch_shapes=[pltpu.VMEM((size, 4 * PANEL), F32)],
        compiler_params=pltpu.CompilerParams(vmem_limit_bytes=VMEM_LIMIT),
        cost_estimate=pl.CostEstimate(flops=9 << 30, bytes_accessed=12 << 20, transcendentals=0),
    )(place, *factors, *sides)


def downdate_kernel(high, low, first, second, base, out):
    lines = split(jnp.concatenate([first[0], second[0]], 0))
    out[...] = base[...] - dot3((high[...], low[...]), lines, NT)


def downdate(solved, gain_cols, base):
    rows, acts = solved[0].shape
    whole = pl.BlockSpec((rows, acts), lambda b: (0, 0))
    line = lambda b: (b % 8) * 2 + b // 8
    block = pl.BlockSpec((rows, 2 * LINE), lambda b: (0, b))
    return pl.pallas_call(
        downdate_kernel,
        grid=(8,),
        in_specs=[
            whole,
            whole,
            pl.BlockSpec((1, LINE, acts), lambda b: (line(2 * b), 0, 0)),
            pl.BlockSpec((1, LINE, acts), lambda b: (line(2 * b + 1), 0, 0)),
            block,
        ],
        out_specs=block,
        out_shape=jax.ShapeDtypeStruct(base.shape, F32),
        compiler_params=pltpu.CompilerParams(vmem_limit_bytes=VMEM_LIMIT),
        cost_estimate=pl.CostEstimate(flops=12 << 30, bytes_accessed=28 << 20, transcendentals=0),
    )(*solved, gain_cols, gain_cols, base)


def stencil_first(field, diagonal):
    centre = field[1:-1]
    side_padded = jnp.pad(centre, ((0, 0), (1, 1), (0, 0)))
    neighbours = field[:-2] + field[2:] + side_padded[:, :-2] + side_padded[:, 2:]
    return diagonal[:, :, None] * centre + COUPLING * neighbours


def plant_kernel(start, sizes, place, *refs):
    columns, at = [], 0
    for size in sizes:
        columns.append(refs[at : at + size])
        at += size
    rows_diag, cols_diag, cost = refs[at : at + 3]
    out, window = refs[-2:]
    step = pl.program_id(0)
    b = step + start
    rows = out.shape[0]
    lanes = lax.broadcasted_iota(jnp.int32, (1, LINE), 1)
    inner = lax.broadcasted_iota(jnp.int32, (LINE, 1), 0)
    column = lambda k: jnp.concatenate([ref[...] for ref in columns[k]], 0)

    @pl.when(step == 0)
    def _():
        window[0] = column(0)
        window[1] = column(1)

    here = window[1]
    after = column(2)
    sides = jnp.where(lanes == 0, 0.0, pltpu.roll(here, 1, 1)) + jnp.where(
        lanes == LINE - 1, 0.0, pltpu.roll(here, LINE - 1, 1)
    )
    field = cols_diag[pl.ds(b, 1), :] * here + COUPLING * (window[0] + after + sides)
    window[0] = here
    window[1] = after
    for a in range(rows // LINE):
        line = lambda k: field[(a + k) * LINE : (a + k + 1) * LINE]
        centre = line(1)
        sides = jnp.where(inner == 0, 0.0, pltpu.roll(centre, 1, 0)) + jnp.where(
            inner == LINE - 1, 0.0, pltpu.roll(centre, LINE - 1, 0)
        )
        here = slice(a * LINE, (a + 1) * LINE)
        out[here, :] = rows_diag[here, :] * centre + COUPLING * (line(0) + line(2) + sides)
    mine = place[1] + b - place[0]

    @pl.when((mine >= 0) & (mine < rows // LINE))
    def _():
        here = pl.ds(pl.multiple_of(mine * LINE, LINE), LINE)
        out[here, :] += jnp.where(inner == lanes, cost[pl.ds(mine, 1), :], 0.0)


def plant_part(start, count, place, value, above, below, left, right, rows_diag, cols_diag, cost, before):
    rows, cols = value.shape
    last = cols // LINE - 1
    array = pl.BlockSpec(memory_space=pltpu.VMEM)
    tall = rows + 2 * LINE

    def column(index):
        blocks = (above, value, below)
        return list(blocks), [pl.BlockSpec((x.shape[0], LINE), index) for x in blocks]

    whole = lambda x: ([x], [pl.BlockSpec((tall, LINE), lambda b: (0, 0))])
    columns = [
        whole(left) if start == 0 else column(lambda b: (0, start - 1)),
        column(lambda b: (0, start)),
        whole(right) if start == last else column(lambda b: (0, b + start + 1)),
    ]
    operands, specs = [place], [pl.BlockSpec(memory_space=pltpu.SMEM)]
    for blocks, block_specs in columns:
        operands += blocks
        specs += block_specs
    operands += [rows_diag, cols_diag, cost]
    specs += [array] * 3
    aliases = {}
    if before is not None:
        aliases = {len(operands): 0}
        operands.append(before)
        specs.append(pl.BlockSpec(memory_space=pl.ANY))
    return pl.pallas_call(
        functools.partial(plant_kernel, start, [len(blocks) for blocks, _ in columns]),
        grid=(count,),
        in_specs=specs,
        out_specs=pl.BlockSpec((rows, LINE), lambda b: (0, b + start)),
        out_shape=jax.ShapeDtypeStruct(value.shape, F32),
        scratch_shapes=[pltpu.VMEM((2, tall, LINE), F32)],
        input_output_aliases=aliases,
        compiler_params=pltpu.CompilerParams(vmem_limit_bytes=VMEM_LIMIT),
        cost_estimate=pl.CostEstimate(flops=32 << 20, bytes_accessed=16 << 20, transcendentals=0),
    )(*operands)


def device_of(line):
    chip_row, core, col = line % 8, (line // 8) % 2, line // 16
    return (chip_row * 2 + core) * 8 + col


def local(value_matrix, inputs, plant_diag, state_cost, control_weight):
    row_index = lax.axis_index("row")
    col_index = lax.axis_index("col")
    both = ("row", "col")
    grid_side = plant_diag.shape[0]
    rows_block, cols_block = value_matrix.shape
    actuators = inputs.shape[1]
    lines_rows = rows_block // grid_side
    lines_cols = cols_block // grid_side
    diag_rows = lax.dynamic_slice_in_dim(plant_diag, row_index * lines_rows, lines_rows, 0)
    diag_cols = lax.dynamic_slice_in_dim(plant_diag, col_index * lines_cols, lines_cols, 0)
    me = row_index.astype(jnp.int32).reshape(1)
    trade = [((a * 2 + core) * 8 + b, (b * 2 + core) * 8 + a) for a in range(8) for b in range(8) for core in range(2)]
    mine_inputs = lax.dynamic_slice_in_dim(inputs, col_index * LINE, LINE, 0)
    mine_inputs = lax.ppermute(mine_inputs, both, trade)

    def shifted(x, axis, by):
        count = lax.axis_size(axis)
        return lax.ppermute(x, axis, [(i, i + by) for i in range(count) if 0 <= i + by < count])

    above = shifted(value_matrix[-LINE:], "row", 1)
    below = shifted(value_matrix[:LINE], "row", -1)
    tall = lambda cols: jnp.concatenate([above[:, cols], value_matrix[:, cols], below[:, cols]], 0)
    left = shifted(tall(slice(-LINE, None)), "col", 1)
    right = shifted(tall(slice(None, LINE)), "col", -1)
    operands = (
        jnp.stack([row_index * lines_rows, col_index * lines_cols]).astype(jnp.int32),
        value_matrix,
        above,
        below,
        left,
        right,
        jnp.broadcast_to(diag_rows.reshape(rows_block, 1), (rows_block, LINE)),
        diag_cols,
        state_cost.reshape(lines_rows, grid_side),
    )
    odd = product_lines(me, value_matrix, inputs, 1)
    even = product_lines(me, value_matrix, inputs, 0)
    held = {}

    def begun(got):
        got, held["above"], held["below"] = tied(got, above, below)
        return got

    def first_wait(c_got, d_got):
        return c_got, d_got

    def second_wait(came):
        came, held["inputs"] = tied(came, mine_inputs)
        return came

    def third_wait(a_got, b_got):
        a_got, b_got, held["left"], held["right"] = tied(a_got, b_got, left, right)
        return a_got, b_got

    product = scatter_lines(even, odd, begun, first_wait, second_wait, third_wait)
    mine_inputs = held["inputs"]
    operands = (*operands[:2], held["above"], held["below"], held["left"], held["right"], *operands[6:])

    gram = gram_blocks(mine_inputs, product)
    product, gram = tied(product, gram)
    core, x_low, y = row_index & 1, (row_index >> 1) & 1, row_index >> 2
    x_high, z = col_index & 1, col_index >> 1
    x_place = x_high * 2 + x_low

    lines = grid_side
    over = lax.ppermute(product, both, [(device_of(i), device_of(i + 1)) for i in range(lines - 1)])
    under = lax.ppermute(product, both, [(device_of(i + 1), device_of(i)) for i in range(lines - 1)])
    total = sum_start(gram.reshape(10 * PANEL, PANEL), core, z, x_place)
    line = col_index * 16 + line_of(row_index)
    diagonal = lax.dynamic_slice_in_dim(plant_diag, line, 1, 0)
    gain = stencil_first(jnp.stack([over, product, under]), diagonal)[0]
    gain, total = tied(gain, total)
    total = sum_middle(total)
    gain, total = tied(gain, total)
    traded = lax.ppermute(gain, both, trade)
    total = gather_four(total, x_place, X)
    total, value = tied(total, value_matrix)
    total = gather_four(total, z, Z)
    operands = (operands[0], value, *operands[2:])
    base = plant_part(1, 7, *operands, None)
    base = plant_part(8, 7, *operands, base)
    traded, gain, total, base = tied(traded, gain, total, base)

    gain_cols = lax.all_gather(gain, "row", axis=0)
    pair, quad = gather_rows_start(traded)
    total = joined(total, swap(total, CORE), core == 1)
    base = plant_part(0, 1, *operands, base)
    pair, quad, total, base = tied(pair, quad, total, base)
    sides = gather_rows_end(pair, quad)
    factors = factored(control_weight, total.reshape(10, PANEL, PANEL))
    *factors, base = tied(*factors, base)
    base = plant_part(lines_cols - 1, 1, *operands, base)
    *sides, base = tied(*sides, base)
    solved = solve(jnp.stack([z, x_high]).astype(jnp.int32), factors, sides)
    return downdate(solved, gain_cols, base)


def solution(mesh):
    in_specs = (P("row", "col"), P("row", None), P(), P("row"), P())
    out_specs = P("row", "col")
    return jax.shard_map(local, mesh=mesh, in_specs=in_specs, out_specs=out_specs, check_vma=False)
```
